256 devices in a mesh: tx: 128 (over x_lo, z, y, core), ty: 2 (over x_hi).
Axes of the slice: x: 4 (x_hi: 2, x_lo: 2; x = x_hi * 2 + x_lo), y: 4, z: 8, core: 2. Of those that a mesh axis runs over, the one named last changes fastest.
Arguments:
- obj_re: float32 [65536, 512], P('tx', 'ty')
- obj_im: float32 [65536, 512], P('tx', 'ty')
- probe_re: float32 [256, 256], replicated, may hold values from -6 to 6
- probe_im: float32 [256, 256], replicated, may hold values from -6 to 6
- amplitude: float32 [128, 2, 12, 256, 256], P('tx', 'ty'), may hold values from 0 to 2
- offsets: int32 [128, 2, 12, 2], P('tx'), may hold values from 0 to 65280, as said below
- counts: int32 [128, 2], P('tx'), may hold values from 3 to 12, as said below
Outputs:
- grad_obj_re: float32 [65536, 512], P('tx', 'ty')
- grad_obj_im: float32 [65536, 512], P('tx', 'ty')
- grad_probe_re: float32 [256, 256], replicated
- grad_probe_im: float32 [256, 256], replicated
The draws below stay inside these ranges and needn't reach their ends.
Inputs may be any that keep to these rules, and one draw needn't show every extreme that they name: Tile (a, b)'s slots hold positions whose top-left row lies in rows a * 512 to (a + 1) * 512 - 1 and whose centre column lies in columns b * 256 to (b + 1) * 256 - 1; every window lies inside the object. Slots at or beyond the tile's count hold such offsets too. `counts`: live positions per tile.
All inputs are finite; a program needn't handle non-finite values.
Results may differ from the reference program's by a relative error of at most 0.0001.
Values sent between devices are 32-bit elements; how exact they have to be, the bound alone decides.
A program may use at most 64 MiB of HBM per device.

```python
import jax
import jax.numpy as jnp
from jax import lax

PATCH = 256
WIDTH = 512
TR = 512
SLOTS = 12
NROWS = 65536
N_TX = 128
N_TY = 2


def draw_obj_re(key, part):
    key = jax.random.fold_in(key, 1)
    rows_f = jnp.arange(NROWS, dtype=jnp.float32)
    growth = 0.5 + rows_f / NROWS
    values = jax.random.normal(key, (NROWS, WIDTH), jnp.float32)
    return (values * growth[:, None]).astype(jnp.float32)


def draw_obj_im(key, part):
    key = jax.random.fold_in(key, 2)
    rows_f = jnp.arange(NROWS, dtype=jnp.float32)
    growth = 0.5 + rows_f / NROWS
    values = jax.random.normal(key, (NROWS, WIDTH), jnp.float32)
    return (values * growth[:, None]).astype(jnp.float32)


def draw_offsets(key, part):
    key = jax.random.fold_in(key, 12)
    row_key, col_key, slot_key = jax.random.split(key, 3)
    grid_shape = (N_TX, N_TY, SLOTS)
    tile_ids = jnp.arange(N_TX, dtype=jnp.int32)[:, None, None]
    side_ids = jnp.arange(N_TY, dtype=jnp.int32)[None, :, None]
    row_limit = jnp.broadcast_to(jnp.where(tile_ids == N_TX - 1, TR - PATCH + 1, TR), grid_shape)
    local_rows = jax.random.randint(row_key, grid_shape, 0, row_limit)
    col_low = jnp.broadcast_to(jnp.where(side_ids == 0, 0, PATCH // 2), grid_shape)
    col_high = jnp.broadcast_to(jnp.where(side_ids == 0, PATCH // 2, WIDTH - PATCH + 1), grid_shape)
    columns = jax.random.randint(col_key, grid_shape, col_low, col_high)
    chosen = jax.random.randint(slot_key, (), 0, SLOTS // 4)
    local_rows = local_rows.at[0, :, chosen].set(0).at[N_TX - 1, :, chosen].set(TR - PATCH)
    columns = columns.at[:, 0, chosen].set(0).at[:, 1, chosen].set(WIDTH - PATCH)
    return jnp.stack([tile_ids * TR + local_rows, columns], axis=-1).astype(jnp.int32)


def draw_counts(key, part):
    key = jax.random.fold_in(key, 11)
    first_key, second_key, pick_key, other_key = jax.random.split(key, 4)
    lowest = SLOTS // 4
    tiles = N_TX * N_TY
    first_draw = jax.random.randint(first_key, (tiles,), 0, SLOTS - lowest + 1)
    second_draw = jax.random.randint(second_key, (tiles,), 0, SLOTS - lowest + 1)
    values = lowest + jnp.minimum(first_draw, second_draw)
    busiest = jax.random.randint(pick_key, (), 0, tiles)
    quietest = (busiest + 1 + jax.random.randint(other_key, (), 0, tiles - 1)) % tiles
    values = values.at[busiest].set(SLOTS).at[quietest].set(lowest)
    return values.reshape(N_TX, N_TY).astype(jnp.int32)


def level_of(stream_key, shape, pieces, low, largest):
    loudness, own = 1.0, jax.random.fold_in(stream_key, 6)
    for axis_at, blocks in pieces:
        heights = jnp.exp(jax.random.uniform(jax.random.fold_in(own, axis_at), (blocks,), jnp.float32, low / len(pieces), largest / len(pieces)))
        loudness = loudness * jnp.repeat(heights, shape[axis_at] // blocks).reshape([-1 if axis == axis_at else 1 for axis in range(len(shape))])
    return loudness


def normal_values(rng, dims, scale, limit, kind=jnp.bfloat16):
    return jnp.clip(scale * jax.random.normal(rng, dims, jnp.float32), -limit, limit).astype(kind)


def setup_inputs(seed: int = 0) -> dict:
    arg_keys = jax.random.split(jax.random.key(seed), 8)
    return {
        "obj_re": draw_obj_re(jax.random.fold_in(arg_keys[7], 71), 0),
        "obj_im": draw_obj_im(jax.random.fold_in(arg_keys[7], 71), 0),
        "probe_re": normal_values(arg_keys[2], (PATCH, PATCH), 1.0, 6.0, jnp.float32),
        "probe_im": normal_values(arg_keys[3], (PATCH, PATCH), 1.0, 6.0, jnp.float32),
        "amplitude": jnp.clip(2.0 * jax.random.uniform(arg_keys[4], (N_TX, N_TY, SLOTS, PATCH, PATCH), jnp.float32) ** level_of(arg_keys[4], (N_TX, N_TY, SLOTS, PATCH, PATCH), ((0, 128), (1, 2)), -0.2, 0.2), 0.0, 2.0),
        "offsets": draw_offsets(jax.random.fold_in(arg_keys[7], 71), 0),
        "counts": draw_counts(jax.random.fold_in(arg_keys[7], 71), 0),
    }


def reference(obj_re, obj_im, probe_re, probe_im, amplitude, offsets, counts):
    probe = lax.complex(probe_re, probe_im)
    measured = amplitude.reshape(N_TX * N_TY * SLOTS, PATCH, PATCH)
    places = offsets.reshape(N_TX * N_TY * SLOTS, 2).astype(jnp.int32)
    slot_ids = jnp.arange(SLOTS, dtype=jnp.int32)
    active = (slot_ids[None, None, :] < counts[:, :, None]).reshape(-1).astype(obj_re.dtype)

    def visit(totals, item):
        grad_re, grad_im, pgrad_re, pgrad_im = totals
        amp_here, place, weight = item
        row_at = place[0]
        col_at = place[1]
        piece_re = lax.dynamic_slice(obj_re, (row_at, col_at), (PATCH, PATCH))
        piece_im = lax.dynamic_slice(obj_im, (row_at, col_at), (PATCH, PATCH))
        window = lax.complex(piece_re, piece_im)
        wave_far = jnp.fft.fft2(probe * window, norm="ortho")
        modulus = jnp.abs(wave_far)
        diff = wave_far * (1.0 - amp_here / jnp.maximum(modulus, 1.0))
        chi = jnp.fft.ifft2(diff, norm="ortho")
        chi_re = jnp.real(chi)
        chi_im = jnp.imag(chi)
        obj_part_re = (probe_re * chi_re + probe_im * chi_im) * weight
        obj_part_im = (probe_re * chi_im - probe_im * chi_re) * weight
        now_re = lax.dynamic_slice(grad_re, (row_at, col_at), (PATCH, PATCH))
        now_im = lax.dynamic_slice(grad_im, (row_at, col_at), (PATCH, PATCH))
        grad_re = lax.dynamic_update_slice(grad_re, now_re + obj_part_re, (row_at, col_at))
        grad_im = lax.dynamic_update_slice(grad_im, now_im + obj_part_im, (row_at, col_at))
        pgrad_re = pgrad_re + (piece_re * chi_re + piece_im * chi_im) * weight
        pgrad_im = pgrad_im + (piece_re * chi_im - piece_im * chi_re) * weight
        return (grad_re, grad_im, pgrad_re, pgrad_im), None

    start_totals = (jnp.zeros_like(obj_re), jnp.zeros_like(obj_im), jnp.zeros_like(probe_re), jnp.zeros_like(probe_im))
    totals, unused = lax.scan(visit, start_totals, (measured, places, active))
    scale_by = 1.0 / (N_TX * N_TY * SLOTS)
    return totals[0], totals[1], totals[2] * scale_by, totals[3] * scale_by
```

```python
import math

import jax
import jax.numpy as jnp
import ml_dtypes
import numpy as np
from jax import lax
from jax.experimental import pallas as pl
from jax.experimental.pallas import tpu as pltpu
from jax.sharding import PartitionSpec as P

N = 256
H = 128
TR = 512
SLOTS = 12
NTX = 128
ROWS = TR + N
MESH = pl.DeviceIdType.MESH
F32 = jnp.float32
BF16 = jnp.bfloat16


def half_dft_tables():
    n = np.arange(H, dtype=np.float64)[:, None]
    k = np.arange(H, dtype=np.float64)[None, :]
    tables = []
    for odd in (0, 1):
        angle = -2.0 * math.pi * (n * (2 * k + odd)) / N
        re, im = np.cos(angle) / 16.0, np.sin(angle) / 16.0
        tables.append(np.block([[re, im], [-im, re]]))
    both = np.stack([tables[0], tables[1], tables[0].T, tables[1].T])
    high = both.astype(ml_dtypes.bfloat16)
    low = (both - high.astype(np.float64)).astype(ml_dtypes.bfloat16)
    return np.stack([high, low])


def even_odd_lanes():
    table = np.zeros((N, N), np.float32)
    j = np.arange(H)
    table[2 * j, j] = 1.0
    table[2 * j + 1, H + j] = 1.0
    return table.astype(ml_dtypes.bfloat16)


def split(x):
    high = x.astype(BF16)
    return high, (x - high.astype(F32)).astype(BF16)


def dot(a, b):
    return jnp.dot(a, b, preferred_element_type=F32)


def halo_kernel(
    obj_re, obj_im, amp, perm, reg, amp_out, raw, sorted_amp,
    ty_send, ty_recv, up_send, up_recv, diag_send, diag_recv, own_sem, raw_sem, amp_sem,
):
    tx, ty = lax.axis_index("tx"), lax.axis_index("ty")
    up, down = lax.rem(tx + NTX - 1, NTX), lax.rem(tx + 1, NTX)
    partner = (tx, 1 - ty)
    barrier = pltpu.get_barrier_semaphore()
    for device in (partner, (up, ty), (down, ty)):
        pl.semaphore_signal(barrier, inc=1, device_id=device, device_id_type=MESH)
    raw_copies = []
    for t in range(2):
        c = pltpu.make_async_copy(amp.at[0, 0, :, :, pl.ds(t * H, H)], raw.at[t], raw_sem.at[t])
        c.start()
        raw_copies.append(c)
    own = []
    for p, obj in enumerate((obj_re, obj_im)):
        for t in range(2):
            c = pltpu.make_async_copy(
                obj.at[:, pl.ds(t * H, H)], reg.at[p, ty + t, pl.ds(0, TR)], own_sem.at[p, t])
            c.start()
            own.append(c)
    pl.semaphore_wait(barrier, 3)

    edge = pl.multiple_of((1 - ty) * H, H)
    across = [[], []]
    for half in range(2):
        for p, obj in enumerate((obj_re, obj_im)):
            rows = pl.ds(half * N, N)
            c = pltpu.make_async_remote_copy(
                src_ref=obj.at[rows, pl.ds(edge, H)], dst_ref=reg.at[p, 2 * ty, rows],
                send_sem=ty_send.at[half, p], recv_sem=ty_recv.at[half, p],
                device_id=partner, device_id_type=MESH)
            c.start()
            across[half].append(c)
    below = []
    for p, obj in enumerate((obj_re, obj_im)):
        for t in range(2):
            c = pltpu.make_async_remote_copy(
                src_ref=obj.at[pl.ds(0, N), pl.ds(t * H, H)], dst_ref=reg.at[p, ty + t, pl.ds(TR, N)],
                send_sem=up_send.at[p, t], recv_sem=up_recv.at[p, t],
                device_id=(up, ty), device_id_type=MESH)
            c.start()
            below.append(c)
    for c in raw_copies:
        c.wait()

    def sort_slot(i, carry):
        for h in range(2):
            rows = [raw[t, i, pl.ds(h, H, stride=2), :] for t in range(2)]
            high, low = split(jnp.concatenate(rows, axis=1))
            sorted_amp[i, pl.ds(h * H, H), :] = dot(high, perm[...]) + dot(low, perm[...])
        pltpu.make_async_copy(sorted_amp.at[i], amp_out.at[i], amp_sem.at[i]).start()
        return carry

    lax.fori_loop(0, SLOTS // 2, sort_slot, 0)
    diag = []
    for p in range(2):
        across[0][p].wait()
        side = 2 - 2 * ty
        c = pltpu.make_async_remote_copy(
            src_ref=reg.at[p, side, pl.ds(0, N)], dst_ref=reg.at[p, side, pl.ds(TR, N)],
            send_sem=diag_send.at[p], recv_sem=diag_recv.at[p],
            device_id=(up, ty), device_id_type=MESH)
        c.start()
        diag.append(c)
    lax.fori_loop(SLOTS // 2, SLOTS, sort_slot, 0)

    def finish_slot(i, carry):
        pltpu.make_async_copy(sorted_amp.at[i], amp_out.at[i], amp_sem.at[i]).wait()
        return carry

    lax.fori_loop(0, SLOTS, finish_slot, 0)
    for c in own + across[1] + below + diag:
        c.wait()


def halo(obj_re, obj_im, amp, perm):
    anywhere = pl.BlockSpec(memory_space=pl.ANY)
    dma = pltpu.SemaphoreType.DMA
    return pl.pallas_call(
        halo_kernel,
        out_shape=(
            jax.ShapeDtypeStruct((2, 3, ROWS, H), F32),
            jax.ShapeDtypeStruct((SLOTS, N, N), F32),
        ),
        in_specs=[anywhere, anywhere, anywhere, pl.BlockSpec(memory_space=pltpu.VMEM)],
        out_specs=(anywhere, anywhere),
        scratch_shapes=[
            pltpu.VMEM((2, SLOTS, N, H), F32),
            pltpu.VMEM((SLOTS, N, N), F32),
            dma((2, 2)), dma((2, 2)), dma((2, 2)), dma((2, 2)), dma((2,)), dma((2,)),
            dma((2, 2)), dma((2,)), dma((SLOTS,)),
        ],
        compiler_params=pltpu.CompilerParams(
            collective_id=0, has_side_effects=True, vmem_limit_bytes=40 << 20),
        name="halo",
    )(obj_re, obj_im, amp, perm)


def positions_kernel(
    offsets, counts, reg, probe_re, probe_im, tables, amp_in, grad, pgrad,
    amp, win, sp, mid, amp_sem,
):
    tx, ty = lax.axis_index("tx"), lax.axis_index("ty")
    live = counts[0, ty]
    probe = (probe_re, probe_im)
    CH = 32

    def fetch(i):
        return pltpu.make_async_copy(amp_in.at[i], amp.at[i], amp_sem.at[i])

    def start_fetch(i, carry):
        fetch(i).start()
        return carry

    lax.fori_loop(0, live, start_fetch, 0)
    grad[...] = jnp.zeros_like(grad)
    pgrad[...] = jnp.zeros_like(pgrad)
    lane = lax.broadcasted_iota(jnp.int32, (CH, H), 1)

    def put(q, rows, lanes, value):
        high, low = split(value)
        sp[0, q, rows, lanes] = high
        sp[1, q, rows, lanes] = low

    def right(q, which):
        return (dot(sp[0, q], tables[0, which]) + dot(sp[1, q], tables[0, which])
                + dot(sp[0, q], tables[1, which]))

    def left(q, which):
        return (dot(tables[0, which], sp[0, q]) + dot(tables[1, which], sp[0, q])
                + dot(tables[0, which], sp[1, q]))

    def lanes(t):
        return pl.ds(t * H, H)

    def one(i, carry):
        row_at = offsets[0, ty, i, 0] - tx * TR
        col_at = offsets[0, ty, i, 1] - ty * H
        back = lax.rem(H - col_at, H)
        ahead = lax.rem(col_at, H)
        from_next = lane >= H - col_at
        to_next = lane < col_at
        for j in range(N // CH):
            rows = pl.ds(j * CH, CH)
            ex = [[None, None], [None, None]]
            w = [[None, None], [None, None]]
            for p in range(2):
                turned = [pltpu.roll(reg[p, t, pl.ds(row_at + j * CH, CH), :], back, 1) for t in range(3)]
                for t in range(2):
                    w[p][t] = jnp.where(from_next, turned[t + 1], turned[t])
                    win[p, t, rows, :] = w[p][t]
            for t in range(2):
                pr, pi = probe_re[rows, lanes(t)], probe_im[rows, lanes(t)]
                ex[0][t] = pr * w[0][t] - pi * w[1][t]
                ex[1][t] = pr * w[1][t] + pi * w[0][t]
            for p in range(2):
                put(0, rows, lanes(p), ex[p][0] + ex[p][1])
                put(1, rows, lanes(p), ex[p][0] - ex[p][1])
        for q in range(2):
            mid[q] = right(q, q)
        for j in range(H // CH):
            for q in range(2):
                for p in range(2):
                    top = mid[q, pl.ds(j * CH, CH), lanes(p)]
                    low = mid[q, pl.ds(H + j * CH, CH), lanes(p)]
                    rows = pl.ds(p * H + j * CH, CH)
                    put(0, rows, lanes(q), top + low)
                    put(1, rows, lanes(q), top - low)
        for h in range(2):
            mid[h] = left(h, 2 + h)
        fetch(i).wait()
        for j in range(H // CH):
            for h in range(2):
                rows_re, rows_im = pl.ds(j * CH, CH), pl.ds(H + j * CH, CH)
                re, im = mid[h, rows_re, :], mid[h, rows_im, :]
                measured = amp[i, pl.ds(h * H + j * CH, CH), :]
                keep = 1.0 - measured * lax.rsqrt(jnp.maximum(re * re + im * im, 1.0))
                put(h, rows_re, slice(None), re * keep)
                put(h, rows_im, slice(None), im * keep)
        for h in range(2):
            mid[h] = left(h, h)
        for j in range(H // CH):
            for p in range(2):
                for q in range(2):
                    a = mid[0, pl.ds(p * H + j * CH, CH), lanes(q)]
                    b = mid[1, pl.ds(p * H + j * CH, CH), lanes(q)]
                    put(q, pl.ds(j * CH, CH), lanes(p), a + b)
                    put(q, pl.ds(H + j * CH, CH), lanes(p), a - b)
        for q in range(2):
            mid[q] = right(q, 2 + q)
        for j in range(N // CH):
            rows = pl.ds(j * CH, CH)
            g = [[None, None], [None, None]]
            for t in range(2):
                chi = []
                for p in range(2):
                    a, b = mid[0, rows, lanes(p)], mid[1, rows, lanes(p)]
                    chi.append(a + b if t == 0 else a - b)
                pr, pi = probe_re[rows, lanes(t)], probe_im[rows, lanes(t)]
                wr, wi = win[0, t, rows, :], win[1, t, rows, :]
                g[0][t] = pltpu.roll(pr * chi[0] + pi * chi[1], ahead, 1)
                g[1][t] = pltpu.roll(pr * chi[1] - pi * chi[0], ahead, 1)
                pgrad[0, t, rows, :] += wr * chi[0] + wi * chi[1]
                pgrad[1, t, rows, :] += wr * chi[1] - wi * chi[0]
            at = pl.ds(row_at + j * CH, CH)
            for p in range(2):
                grad[p, 0, at, :] += jnp.where(to_next, 0.0, g[p][0])
                grad[p, 1, at, :] += jnp.where(to_next, g[p][0], g[p][1])
                grad[p, 2, at, :] += jnp.where(to_next, g[p][1], 0.0)
        return carry

    lax.fori_loop(0, live, one, 0)


def positions(offsets, counts, reg, probe_re, probe_im, tables, amp):
    smem = pl.BlockSpec(memory_space=pltpu.SMEM)
    vmem = pl.BlockSpec(memory_space=pltpu.VMEM)
    return pl.pallas_call(
        positions_kernel,
        out_shape=(
            jax.ShapeDtypeStruct((2, 3, ROWS, H), F32),
            jax.ShapeDtypeStruct((2, 2, N, H), F32),
        ),
        in_specs=[smem, smem, vmem, vmem, vmem, vmem, pl.BlockSpec(memory_space=pl.ANY)],
        out_specs=(vmem, vmem),
        scratch_shapes=[
            pltpu.VMEM((SLOTS, N, N), F32),
            pltpu.VMEM((2, 2, N, H), F32),
            pltpu.VMEM((2, 2, N, N), BF16),
            pltpu.VMEM((2, N, N), F32),
            pltpu.SemaphoreType.DMA((SLOTS,)),
        ],
        compiler_params=pltpu.CompilerParams(vmem_limit_bytes=40 << 20),
        name="positions",
    )(offsets, counts, reg, probe_re, probe_im, tables, amp)


def out_kernel(
    grad, pgrad, out_re, out_im, pout_re, pout_im,
    came_ty, came_up, came_diag, edge, core_in, acc, y_in, z_in, x_all, full, other,
    ty_send, ty_recv, up_send, up_recv, diag_send, diag_recv,
    core_send, core_recv, y_send, y_recv, z_send, z_recv, x_send, x_recv,
):
    tx, ty = lax.axis_index("tx"), lax.axis_index("ty")
    up, down = lax.rem(tx + NTX - 1, NTX), lax.rem(tx + 1, NTX)
    partner = (tx, 1 - ty)
    core, y, z, x_lo = lax.rem(tx, 2), lax.rem(tx // 2, 4), lax.rem(tx // 8, 8), tx // 64
    x = ty * 2 + x_lo

    def at(core_, y_, z_, x_):
        return (((lax.rem(x_, 2) * 8 + z_) * 4 + y_) * 2 + core_, x_ // 2)

    core_mate = at(1 - core, y, z, x)
    y_mates = [at(core, lax.rem(y + d, 4), z, x) for d in range(1, 4)]
    z_mates = [at(core, y, lax.rem(z + d, 8), x) for d in range(1, 8)]
    x_mates = [at(core, y, z, lax.rem(x + d, 4)) for d in range(1, 4)]
    greeted = [partner, (up, ty), (down, ty), core_mate] + y_mates + z_mates + x_mates
    barrier = pltpu.get_barrier_semaphore()
    for device in greeted:
        pl.semaphore_signal(barrier, inc=1, device_id=device, device_id_type=MESH)
    pl.semaphore_wait(barrier, len(greeted))

    def send(src, dst, send_sem, recv_sem, device):
        c = pltpu.make_async_remote_copy(
            src_ref=src, dst_ref=dst, send_sem=send_sem, recv_sem=recv_sem,
            device_id=device, device_id_type=MESH)
        c.start()
        return c

    side = 2 - 2 * ty
    core_copy = send(pgrad.at[1 - core], core_in, core_send.at[0], core_recv.at[0], core_mate)
    diag = send(grad.at[:, side, pl.ds(TR, N)], came_diag, diag_send, diag_recv, (down, ty))
    far_rows = send(
        grad.at[:, side, pl.ds(N, N)], came_ty.at[:, pl.ds(N, N)], ty_send.at[1], ty_recv.at[1], partner)
    below = send(
        grad.at[:, pl.ds(ty, 2), pl.ds(TR, N)], came_up, up_send, up_recv, (down, ty))

    core_copy.wait()
    for t in range(2):
        acc[pl.ds(t * N, N), :] = pgrad[core, t] + core_in[t]
    y_copies = [
        send(acc.at[pl.ds(pl.multiple_of(lax.rem(y + d, 4) * H, H), H)], y_in.at[d - 1],
             y_send.at[0, d - 1], y_recv.at[0, d - 1], y_mates[d - 1])
        for d in range(1, 4)]

    diag.wait()
    for p in range(2):
        edge[p] = grad[p, side, pl.ds(0, N)] + came_diag[p]
    near_rows = send(edge, came_ty.at[:, pl.ds(0, N)], ty_send.at[0], ty_recv.at[0], partner)

    for c in y_copies:
        c.wait()
    y_rows = pl.ds(pl.multiple_of(y * H, H), H)
    acc[y_rows, :] = acc[y_rows, :] + y_in[0] + y_in[1] + y_in[2]
    z_copies = [
        send(acc.at[pl.ds(pl.multiple_of(y * H + lax.rem(z + d, 8) * 16, 16), 16)], z_in.at[d - 1],
             z_send.at[0, d - 1], z_recv.at[0, d - 1], z_mates[d - 1])
        for d in range(1, 8)]
    for c in z_copies:
        c.wait()
    z_rows = pl.ds(pl.multiple_of(y * H + z * 16, 16), 16)
    total = acc[z_rows, :]
    for d in range(7):
        total = total + z_in[d]
    x_all[x] = total
    x_copies = [
        send(x_all.at[x], x_all.at[x], x_send.at[d - 1], x_recv.at[d - 1], x_mates[d - 1])
        for d in range(1, 4)]
    for c in x_copies:
        c.wait()
    full[z_rows, :] = ((x_all[0] + x_all[1]) + (x_all[2] + x_all[3])) * (1.0 / (NTX * 2 * SLOTS))
    z_copies = [
        send(full.at[z_rows], full.at[z_rows], z_send.at[1, d - 1], z_recv.at[1, d - 1], z_mates[d - 1])
        for d in range(1, 8)]
    for c in z_copies:
        c.wait()
    y_copies = [
        send(full.at[y_rows], full.at[y_rows], y_send.at[1, d - 1], y_recv.at[1, d - 1], y_mates[d - 1])
        for d in range(1, 4)]
    for c in y_copies:
        c.wait()
    core_copy = send(full, other, core_send.at[1], core_recv.at[1], core_mate)

    below.wait()
    far_rows.wait()
    near_rows.wait()
    for p, out in enumerate((out_re, out_im)):
        for t in range(2):
            lanes = pl.ds(t * H, H)
            mine = ty == 1 - t
            ty_rows = [jnp.where(mine, came_ty[p, pl.ds(h * N, N)], 0.0) for h in range(2)]
            out[pl.ds(0, N), lanes] = (
                grad[p, ty + t, pl.ds(0, N)] + came_up[p, t] + ty_rows[0])
            out[pl.ds(N, N), lanes] = grad[p, ty + t, pl.ds(N, N)] + ty_rows[1]
    core_copy.wait()
    for t in range(2):
        rows, lanes = pl.ds(t * N, N), pl.ds(t * H, H)
        a, b = full[rows, :], other[rows, :]
        pout_re[:, lanes] = jnp.where(core == 0, a, b)
        pout_im[:, lanes] = jnp.where(core == 0, b, a)


def gather_out(grad, pgrad):
    vmem = pl.BlockSpec(memory_space=pltpu.VMEM)
    dma = pltpu.SemaphoreType.DMA
    tile = jax.ShapeDtypeStruct((TR, N), F32)
    patch = jax.ShapeDtypeStruct((N, N), F32)
    return pl.pallas_call(
        out_kernel,
        out_shape=(tile, tile, patch, patch),
        in_specs=[vmem, vmem],
        out_specs=(vmem, vmem, vmem, vmem),
        scratch_shapes=[
            pltpu.VMEM((2, TR, H), F32),
            pltpu.VMEM((2, 2, N, H), F32),
            pltpu.VMEM((2, N, H), F32),
            pltpu.VMEM((2, N, H), F32),
            pltpu.VMEM((2, N, H), F32),
            pltpu.VMEM((2 * N, H), F32),
            pltpu.VMEM((3, H, H), F32),
            pltpu.VMEM((7, 16, H), F32),
            pltpu.VMEM((4, 16, H), F32),
            pltpu.VMEM((2 * N, H), F32),
            pltpu.VMEM((2 * N, H), F32),
            dma((2,)), dma((2,)), dma(()), dma(()), dma(()), dma(()),
            dma((2,)), dma((2,)), dma((2, 3)), dma((2, 3)), dma((2, 7)), dma((2, 7)), dma((3,)), dma((3,)),
        ],
        compiler_params=pltpu.CompilerParams(
            collective_id=1, has_side_effects=True, vmem_limit_bytes=40 << 20),
        name="gather_out",
    )(grad, pgrad)


def per_device(obj_re, obj_im, probe_re, probe_im, amplitude, offsets, counts):
    tables = jnp.asarray(half_dft_tables())
    perm = jnp.asarray(even_odd_lanes())
    reg, amp = halo(obj_re, obj_im, amplitude, perm)
    grad, pgrad = positions(offsets, counts, reg, probe_re, probe_im, tables, amp)
    return gather_out(grad, pgrad)


def solution(mesh):
    return jax.shard_map(
        per_device,
        mesh=mesh,
        in_specs=(
            P("tx", "ty"),
            P("tx", "ty"),
            P(),
            P(),
            P("tx", "ty", None, None, None),
            P("tx", None, None, None),
            P("tx", None),
        ),
        out_specs=(P("tx", "ty"), P("tx", "ty"), P(), P()),
        check_vma=False,
    )
```

```python
import math

import jax
import jax.numpy as jnp
import ml_dtypes
import numpy as np
from jax import lax
from jax.experimental import pallas as pl
from jax.experimental.pallas import tpu as pltpu
from jax.sharding import PartitionSpec as P

N = 256
H = 128
TR = 512
SLOTS = 12
NTX = 128
ROWS = TR + N
MESH = pl.DeviceIdType.MESH
F32 = jnp.float32
BF16 = jnp.bfloat16


def half_dft_tables():
    n = np.arange(H, dtype=np.float64)[:, None]
    k = np.arange(H, dtype=np.float64)[None, :]
    tables = []
    for odd in (0, 1):
        angle = -2.0 * math.pi * (n * (2 * k + odd)) / N
        re, im = np.cos(angle) / 16.0, np.sin(angle) / 16.0
        tables.append(np.block([[re, im], [-im, re]]))
    both = np.stack([tables[0], tables[1], tables[0].T, tables[1].T])
    high = both.astype(ml_dtypes.bfloat16)
    low = (both - high.astype(np.float64)).astype(ml_dtypes.bfloat16)
    return np.stack([high, low])


def split(x):
    high = x.astype(BF16)
    return high, (x - high.astype(F32)).astype(BF16)


def dot(a, b):
    return jnp.dot(a, b, preferred_element_type=F32)


def halo_kernel(
    obj_re, obj_im, amp, reg, amp_out, raw, perm, sorted_amp,
    ty_send, ty_recv, up_send, up_recv, diag_send, diag_recv, own_sem, raw_sem, amp_sem,
):
    tx, ty = lax.axis_index("tx"), lax.axis_index("ty")
    up, down = lax.rem(tx + NTX - 1, NTX), lax.rem(tx + 1, NTX)
    partner = (tx, 1 - ty)
    barrier = pltpu.get_barrier_semaphore()
    for device in (partner, (up, ty), (down, ty)):
        pl.semaphore_signal(barrier, inc=1, device_id=device, device_id_type=MESH)
    raw_copies = []
    for t in range(2):
        c = pltpu.make_async_copy(amp.at[0, 0, :, :, pl.ds(t * H, H)], raw.at[t], raw_sem.at[t])
        c.start()
        raw_copies.append(c)
    own = []
    for p, obj in enumerate((obj_re, obj_im)):
        for t in range(2):
            c = pltpu.make_async_copy(
                obj.at[:, pl.ds(t * H, H)], reg.at[p, ty + t, pl.ds(0, TR)], own_sem.at[p, t])
            c.start()
            own.append(c)
    i, j = (lax.broadcasted_iota(jnp.int32, (N, N), d) for d in range(2))
    perm[...] = jnp.where(i == jnp.where(j < H, 2 * j, 2 * (j - H) + 1), 1.0, 0.0).astype(BF16)
    pl.semaphore_wait(barrier, 3)

    edge = pl.multiple_of((1 - ty) * H, H)
    across = [[], []]
    for half in range(2):
        for p, obj in enumerate((obj_re, obj_im)):
            rows = pl.ds(half * N, N)
            c = pltpu.make_async_remote_copy(
                src_ref=obj.at[rows, pl.ds(edge, H)], dst_ref=reg.at[p, 2 * ty, rows],
                send_sem=ty_send.at[half, p], recv_sem=ty_recv.at[half, p],
                device_id=partner, device_id_type=MESH)
            c.start()
            across[half].append(c)
    below = []
    for p, obj in enumerate((obj_re, obj_im)):
        for t in range(2):
            c = pltpu.make_async_remote_copy(
                src_ref=obj.at[pl.ds(0, N), pl.ds(t * H, H)], dst_ref=reg.at[p, ty + t, pl.ds(TR, N)],
                send_sem=up_send.at[p, t], recv_sem=up_recv.at[p, t],
                device_id=(up, ty), device_id_type=MESH)
            c.start()
            below.append(c)
    for c in raw_copies:
        c.wait()

    def sort_slot(i, carry):
        for h in range(2):
            rows = [raw[t, i, pl.ds(h, H, stride=2), :] for t in range(2)]
            high, low = split(jnp.concatenate(rows, axis=1))
            sorted_amp[i, pl.ds(h * H, H), :] = dot(high, perm[...]) + dot(low, perm[...])
        pltpu.make_async_copy(sorted_amp.at[i], amp_out.at[i], amp_sem.at[i]).start()
        return carry

    lax.fori_loop(0, SLOTS // 2, sort_slot, 0)
    diag = []
    for p in range(2):
        across[0][p].wait()
        side = 2 - 2 * ty
        c = pltpu.make_async_remote_copy(
            src_ref=reg.at[p, side, pl.ds(0, N)], dst_ref=reg.at[p, side, pl.ds(TR, N)],
            send_sem=diag_send.at[p], recv_sem=diag_recv.at[p],
            device_id=(up, ty), device_id_type=MESH)
        c.start()
        diag.append(c)
    lax.fori_loop(SLOTS // 2, SLOTS, sort_slot, 0)

    def finish_slot(i, carry):
        pltpu.make_async_copy(sorted_amp.at[i], amp_out.at[i], amp_sem.at[i]).wait()
        return carry

    lax.fori_loop(0, SLOTS, finish_slot, 0)
    for c in own + across[1] + below + diag:
        c.wait()


def halo(obj_re, obj_im, amp):
    anywhere = pl.BlockSpec(memory_space=pl.ANY)
    hbm = pl.BlockSpec(memory_space=pltpu.HBM)
    dma = pltpu.SemaphoreType.DMA
    return pl.pallas_call(
        halo_kernel,
        out_shape=(
            jax.ShapeDtypeStruct((2, 3, ROWS, H), F32),
            jax.ShapeDtypeStruct((SLOTS, N, N), F32),
        ),
        in_specs=[hbm, hbm, hbm],
        out_specs=(anywhere, anywhere),
        scratch_shapes=[
            pltpu.VMEM((2, SLOTS, N, H), F32),
            pltpu.VMEM((N, N), BF16),
            pltpu.VMEM((SLOTS, N, N), F32),
            dma((2, 2)), dma((2, 2)), dma((2, 2)), dma((2, 2)), dma((2,)), dma((2,)),
            dma((2, 2)), dma((2,)), dma((SLOTS,)),
        ],
        compiler_params=pltpu.CompilerParams(
            collective_id=0, has_side_effects=True, vmem_limit_bytes=58 << 20),
        name="halo",
    )(obj_re, obj_im, amp)


def positions_kernel(
    offsets, counts, reg, probe_re, probe_im, tables, amp_in, grad, pgrad,
    amp, win, sp, mid, amp_sem,
):
    tx, ty = lax.axis_index("tx"), lax.axis_index("ty")
    live = counts[0, ty]
    probe = (probe_re, probe_im)
    CH = 32

    def fetch(i):
        return pltpu.make_async_copy(amp_in.at[i], amp.at[i], amp_sem.at[i])

    def start_fetch(i, carry):
        fetch(i).start()
        return carry

    lax.fori_loop(0, live, start_fetch, 0)
    grad[...] = jnp.zeros_like(grad)
    pgrad[...] = jnp.zeros_like(pgrad)
    lane = lax.broadcasted_iota(jnp.int32, (CH, H), 1)

    def put(s, q, rows, lanes, value):
        high, low = split(value)
        sp[s, 0, q, rows, lanes] = high
        sp[s, 1, q, rows, lanes] = low

    def right(s, q, which):
        high, low = sp[s, 0, q], sp[s, 1, q]
        mid[s, q] = dot(jnp.concatenate([high, low, high], axis=1),
                        jnp.concatenate([tables[0, which], tables[0, which], tables[1, which]], axis=0))

    def left(s, q, which):
        high, low = sp[s, 0, q], sp[s, 1, q]
        mid[s, q] = dot(jnp.concatenate([tables[0, which], tables[1, which], tables[0, which]], axis=1),
                        jnp.concatenate([high, high, low], axis=0))

    def lanes(t):
        return pl.ds(t * H, H)

    def enter(s, place):
        row_at, col_at = place
        back = lax.rem(H - col_at, H)
        from_next = lane >= H - col_at
        for j in range(N // CH):
            rows = pl.ds(j * CH, CH)
            ex = [[None, None], [None, None]]
            w = [[None, None], [None, None]]
            for p in range(2):
                turned = [pltpu.roll(reg[p, t, pl.ds(row_at + j * CH, CH), :], back, 1) for t in range(3)]
                for t in range(2):
                    w[p][t] = jnp.where(from_next, turned[t + 1], turned[t])
                    win[s, p, t, rows, :] = w[p][t]
            for t in range(2):
                pr, pi = probe_re[rows, lanes(t)], probe_im[rows, lanes(t)]
                ex[0][t] = pr * w[0][t] - pi * w[1][t]
                ex[1][t] = pr * w[1][t] + pi * w[0][t]
            for p in range(2):
                put(s, 0, rows, lanes(p), ex[p][0] + ex[p][1])
                put(s, 1, rows, lanes(p), ex[p][0] - ex[p][1])

    def fold_rows(s):
        for j in range(H // CH):
            for q in range(2):
                for p in range(2):
                    top = mid[s, q, pl.ds(j * CH, CH), lanes(p)]
                    low = mid[s, q, pl.ds(H + j * CH, CH), lanes(p)]
                    rows = pl.ds(p * H + j * CH, CH)
                    put(s, 0, rows, lanes(q), top + low)
                    put(s, 1, rows, lanes(q), top - low)

    def compare(s, i, used):
        for j in range(H // CH):
            for h in range(2):
                rows_re, rows_im = pl.ds(j * CH, CH), pl.ds(H + j * CH, CH)
                re, im = mid[s, h, rows_re, :], mid[s, h, rows_im, :]
                measured = amp[i, pl.ds(h * H + j * CH, CH), :]
                keep = 1.0 - measured * lax.rsqrt(jnp.maximum(re * re + im * im, 1.0))
                keep = jnp.where(used, keep, 0.0)
                put(s, h, rows_re, slice(None), re * keep)
                put(s, h, rows_im, slice(None), im * keep)

    def unfold_rows(s):
        for j in range(H // CH):
            for p in range(2):
                for q in range(2):
                    a = mid[s, 0, pl.ds(p * H + j * CH, CH), lanes(q)]
                    b = mid[s, 1, pl.ds(p * H + j * CH, CH), lanes(q)]
                    put(s, q, pl.ds(j * CH, CH), lanes(p), a + b)
                    put(s, q, pl.ds(H + j * CH, CH), lanes(p), a - b)

    def leave(s, place):
        row_at, col_at = place
        ahead = lax.rem(col_at, H)
        to_next = lane < col_at
        for j in range(N // CH):
            rows = pl.ds(j * CH, CH)
            g = [[None, None], [None, None]]
            for t in range(2):
                chi = []
                for p in range(2):
                    a, b = mid[s, 0, rows, lanes(p)], mid[s, 1, rows, lanes(p)]
                    chi.append(a + b if t == 0 else a - b)
                pr, pi = probe_re[rows, lanes(t)], probe_im[rows, lanes(t)]
                wr, wi = win[s, 0, t, rows, :], win[s, 1, t, rows, :]
                g[0][t] = pltpu.roll(pr * chi[0] + pi * chi[1], ahead, 1)
                g[1][t] = pltpu.roll(pr * chi[1] - pi * chi[0], ahead, 1)
                pgrad[0, t, rows, :] += wr * chi[0] + wi * chi[1]
                pgrad[1, t, rows, :] += wr * chi[1] - wi * chi[0]
            at = pl.ds(row_at + j * CH, CH)
            for p in range(2):
                grad[p, 0, at, :] += jnp.where(to_next, 0.0, g[p][0])
                grad[p, 1, at, :] += jnp.where(to_next, g[p][0], g[p][1])
                grad[p, 2, at, :] += jnp.where(to_next, g[p][1], 0.0)

    def place_of(i):
        return offsets[0, ty, 0, i] - tx * TR, offsets[0, ty, 1, i] - ty * H

    def pair(k, carry):
        ids = [2 * k, jnp.minimum(2 * k + 1, live - 1)]
        used = [True, 2 * k + 1 < live]
        places = [place_of(i) for i in ids]
        fetch(ids[0]).wait()

        @pl.when(used[1])
        def _():
            fetch(ids[1]).wait()

        steps = [
            lambda s: enter(s, places[s]),
            lambda s: [right(s, q, q) for q in range(2)],
            lambda s: fold_rows(s),
            lambda s: [left(s, h, 2 + h) for h in range(2)],
            lambda s: compare(s, ids[s], used[s]),
            lambda s: [left(s, h, h) for h in range(2)],
            lambda s: unfold_rows(s),
            lambda s: [right(s, q, 2 + q) for q in range(2)],
            lambda s: leave(s, places[s]),
        ]
        steps[0](0)
        for n in range(1, len(steps)):
            steps[n](0)
            steps[n - 1](1)
        steps[-1](1)
        return carry

    lax.fori_loop(0, (live + 1) // 2, pair, 0)


def positions(offsets, counts, reg, probe_re, probe_im, tables, amp):
    smem = pl.BlockSpec(memory_space=pltpu.SMEM)
    vmem = pl.BlockSpec(memory_space=pltpu.VMEM)
    return pl.pallas_call(
        positions_kernel,
        out_shape=(
            jax.ShapeDtypeStruct((2, 3, ROWS, H), F32),
            jax.ShapeDtypeStruct((2, 2, N, H), F32),
        ),
        in_specs=[smem, smem, vmem, vmem, vmem, vmem, pl.BlockSpec(memory_space=pl.ANY)],
        out_specs=(vmem, vmem),
        scratch_shapes=[
            pltpu.VMEM((SLOTS, N, N), F32),
            pltpu.VMEM((2, 2, 2, N, H), F32),
            pltpu.VMEM((2, 2, 2, N, N), BF16),
            pltpu.VMEM((2, 2, N, N), F32),
            pltpu.SemaphoreType.DMA((SLOTS,)),
        ],
        compiler_params=pltpu.CompilerParams(vmem_limit_bytes=46 << 20),
        name="positions",
    )(offsets, counts, reg, probe_re, probe_im, tables, amp)


def out_kernel(
    grad, pgrad, out_ty, out_up, out_full, out_other,
    came_diag, edge, core_in, acc, xy_in, z_all,
    ty_send, ty_recv, up_send, up_recv, diag_send, diag_recv,
    core_send, core_recv, xy_send, xy_recv, z_send, z_recv,
):
    tx, ty = lax.axis_index("tx"), lax.axis_index("ty")
    up, down = lax.rem(tx + NTX - 1, NTX), lax.rem(tx + 1, NTX)
    partner = (tx, 1 - ty)
    core, y, z, x_lo = lax.rem(tx, 2), lax.rem(tx // 2, 4), lax.rem(tx // 8, 8), tx // 64
    x = ty * 2 + x_lo

    def at(core_, y_, z_, x_):
        return (((lax.rem(x_, 2) * 8 + z_) * 4 + y_) * 2 + core_, x_ // 2)

    core_mate = at(1 - core, y, z, x)
    steps = [(i, j) for i in range(4) for j in range(4) if i or j]
    steps.sort(key=lambda s: -(min(s[0], 4 - s[0]) + min(s[1], 4 - s[1])))
    xy_at = [(lax.rem(y + i, 4), lax.rem(x + j, 4)) for i, j in steps]
    xy_mates = [at(core, y_, z, x_) for y_, x_ in xy_at]
    z_mates = [at(core, y, lax.rem(z + d, 8), x) for d in (4, 3, 5, 2, 6, 1, 7)]
    greeted = [partner, (up, ty), (down, ty), core_mate] + xy_mates + z_mates
    barrier = pltpu.get_barrier_semaphore()
    for device in greeted:
        pl.semaphore_signal(barrier, inc=1, device_id=device, device_id_type=MESH)
    pl.semaphore_wait(barrier, len(greeted))

    def send(src, dst, send_sem, recv_sem, device):
        c = pltpu.make_async_remote_copy(
            src_ref=src, dst_ref=dst, send_sem=send_sem, recv_sem=recv_sem,
            device_id=device, device_id_type=MESH)
        c.start()
        return c

    def part(i, j):
        return pl.ds(pl.multiple_of((i * 4 + j) * 32, 32), 32)

    side = 2 - 2 * ty
    core_copy = send(pgrad.at[1 - core], core_in, core_send.at[0], core_recv.at[0], core_mate)
    diag = send(grad.at[:, side, pl.ds(TR, N)], came_diag, diag_send, diag_recv, (down, ty))
    core_copy.wait()
    for t in range(2):
        acc[pl.ds(t * N, N), :] = pgrad[core, t] + core_in[t]
    xy_copies = [
        send(acc.at[part(*xy_at[d])], xy_in.at[d], xy_send.at[0, d], xy_recv.at[0, d], xy_mates[d])
        for d in range(15)]

    for c in xy_copies:
        c.wait()
    total = acc[part(y, x), :]
    for d in range(15):
        total = total + xy_in[d]
    z_all[z] = total
    z_copies = [
        send(z_all.at[z], z_all.at[z], z_send.at[d], z_recv.at[d], z_mates[d]) for d in range(7)]
    far_rows = send(
        grad.at[:, side, pl.ds(N, N)], out_ty.at[:, pl.ds(N, N)], ty_send.at[1], ty_recv.at[1], partner)
    below = send(grad.at[:, pl.ds(ty, 2), pl.ds(TR, N)], out_up, up_send, up_recv, (down, ty))
    diag.wait()
    for p in range(2):
        edge[p] = grad[p, side, pl.ds(0, N)] + came_diag[p]
    near_rows = send(edge, out_ty.at[:, pl.ds(0, N)], ty_send.at[0], ty_recv.at[0], partner)

    for c in z_copies:
        c.wait()
    total = z_all[0]
    for d in range(1, 8):
        total = total + z_all[d]
    out_full[part(y, x), :] = total * (1.0 / (NTX * 2 * SLOTS))
    xy_copies = [
        send(out_full.at[part(y, x)], out_full.at[part(y, x)], xy_send.at[1, d], xy_recv.at[1, d], xy_mates[d])
        for d in range(15)]

    for c in xy_copies:
        c.wait()
    core_copy = send(out_full, out_other, core_send.at[1], core_recv.at[1], core_mate)
    below.wait()
    far_rows.wait()
    near_rows.wait()
    core_copy.wait()


def finish_kernel(grad, came_ty, came_up, full, other, out_re, out_im, pout_re, pout_im):
    core, ty = lax.rem(lax.axis_index("tx"), 2), lax.axis_index("ty")
    for p, out in enumerate((out_re, out_im)):
        for t in range(2):
            lanes = pl.ds(t * H, H)
            mine = ty == 1 - t
            ty_rows = [jnp.where(mine, came_ty[p, pl.ds(h * N, N)], 0.0) for h in range(2)]
            out[pl.ds(0, N), lanes] = grad[p, ty + t, pl.ds(0, N)] + came_up[p, t] + ty_rows[0]
            out[pl.ds(N, N), lanes] = grad[p, ty + t, pl.ds(N, N)] + ty_rows[1]
    for t in range(2):
        rows, lanes = pl.ds(t * N, N), pl.ds(t * H, H)
        a, b = full[rows, :], other[rows, :]
        pout_re[:, lanes] = jnp.where(core == 0, a, b)
        pout_im[:, lanes] = jnp.where(core == 0, b, a)


def gather_out(grad, pgrad):
    vmem = pl.BlockSpec(memory_space=pltpu.VMEM)
    dma = pltpu.SemaphoreType.DMA
    tile = jax.ShapeDtypeStruct((TR, N), F32)
    patch = jax.ShapeDtypeStruct((N, N), F32)
    came = pl.pallas_call(
        out_kernel,
        out_shape=(
            jax.ShapeDtypeStruct((2, TR, H), F32),
            jax.ShapeDtypeStruct((2, 2, N, H), F32),
            jax.ShapeDtypeStruct((2 * N, H), F32),
            jax.ShapeDtypeStruct((2 * N, H), F32),
        ),
        in_specs=[vmem, vmem],
        out_specs=(vmem, vmem, vmem, vmem),
        scratch_shapes=[
            pltpu.VMEM((2, N, H), F32),
            pltpu.VMEM((2, N, H), F32),
            pltpu.VMEM((2, N, H), F32),
            pltpu.VMEM((2 * N, H), F32),
            pltpu.VMEM((15, 32, H), F32),
            pltpu.VMEM((8, 32, H), F32),
            dma((2,)), dma((2,)), dma(()), dma(()), dma(()), dma(()),
            dma((2,)), dma((2,)), dma((2, 15)), dma((2, 15)), dma((7,)), dma((7,)),
        ],
        compiler_params=pltpu.CompilerParams(
            collective_id=1, has_side_effects=True, vmem_limit_bytes=20 << 20),
        name="gather_out",
    )(grad, pgrad)
    return pl.pallas_call(
        finish_kernel,
        out_shape=(tile, tile, patch, patch),
        in_specs=[vmem] * 5,
        out_specs=(vmem,) * 4,
        compiler_params=pltpu.CompilerParams(vmem_limit_bytes=20 << 20),
        name="finish",
    )(grad, *came)


def per_device(obj_re, obj_im, probe_re, probe_im, amplitude, offsets, counts):
    tables = jnp.asarray(half_dft_tables())
    reg, amp = halo(obj_re, obj_im, amplitude)
    grad, pgrad = positions(jnp.swapaxes(offsets, 2, 3), counts, reg, probe_re, probe_im, tables, amp)
    return gather_out(grad, pgrad)


def solution(mesh):
    return jax.shard_map(
        per_device,
        mesh=mesh,
        in_specs=(
            P("tx", "ty"),
            P("tx", "ty"),
            P(),
            P(),
            P("tx", "ty", None, None, None),
            P("tx", None, None, None),
            P("tx", None),
        ),
        out_specs=(P("tx", "ty"), P("tx", "ty"), P(), P()),
        check_vma=False,
    )
```

```python
import math

import jax
import jax.numpy as jnp
import ml_dtypes
import numpy as np
from jax import lax
from jax.experimental import pallas as pl
from jax.experimental.pallas import tpu as pltpu
from jax.sharding import PartitionSpec as P

N = 256
H = 128
TR = 512
SLOTS = 12
NTX = 128
ROWS = TR + N
MESH = pl.DeviceIdType.MESH
F32 = jnp.float32
BF16 = jnp.bfloat16


def half_dft_tables():
    n = np.arange(H, dtype=np.float64)[:, None]
    k = np.arange(H, dtype=np.float64)[None, :]
    tables = []
    for odd in (0, 1):
        angle = -2.0 * math.pi * (n * (2 * k + odd)) / N
        re, im = np.cos(angle) / 16.0, np.sin(angle) / 16.0
        tables.append(np.block([[re, im], [-im, re]]))
    both = np.stack([tables[0], tables[1], tables[0].T, tables[1].T])
    high = both.astype(ml_dtypes.bfloat16)
    low = (both - high.astype(np.float64)).astype(ml_dtypes.bfloat16)
    return np.stack([high, low])


def split(x):
    high = x.astype(BF16)
    return high, (x - high.astype(F32)).astype(BF16)


def dot(a, b):
    return jnp.dot(a, b, preferred_element_type=F32)


def halo_kernel(
    obj_re, obj_im, amp, reg, amp_out, raw, perm,
    ty_send, ty_recv, up_send, up_recv, diag_send, diag_recv, own_sem, raw_sem,
):
    tx, ty = lax.axis_index("tx"), lax.axis_index("ty")
    up, down = lax.rem(tx + NTX - 1, NTX), lax.rem(tx + 1, NTX)
    partner = (tx, 1 - ty)
    barrier = pltpu.get_barrier_semaphore()
    for device in (partner, (up, ty), (down, ty)):
        pl.semaphore_signal(barrier, inc=1, device_id=device, device_id_type=MESH)
    raw_copies = []
    for t in range(2):
        c = pltpu.make_async_copy(amp.at[0, 0, :, :, pl.ds(t * H, H)], raw.at[t], raw_sem.at[t])
        c.start()
        raw_copies.append(c)
    own = []
    for p, obj in enumerate((obj_re, obj_im)):
        for t in range(2):
            c = pltpu.make_async_copy(
                obj.at[:, pl.ds(t * H, H)], reg.at[p, ty + t, pl.ds(0, TR)], own_sem.at[p, t])
            c.start()
            own.append(c)
    i, j = (lax.broadcasted_iota(jnp.int32, (N, N), d) for d in range(2))
    perm[...] = jnp.where(i == jnp.where(j < H, 2 * j, 2 * (j - H) + 1), 1.0, 0.0).astype(BF16)
    pl.semaphore_wait(barrier, 3)

    edge = pl.multiple_of((1 - ty) * H, H)
    across = [[], []]
    for half in range(2):
        for p, obj in enumerate((obj_re, obj_im)):
            rows = pl.ds(half * N, N)
            c = pltpu.make_async_remote_copy(
                src_ref=obj.at[rows, pl.ds(edge, H)], dst_ref=reg.at[p, 2 * ty, rows],
                send_sem=ty_send.at[half, p], recv_sem=ty_recv.at[half, p],
                device_id=partner, device_id_type=MESH)
            c.start()
            across[half].append(c)
    below = []
    for p, obj in enumerate((obj_re, obj_im)):
        for t in range(2):
            c = pltpu.make_async_remote_copy(
                src_ref=obj.at[pl.ds(0, N), pl.ds(t * H, H)], dst_ref=reg.at[p, ty + t, pl.ds(TR, N)],
                send_sem=up_send.at[p, t], recv_sem=up_recv.at[p, t],
                device_id=(up, ty), device_id_type=MESH)
            c.start()
            below.append(c)
    for c in raw_copies:
        c.wait()

    def sort_slot(i, carry):
        for h in range(2):
            rows = [raw[t, i, pl.ds(h, H, stride=2), :] for t in range(2)]
            high, low = split(jnp.concatenate(rows, axis=1))
            amp_out[i, pl.ds(h * H, H), :] = dot(high, perm[...]) + dot(low, perm[...])
        return carry

    lax.fori_loop(0, SLOTS // 2, sort_slot, 0)
    diag = []
    for p in range(2):
        across[0][p].wait()
        side = 2 - 2 * ty
        c = pltpu.make_async_remote_copy(
            src_ref=reg.at[p, side, pl.ds(0, N)], dst_ref=reg.at[p, side, pl.ds(TR, N)],
            send_sem=diag_send.at[p], recv_sem=diag_recv.at[p],
            device_id=(up, ty), device_id_type=MESH)
        c.start()
        diag.append(c)
    lax.fori_loop(SLOTS // 2, SLOTS, sort_slot, 0)

    for c in own + across[1] + below + diag:
        c.wait()


def halo(obj_re, obj_im, amp):
    hbm, vmem = (pl.BlockSpec(memory_space=m) for m in (pltpu.HBM, pltpu.VMEM))
    dma = pltpu.SemaphoreType.DMA
    return pl.pallas_call(
        halo_kernel,
        out_shape=(
            pltpu.VMEM((2, 3, ROWS, H), F32),
            pltpu.VMEM((SLOTS, N, N), F32),
        ),
        in_specs=[hbm, hbm, hbm],
        out_specs=(vmem, vmem),
        scratch_shapes=[
            pltpu.VMEM((2, SLOTS, N, H), F32),
            pltpu.VMEM((N, N), BF16),
            dma((2, 2)), dma((2, 2)), dma((2, 2)), dma((2, 2)), dma((2,)), dma((2,)),
            dma((2, 2)), dma((2,)),
        ],
        compiler_params=pltpu.CompilerParams(
            collective_id=0, has_side_effects=True, vmem_limit_bytes=20 << 20),
        name="halo",
    )(*(pltpu.with_memory_space_constraint(x, pltpu.HBM) for x in (obj_re, obj_im, amp)))


def positions_kernel(
    offsets, counts, reg, probe_re, probe_im, tables, amp, grad, pgrad, win, sp, mid,
):
    tx, ty = lax.axis_index("tx"), lax.axis_index("ty")
    live = counts[0, ty]
    probe = (probe_re, probe_im)
    CH = 32

    grad[...] = jnp.zeros_like(grad)
    pgrad[...] = jnp.zeros_like(pgrad)
    lane = lax.broadcasted_iota(jnp.int32, (CH, H), 1)

    def put(s, q, rows, lanes, value):
        high, low = split(value)
        sp[s, 0, q, rows, lanes] = high
        sp[s, 1, q, rows, lanes] = low

    def right(s, q, which):
        high, low = sp[s, 0, q], sp[s, 1, q]
        mid[s, q] = dot(jnp.concatenate([high, low, high], axis=1),
                        jnp.concatenate([tables[0, which], tables[0, which], tables[1, which]], axis=0))

    def left(s, q, which):
        high, low = sp[s, 0, q], sp[s, 1, q]
        mid[s, q] = dot(jnp.concatenate([tables[0, which], tables[1, which], tables[0, which]], axis=1),
                        jnp.concatenate([high, high, low], axis=0))

    def lanes(t):
        return pl.ds(t * H, H)

    def enter(s, place):
        row_at, col_at = place
        back = lax.rem(H - col_at, H)
        from_next = lane >= H - col_at
        for j in range(N // CH):
            rows = pl.ds(j * CH, CH)
            ex = [[None, None], [None, None]]
            w = [[None, None], [None, None]]
            for p in range(2):
                turned = [pltpu.roll(reg[p, t, pl.ds(row_at + j * CH, CH), :], back, 1) for t in range(3)]
                for t in range(2):
                    w[p][t] = jnp.where(from_next, turned[t + 1], turned[t])
                    win[s, p, t, rows, :] = w[p][t]
            for t in range(2):
                pr, pi = probe_re[rows, lanes(t)], probe_im[rows, lanes(t)]
                ex[0][t] = pr * w[0][t] - pi * w[1][t]
                ex[1][t] = pr * w[1][t] + pi * w[0][t]
            for p in range(2):
                put(s, 0, rows, lanes(p), ex[p][0] + ex[p][1])
                put(s, 1, rows, lanes(p), ex[p][0] - ex[p][1])

    def fold_rows(s):
        for j in range(H // CH):
            for q in range(2):
                for p in range(2):
                    top = mid[s, q, pl.ds(j * CH, CH), lanes(p)]
                    low = mid[s, q, pl.ds(H + j * CH, CH), lanes(p)]
                    rows = pl.ds(p * H + j * CH, CH)
                    put(s, 0, rows, lanes(q), top + low)
                    put(s, 1, rows, lanes(q), top - low)

    def compare(s, i, used):
        for j in range(H // CH):
            for h in range(2):
                rows_re, rows_im = pl.ds(j * CH, CH), pl.ds(H + j * CH, CH)
                re, im = mid[s, h, rows_re, :], mid[s, h, rows_im, :]
                measured = amp[i, pl.ds(h * H + j * CH, CH), :]
                keep = 1.0 - measured * lax.rsqrt(jnp.maximum(re * re + im * im, 1.0))
                keep = jnp.where(used, keep, 0.0)
                put(s, h, rows_re, slice(None), re * keep)
                put(s, h, rows_im, slice(None), im * keep)

    def unfold_rows(s):
        for j in range(H // CH):
            for p in range(2):
                for q in range(2):
                    a = mid[s, 0, pl.ds(p * H + j * CH, CH), lanes(q)]
                    b = mid[s, 1, pl.ds(p * H + j * CH, CH), lanes(q)]
                    put(s, q, pl.ds(j * CH, CH), lanes(p), a + b)
                    put(s, q, pl.ds(H + j * CH, CH), lanes(p), a - b)

    def leave(s, place):
        row_at, col_at = place
        ahead = lax.rem(col_at, H)
        to_next = lane < col_at
        for j in range(N // CH):
            rows = pl.ds(j * CH, CH)
            g = [[None, None], [None, None]]
            for t in range(2):
                chi = []
                for p in range(2):
                    a, b = mid[s, 0, rows, lanes(p)], mid[s, 1, rows, lanes(p)]
                    chi.append(a + b if t == 0 else a - b)
                pr, pi = probe_re[rows, lanes(t)], probe_im[rows, lanes(t)]
                wr, wi = win[s, 0, t, rows, :], win[s, 1, t, rows, :]
                g[0][t] = pltpu.roll(pr * chi[0] + pi * chi[1], ahead, 1)
                g[1][t] = pltpu.roll(pr * chi[1] - pi * chi[0], ahead, 1)
                pgrad[0, t, rows, :] += wr * chi[0] + wi * chi[1]
                pgrad[1, t, rows, :] += wr * chi[1] - wi * chi[0]
            at = pl.ds(row_at + j * CH, CH)
            for p in range(2):
                grad[p, 0, at, :] += jnp.where(to_next, 0.0, g[p][0])
                grad[p, 1, at, :] += jnp.where(to_next, g[p][0], g[p][1])
                grad[p, 2, at, :] += jnp.where(to_next, g[p][1], 0.0)

    def place_of(i):
        return offsets[0, ty, 0, i] - tx * TR, offsets[0, ty, 1, i] - ty * H

    def pair(k, carry):
        ids = [2 * k, jnp.minimum(2 * k + 1, live - 1)]
        used = [True, 2 * k + 1 < live]
        places = [place_of(i) for i in ids]
        steps = [
            lambda s: enter(s, places[s]),
            lambda s: [right(s, q, q) for q in range(2)],
            lambda s: fold_rows(s),
            lambda s: [left(s, h, 2 + h) for h in range(2)],
            lambda s: compare(s, ids[s], used[s]),
            lambda s: [left(s, h, h) for h in range(2)],
            lambda s: unfold_rows(s),
            lambda s: [right(s, q, 2 + q) for q in range(2)],
            lambda s: leave(s, places[s]),
        ]
        steps[0](0)
        for n in range(1, len(steps)):
            steps[n](0)
            steps[n - 1](1)
        steps[-1](1)
        return carry

    lax.fori_loop(0, (live + 1) // 2, pair, 0)


def positions(offsets, counts, reg, probe_re, probe_im, tables, amp):
    smem = pl.BlockSpec(memory_space=pltpu.SMEM)
    vmem = pl.BlockSpec(memory_space=pltpu.VMEM)
    return pl.pallas_call(
        positions_kernel,
        out_shape=(
            pltpu.VMEM((2, 3, ROWS, H), F32),
            pltpu.VMEM((2, 2, N, H), F32),
        ),
        in_specs=[smem, smem, vmem, vmem, vmem, vmem, vmem],
        out_specs=(vmem, vmem),
        scratch_shapes=[
            pltpu.VMEM((2, 2, 2, N, H), F32),
            pltpu.VMEM((2, 2, 2, N, N), BF16),
            pltpu.VMEM((2, 2, N, N), F32),
        ],
        compiler_params=pltpu.CompilerParams(vmem_limit_bytes=20 << 20),
        name="positions",
    )(offsets, counts, reg, probe_re, probe_im, tables, amp)


def out_kernel(
    grad, pgrad, out_ty, out_up, out_full, out_other,
    came_diag, edge, core_in, acc, yz_in, shared,
    ty_send, ty_recv, up_send, up_recv, diag_send, diag_recv,
    core_send, core_recv, yz_send, yz_recv, far_send, far_recv,
):
    tx, ty = lax.axis_index("tx"), lax.axis_index("ty")
    up, down = lax.rem(tx + NTX - 1, NTX), lax.rem(tx + 1, NTX)
    partner = (tx, 1 - ty)
    core, y, z, x_lo = lax.rem(tx, 2), lax.rem(tx // 2, 4), lax.rem(tx // 8, 8), tx // 64
    x = ty * 2 + x_lo

    def at(core_, y_, z_, x_):
        return (((lax.rem(x_, 2) * 8 + z_) * 4 + y_) * 2 + core_, x_ // 2)

    core_mate = at(1 - core, y, z, x)
    z_low, z_high = lax.rem(z, 4), z // 4
    steps = [(i, j) for i in range(4) for j in range(4) if i or j]
    steps.sort(key=lambda s: -(min(s[0], 4 - s[0]) + min(s[1], 4 - s[1])))
    yz_at = [(lax.rem(y + i, 4), lax.rem(z_low + j, 4)) for i, j in steps]
    yz_mates = [at(core, i, z_high * 4 + j, x) for i, j in yz_at]
    hops = [(1, 2), (1, 1), (1, 3), (1, 0), (0, 2), (0, 1), (0, 3)]
    far_mates = [at(core, y, lax.rem(z_high + i, 2) * 4 + z_low, lax.rem(x + j, 4)) for i, j in hops]
    greeted = [partner, (up, ty), (down, ty), core_mate] + yz_mates + far_mates
    barrier = pltpu.get_barrier_semaphore()
    for device in greeted:
        pl.semaphore_signal(barrier, inc=1, device_id=device, device_id_type=MESH)
    pl.semaphore_wait(barrier, len(greeted))

    def send(src, dst, send_sem, recv_sem, device):
        c = pltpu.make_async_remote_copy(
            src_ref=src, dst_ref=dst, send_sem=send_sem, recv_sem=recv_sem,
            device_id=device, device_id_type=MESH)
        c.start()
        return c

    def part(i, j):
        return pl.ds(pl.multiple_of((i * 4 + j) * 32, 32), 32)

    side = 2 - 2 * ty
    core_copy = send(pgrad.at[1 - core], core_in, core_send.at[0], core_recv.at[0], core_mate)
    diag = send(grad.at[:, side, pl.ds(TR, N)], came_diag, diag_send, diag_recv, (down, ty))
    far_rows = send(
        grad.at[:, side, pl.ds(N, N)], out_ty.at[:, pl.ds(N, N)], ty_send.at[1], ty_recv.at[1], partner)
    core_copy.wait()
    for t in range(2):
        acc[pl.ds(t * N, N), :] = pgrad[core, t] + core_in[t]
    yz_copies = [
        send(acc.at[part(*yz_at[d])], yz_in.at[d], yz_send.at[0, d], yz_recv.at[0, d], yz_mates[d])
        for d in range(15)]
    diag.wait()
    for p in range(2):
        edge[p] = grad[p, side, pl.ds(0, N)] + came_diag[p]
    for c in yz_copies:
        c.wait()
    total = acc[part(y, z_low), :]
    for d in range(15):
        total = total + yz_in[d]
    mine = x * 2 + z_high
    shared[mine] = total
    far_copies = [
        send(shared.at[mine], shared.at[mine], far_send.at[d], far_recv.at[d], far_mates[d]) for d in range(7)]
    below = send(grad.at[:, pl.ds(ty, 2), pl.ds(TR, N)], out_up, up_send, up_recv, (down, ty))
    for c in far_copies:
        c.wait()
    total = shared[0]
    for d in range(1, 8):
        total = total + shared[d]
    out_full[part(y, z_low), :] = total * (1.0 / (NTX * 2 * SLOTS))
    yz_copies = [
        send(out_full.at[part(y, z_low)], out_full.at[part(y, z_low)],
             yz_send.at[1, d], yz_recv.at[1, d], yz_mates[d])
        for d in range(15)]
    near_rows = send(edge, out_ty.at[:, pl.ds(0, N)], ty_send.at[0], ty_recv.at[0], partner)
    for c in yz_copies:
        c.wait()
    core_copy = send(out_full, out_other, core_send.at[1], core_recv.at[1], core_mate)
    below.wait()
    far_rows.wait()
    near_rows.wait()
    core_copy.wait()


def finish_kernel(grad, came_ty, came_up, full, other, out_re, out_im, pout_re, pout_im):
    core, ty = lax.rem(lax.axis_index("tx"), 2), lax.axis_index("ty")
    for p, out in enumerate((out_re, out_im)):
        for t in range(2):
            lanes = pl.ds(t * H, H)
            mine = ty == 1 - t
            ty_rows = [jnp.where(mine, came_ty[p, pl.ds(h * N, N)], 0.0) for h in range(2)]
            out[pl.ds(0, N), lanes] = grad[p, ty + t, pl.ds(0, N)] + came_up[p, t] + ty_rows[0]
            out[pl.ds(N, N), lanes] = grad[p, ty + t, pl.ds(N, N)] + ty_rows[1]
    for t in range(2):
        rows, lanes = pl.ds(t * N, N), pl.ds(t * H, H)
        a, b = full[rows, :], other[rows, :]
        pout_re[:, lanes] = jnp.where(core == 0, a, b)
        pout_im[:, lanes] = jnp.where(core == 0, b, a)


def gather_out(grad, pgrad):
    vmem = pl.BlockSpec(memory_space=pltpu.VMEM)
    dma = pltpu.SemaphoreType.DMA
    tile = jax.ShapeDtypeStruct((TR, N), F32)
    patch = jax.ShapeDtypeStruct((N, N), F32)
    came = pl.pallas_call(
        out_kernel,
        out_shape=(
            jax.ShapeDtypeStruct((2, TR, H), F32),
            jax.ShapeDtypeStruct((2, 2, N, H), F32),
            jax.ShapeDtypeStruct((2 * N, H), F32),
            jax.ShapeDtypeStruct((2 * N, H), F32),
        ),
        in_specs=[vmem, vmem],
        out_specs=(vmem, vmem, vmem, vmem),
        scratch_shapes=[
            pltpu.VMEM((2, N, H), F32),
            pltpu.VMEM((2, N, H), F32),
            pltpu.VMEM((2, N, H), F32),
            pltpu.VMEM((2 * N, H), F32),
            pltpu.VMEM((15, 32, H), F32),
            pltpu.VMEM((8, 32, H), F32),
            dma((2,)), dma((2,)), dma(()), dma(()), dma(()), dma(()),
            dma((2,)), dma((2,)), dma((2, 15)), dma((2, 15)), dma((7,)), dma((7,)),
        ],
        compiler_params=pltpu.CompilerParams(
            collective_id=1, has_side_effects=True, vmem_limit_bytes=20 << 20),
        name="gather_out",
    )(grad, pgrad)
    return pl.pallas_call(
        finish_kernel,
        out_shape=(tile, tile, patch, patch),
        in_specs=[vmem] * 5,
        out_specs=(vmem,) * 4,
        compiler_params=pltpu.CompilerParams(vmem_limit_bytes=20 << 20),
        name="finish",
    )(grad, *came)


def per_device(obj_re, obj_im, probe_re, probe_im, amplitude, offsets, counts):
    tables = jnp.asarray(half_dft_tables())
    reg, amp = halo(obj_re, obj_im, amplitude)
    grad, pgrad = positions(jnp.swapaxes(offsets, 2, 3), counts, reg, probe_re, probe_im, tables, amp)
    return gather_out(grad, pgrad)


def solution(mesh):
    return jax.shard_map(
        per_device,
        mesh=mesh,
        in_specs=(
            P("tx", "ty"),
            P("tx", "ty"),
            P(),
            P(),
            P("tx", "ty", None, None, None),
            P("tx", None, None, None),
            P("tx", None),
        ),
        out_specs=(P("tx", "ty"), P("tx", "ty"), P(), P()),
        check_vma=False,
    )
```

```python
import math

import jax
import jax.numpy as jnp
import ml_dtypes
import numpy as np
from jax import lax
from jax.experimental import pallas as pl
from jax.experimental.pallas import tpu as pltpu
from jax.sharding import PartitionSpec as P

N = 256
H = 128
TR = 512
SLOTS = 12
NTX = 128
ROWS = TR + N
MESH = pl.DeviceIdType.MESH
EDGE = NTX // 2
DETOUR = ((1, 0, 0), (2, 0, 1), (3, 1, 0), (3, 1, 1))
F32 = jnp.float32
BF16 = jnp.bfloat16


def half_dft_tables():
    n = np.arange(H, dtype=np.float64)[:, None]
    k = np.arange(H, dtype=np.float64)[None, :]
    tables = []
    for odd in (0, 1):
        angle = -2.0 * math.pi * (n * (2 * k + odd)) / N
        re, im = np.cos(angle) / 16.0, np.sin(angle) / 16.0
        tables.append(np.block([[re, im], [-im, re]]))
    both = np.stack([tables[0], tables[1], tables[0].T, tables[1].T])
    high = both.astype(ml_dtypes.bfloat16)
    low = (both - high.astype(np.float64)).astype(ml_dtypes.bfloat16)
    return np.stack([high, low])


def split(x):
    high = x.astype(BF16)
    return high, (x - high.astype(F32)).astype(BF16)


def dot(a, b):
    return jnp.dot(a, b, preferred_element_type=F32)


def halo_kernel(
    obj_re, obj_im, amp, reg, amp_out, raw, perm,
    ty_send, ty_recv, up_send, up_recv, diag_send, diag_recv, own_sem, raw_sem,
    relay, detour_send, detour_recv, relay_send,
):
    tx, ty = lax.axis_index("tx"), lax.axis_index("ty")
    up, down = lax.rem(tx + NTX - 1, NTX), lax.rem(tx + 1, NTX)
    partner = (tx, 1 - ty)
    barrier = pltpu.get_barrier_semaphore()
    for device in (partner, (up, ty), (down, ty)):
        pl.semaphore_signal(barrier, inc=1, device_id=device, device_id_type=MESH)
    is_relay = (tx > EDGE) & (tx <= EDGE + 6) & (lax.rem(tx, 2) == 0)

    @pl.when((tx == EDGE) | (tx == EDGE - 1))
    def _():
        for k in range(1, 4):
            pl.semaphore_signal(barrier, inc=1, device_id=(EDGE + 2 * k, ty), device_id_type=MESH)

    @pl.when(is_relay)
    def _():
        for device in (EDGE, EDGE - 1):
            pl.semaphore_signal(barrier, inc=1, device_id=(device, ty), device_id_type=MESH)

    raw_copies = []
    for t in range(2):
        c = pltpu.make_async_copy(amp.at[0, 0, :, :, pl.ds(t * H, H)], raw.at[t], raw_sem.at[t])
        c.start()
        raw_copies.append(c)
    own = []
    for p, obj in enumerate((obj_re, obj_im)):
        for t in range(2):
            c = pltpu.make_async_copy(
                obj.at[:, pl.ds(t * H, H)], reg.at[p, ty + t, pl.ds(0, TR)], own_sem.at[p, t])
            c.start()
            own.append(c)
    i, j = (lax.broadcasted_iota(jnp.int32, (N, N), d) for d in range(2))
    perm[...] = jnp.where(i == jnp.where(j < H, 2 * j, 2 * (j - H) + 1), 1.0, 0.0).astype(BF16)
    at_edge = (tx == EDGE) | (tx == EDGE - 1)

    @pl.when(at_edge)
    def _():
        pl.semaphore_wait(barrier, 6)

    @pl.when(is_relay)
    def _():
        pl.semaphore_wait(barrier, 5)

    @pl.when(jnp.logical_not(at_edge | is_relay))
    def _():
        pl.semaphore_wait(barrier, 3)


    edge = pl.multiple_of((1 - ty) * H, H)
    across = [[], []]
    for half in range(2):
        for p, obj in enumerate((obj_re, obj_im)):
            rows = pl.ds(half * N, N)
            c = pltpu.make_async_remote_copy(
                src_ref=obj.at[rows, pl.ds(edge, H)], dst_ref=reg.at[p, 2 * ty, rows],
                send_sem=ty_send.at[half, p], recv_sem=ty_recv.at[half, p],
                device_id=partner, device_id_type=MESH)
            c.start()
            across[half].append(c)
    objs = (obj_re, obj_im)
    blocks = [(p, t) for p in range(2) for t in range(2)]

    def below(p, t):
        return pltpu.make_async_remote_copy(
            src_ref=objs[p].at[pl.ds(0, N), pl.ds(t * H, H)], dst_ref=reg.at[p, ty + t, pl.ds(TR, N)],
            send_sem=up_send.at[p, t], recv_sem=up_recv.at[p, t],
            device_id=(up, ty), device_id_type=MESH)

    def detour(n):
        k, p, t = DETOUR[n]
        return pltpu.make_async_remote_copy(
            src_ref=objs[p].at[pl.ds(0, N), pl.ds(t * H, H)], dst_ref=relay.at[max(n - 2, 0)],
            send_sem=detour_send.at[n], recv_sem=detour_recv.at[max(n - 2, 0)],
            device_id=(EDGE + 2 * k, ty), device_id_type=MESH)

    def onward(n):
        _, p, t = DETOUR[n]
        return pltpu.make_async_remote_copy(
            src_ref=relay.at[max(n - 2, 0)], dst_ref=reg.at[p, ty + t, pl.ds(TR, N)],
            send_sem=relay_send.at[max(n - 2, 0)], recv_sem=up_recv.at[p, t],
            device_id=(EDGE - 1, ty), device_id_type=MESH)

    def diag(p):
        side = 2 - 2 * ty
        return pltpu.make_async_remote_copy(
            src_ref=reg.at[p, side, pl.ds(0, N)], dst_ref=reg.at[p, side, pl.ds(TR, N)],
            send_sem=diag_send.at[p], recv_sem=diag_recv.at[p],
            device_id=(up, ty), device_id_type=MESH)

    sends_up = (tx > 0) & (tx != EDGE)

    @pl.when(sends_up)
    def _():
        for p, t in blocks:
            below(p, t).start()

    @pl.when(tx == EDGE)
    def _():
        for n in range(4):
            detour(n).start()

    for n in range(4):

        @pl.when(tx == EDGE + 2 * DETOUR[n][0])
        def _():
            detour(n).wait_recv()
            onward(n).start()

    for c in raw_copies:
        c.wait()

    def sort_slot(i, carry):
        for h in range(2):
            rows = [raw[t, i, pl.ds(h, H, stride=2), :] for t in range(2)]
            high, low = split(jnp.concatenate(rows, axis=1))
            amp_out[i, pl.ds(h * H, H), :] = dot(high, perm[...]) + dot(low, perm[...])
        return carry

    lax.fori_loop(0, SLOTS // 2, sort_slot, 0)
    for p in range(2):
        across[0][p].wait()

        @pl.when(tx > 0)
        def _():
            diag(p).start()

    lax.fori_loop(SLOTS // 2, SLOTS, sort_slot, 0)

    for c in own + across[1]:
        c.wait()

    @pl.when(sends_up)
    def _():
        for p, t in blocks:
            below(p, t).wait_send()

    @pl.when(tx == EDGE)
    def _():
        for n in range(4):
            detour(n).wait_send()

    for n in range(4):

        @pl.when(tx == EDGE + 2 * DETOUR[n][0])
        def _():
            onward(n).wait_send()

    @pl.when(tx > 0)
    def _():
        for p in range(2):
            diag(p).wait_send()

    @pl.when(tx < NTX - 1)
    def _():
        for p, t in blocks:
            below(p, t).wait_recv()
        for p in range(2):
            diag(p).wait_recv()


def halo(obj_re, obj_im, amp):
    hbm, vmem = (pl.BlockSpec(memory_space=m) for m in (pltpu.HBM, pltpu.VMEM))
    dma = pltpu.SemaphoreType.DMA
    return pl.pallas_call(
        halo_kernel,
        out_shape=(
            pltpu.VMEM((2, 3, ROWS, H), F32),
            pltpu.VMEM((SLOTS, N, N), F32),
        ),
        in_specs=[hbm, hbm, hbm],
        out_specs=(vmem, vmem),
        scratch_shapes=[
            pltpu.VMEM((2, SLOTS, N, H), F32),
            pltpu.VMEM((N, N), BF16),
            dma((2, 2)), dma((2, 2)), dma((2, 2)), dma((2, 2)), dma((2,)), dma((2,)),
            dma((2, 2)), dma((2,)),
            pltpu.VMEM((2, N, H), F32), dma((4,)), dma((2,)), dma((2,)),
        ],
        compiler_params=pltpu.CompilerParams(
            collective_id=0, has_side_effects=True, vmem_limit_bytes=20 << 20),
        name="halo",
    )(*(pltpu.with_memory_space_constraint(x, pltpu.HBM) for x in (obj_re, obj_im, amp)))


def positions_kernel(
    offsets, counts, reg, probe_re, probe_im, tables, amp, grad, pgrad, win, sp, mid,
):
    tx, ty = lax.axis_index("tx"), lax.axis_index("ty")
    live = counts[0, ty]
    probe = (probe_re, probe_im)
    CH = 32

    grad[...] = jnp.zeros_like(grad)
    pgrad[...] = jnp.zeros_like(pgrad)
    lane = lax.broadcasted_iota(jnp.int32, (CH, H), 1)

    def put(s, q, rows, lanes, value):
        high, low = split(value)
        sp[s, 0, q, rows, lanes] = high
        sp[s, 1, q, rows, lanes] = low

    def right(s, q, which):
        high, low = sp[s, 0, q], sp[s, 1, q]
        mid[s, q] = dot(jnp.concatenate([high, low, high], axis=1),
                        jnp.concatenate([tables[0, which], tables[0, which], tables[1, which]], axis=0))

    def left(s, q, which):
        high, low = sp[s, 0, q], sp[s, 1, q]
        mid[s, q] = dot(jnp.concatenate([tables[0, which], tables[1, which], tables[0, which]], axis=1),
                        jnp.concatenate([high, high, low], axis=0))

    def lanes(t):
        return pl.ds(t * H, H)

    def enter(s, place):
        row_at, col_at = place
        back = lax.rem(H - col_at, H)
        from_next = lane >= H - col_at
        for j in range(N // CH):
            rows = pl.ds(j * CH, CH)
            ex = [[None, None], [None, None]]
            w = [[None, None], [None, None]]
            for p in range(2):
                turned = [pltpu.roll(reg[p, t, pl.ds(row_at + j * CH, CH), :], back, 1) for t in range(3)]
                for t in range(2):
                    w[p][t] = jnp.where(from_next, turned[t + 1], turned[t])
                    win[s, p, t, rows, :] = w[p][t]
            for t in range(2):
                pr, pi = probe_re[rows, lanes(t)], probe_im[rows, lanes(t)]
                ex[0][t] = pr * w[0][t] - pi * w[1][t]
                ex[1][t] = pr * w[1][t] + pi * w[0][t]
            for p in range(2):
                put(s, 0, rows, lanes(p), ex[p][0] + ex[p][1])
                put(s, 1, rows, lanes(p), ex[p][0] - ex[p][1])

    def fold_rows(s):
        for j in range(H // CH):
            for q in range(2):
                for p in range(2):
                    top = mid[s, q, pl.ds(j * CH, CH), lanes(p)]
                    low = mid[s, q, pl.ds(H + j * CH, CH), lanes(p)]
                    rows = pl.ds(p * H + j * CH, CH)
                    put(s, 0, rows, lanes(q), top + low)
                    put(s, 1, rows, lanes(q), top - low)

    def compare(s, i, used):
        for j in range(H // CH):
            for h in range(2):
                rows_re, rows_im = pl.ds(j * CH, CH), pl.ds(H + j * CH, CH)
                re, im = mid[s, h, rows_re, :], mid[s, h, rows_im, :]
                measured = amp[i, pl.ds(h * H + j * CH, CH), :]
                keep = 1.0 - measured * lax.rsqrt(jnp.maximum(re * re + im * im, 1.0))
                keep = jnp.where(used, keep, 0.0)
                put(s, h, rows_re, slice(None), re * keep)
                put(s, h, rows_im, slice(None), im * keep)

    def unfold_rows(s):
        for j in range(H // CH):
            for p in range(2):
                for q in range(2):
                    a = mid[s, 0, pl.ds(p * H + j * CH, CH), lanes(q)]
                    b = mid[s, 1, pl.ds(p * H + j * CH, CH), lanes(q)]
                    put(s, q, pl.ds(j * CH, CH), lanes(p), a + b)
                    put(s, q, pl.ds(H + j * CH, CH), lanes(p), a - b)

    def leave(s, place):
        row_at, col_at = place
        ahead = lax.rem(col_at, H)
        to_next = lane < col_at
        for j in range(N // CH):
            rows = pl.ds(j * CH, CH)
            g = [[None, None], [None, None]]
            for t in range(2):
                chi = []
                for p in range(2):
                    a, b = mid[s, 0, rows, lanes(p)], mid[s, 1, rows, lanes(p)]
                    chi.append(a + b if t == 0 else a - b)
                pr, pi = probe_re[rows, lanes(t)], probe_im[rows, lanes(t)]
                wr, wi = win[s, 0, t, rows, :], win[s, 1, t, rows, :]
                g[0][t] = pltpu.roll(pr * chi[0] + pi * chi[1], ahead, 1)
                g[1][t] = pltpu.roll(pr * chi[1] - pi * chi[0], ahead, 1)
                pgrad[0, t, rows, :] += wr * chi[0] + wi * chi[1]
                pgrad[1, t, rows, :] += wr * chi[1] - wi * chi[0]
            at = pl.ds(row_at + j * CH, CH)
            for p in range(2):
                grad[p, 0, at, :] += jnp.where(to_next, 0.0, g[p][0])
                grad[p, 1, at, :] += jnp.where(to_next, g[p][0], g[p][1])
                grad[p, 2, at, :] += jnp.where(to_next, g[p][1], 0.0)

    def place_of(i):
        return offsets[0, ty, 0, i] - tx * TR, offsets[0, ty, 1, i] - ty * H

    def pair(k, carry):
        ids = [2 * k, jnp.minimum(2 * k + 1, live - 1)]
        used = [True, 2 * k + 1 < live]
        places = [place_of(i) for i in ids]
        steps = [
            lambda s: enter(s, places[s]),
            lambda s: [right(s, q, q) for q in range(2)],
            lambda s: fold_rows(s),
            lambda s: [left(s, h, 2 + h) for h in range(2)],
            lambda s: compare(s, ids[s], used[s]),
            lambda s: [left(s, h, h) for h in range(2)],
            lambda s: unfold_rows(s),
            lambda s: [right(s, q, 2 + q) for q in range(2)],
            lambda s: leave(s, places[s]),
        ]
        steps[0](0)
        for n in range(1, len(steps)):
            steps[n](0)
            steps[n - 1](1)
        steps[-1](1)
        return carry

    lax.fori_loop(0, (live + 1) // 2, pair, 0)


def positions(offsets, counts, reg, probe_re, probe_im, tables, amp):
    smem = pl.BlockSpec(memory_space=pltpu.SMEM)
    vmem = pl.BlockSpec(memory_space=pltpu.VMEM)
    return pl.pallas_call(
        positions_kernel,
        out_shape=(
            pltpu.VMEM((2, 3, ROWS, H), F32),
            pltpu.VMEM((2, 2, N, H), F32),
        ),
        in_specs=[smem, smem, vmem, vmem, vmem, vmem, vmem],
        out_specs=(vmem, vmem),
        scratch_shapes=[
            pltpu.VMEM((2, 2, 2, N, H), F32),
            pltpu.VMEM((2, 2, 2, N, N), BF16),
            pltpu.VMEM((2, 2, N, N), F32),
        ],
        compiler_params=pltpu.CompilerParams(vmem_limit_bytes=20 << 20),
        name="positions",
    )(offsets, counts, reg, probe_re, probe_im, tables, amp)


def out_kernel(
    grad, pgrad, out_ty, out_up, out_full, out_other,
    came_diag, edge, core_in, acc, yz_in, shared,
    ty_send, ty_recv, up_send, up_recv, diag_send, diag_recv,
    core_send, core_recv, yz_send, yz_recv, far_send, far_recv,
):
    tx, ty = lax.axis_index("tx"), lax.axis_index("ty")
    up, down = lax.rem(tx + NTX - 1, NTX), lax.rem(tx + 1, NTX)
    partner = (tx, 1 - ty)
    core, y, z, x_lo = lax.rem(tx, 2), lax.rem(tx // 2, 4), lax.rem(tx // 8, 8), tx // 64
    x = ty * 2 + x_lo

    def at(core_, y_, z_, x_):
        return (((lax.rem(x_, 2) * 8 + z_) * 4 + y_) * 2 + core_, x_ // 2)

    core_mate = at(1 - core, y, z, x)
    z_low, z_high = lax.rem(z, 4), z // 4
    steps = [(i, j) for i in range(4) for j in range(4) if i or j]
    steps.sort(key=lambda s: -(min(s[0], 4 - s[0]) + min(s[1], 4 - s[1])))
    yz_at = [(lax.rem(y + i, 4), lax.rem(z_low + j, 4)) for i, j in steps]
    yz_mates = [at(core, i, z_high * 4 + j, x) for i, j in yz_at]
    hops = [(1, 2), (1, 1), (1, 3), (1, 0), (0, 2), (0, 1), (0, 3)]
    far_mates = [at(core, y, lax.rem(z_high + i, 2) * 4 + z_low, lax.rem(x + j, 4)) for i, j in hops]
    greeted = far_mates + yz_mates + [partner, (up, ty), (down, ty), core_mate]
    barrier = pltpu.get_barrier_semaphore()
    for device in greeted:
        pl.semaphore_signal(barrier, inc=1, device_id=device, device_id_type=MESH)
    pl.semaphore_wait(barrier, len(greeted))

    def make(src, dst, send_sem, recv_sem, device):
        return pltpu.make_async_remote_copy(
            src_ref=src, dst_ref=dst, send_sem=send_sem, recv_sem=recv_sem,
            device_id=device, device_id_type=MESH)

    def send(*args):
        c = make(*args)
        c.start()
        return c

    def part(i, j):
        return pl.ds(pl.multiple_of((i * 4 + j) * 32, 32), 32)

    side = 2 - 2 * ty
    core_copy = send(pgrad.at[1 - core], core_in, core_send.at[0], core_recv.at[0], core_mate)
    diag = make(grad.at[:, side, pl.ds(TR, N)], came_diag, diag_send, diag_recv, (down, ty))
    below = make(grad.at[:, pl.ds(ty, 2), pl.ds(TR, N)], out_up, up_send, up_recv, (down, ty))

    @pl.when(tx < NTX - 1)
    def _():
        diag.start()

    @pl.when(tx == 0)
    def _():
        came_diag[...] = jnp.zeros_like(came_diag)
        out_up[...] = jnp.zeros_like(out_up)

    far_rows = send(
        grad.at[:, side, pl.ds(N, N)], out_ty.at[:, pl.ds(N, N)], ty_send.at[1], ty_recv.at[1], partner)
    core_copy.wait()
    for t in range(2):
        acc[pl.ds(t * N, N), :] = pgrad[core, t] + core_in[t]
    yz_copies = [
        send(acc.at[part(*yz_at[d])], yz_in.at[d], yz_send.at[0, d], yz_recv.at[0, d], yz_mates[d])
        for d in range(15)]

    @pl.when(tx > 0)
    def _():
        diag.wait_recv()

    for p in range(2):
        edge[p] = grad[p, side, pl.ds(0, N)] + came_diag[p]
    for c in yz_copies:
        c.wait()
    total = acc[part(y, z_low), :]
    for d in range(15):
        total = total + yz_in[d]
    mine = x * 2 + z_high
    shared[mine] = total
    far_copies = [
        send(shared.at[mine], shared.at[mine], far_send.at[d], far_recv.at[d], far_mates[d]) for d in range(7)]

    @pl.when(tx < NTX - 1)
    def _():
        below.start()

    for c in far_copies:
        c.wait()
    total = shared[0]
    for d in range(1, 8):
        total = total + shared[d]
    out_full[part(y, z_low), :] = total * (1.0 / (NTX * 2 * SLOTS))
    yz_copies = [
        send(out_full.at[part(y, z_low)], out_full.at[part(y, z_low)],
             yz_send.at[1, d], yz_recv.at[1, d], yz_mates[d])
        for d in range(15)]
    near_rows = send(edge, out_ty.at[:, pl.ds(0, N)], ty_send.at[0], ty_recv.at[0], partner)
    for c in yz_copies:
        c.wait()
    core_copy = send(out_full, out_other, core_send.at[1], core_recv.at[1], core_mate)

    @pl.when(tx < NTX - 1)
    def _():
        diag.wait_send()
        below.wait_send()

    @pl.when(tx > 0)
    def _():
        below.wait_recv()

    far_rows.wait()
    near_rows.wait()
    core_copy.wait()


def finish_kernel(grad, came_ty, came_up, full, other, out_re, out_im, pout_re, pout_im):
    core, ty = lax.rem(lax.axis_index("tx"), 2), lax.axis_index("ty")
    for p, out in enumerate((out_re, out_im)):
        for t in range(2):
            lanes = pl.ds(t * H, H)
            mine = ty == 1 - t
            ty_rows = [jnp.where(mine, came_ty[p, pl.ds(h * N, N)], 0.0) for h in range(2)]
            out[pl.ds(0, N), lanes] = grad[p, ty + t, pl.ds(0, N)] + came_up[p, t] + ty_rows[0]
            out[pl.ds(N, N), lanes] = grad[p, ty + t, pl.ds(N, N)] + ty_rows[1]
    for t in range(2):
        rows, lanes = pl.ds(t * N, N), pl.ds(t * H, H)
        a, b = full[rows, :], other[rows, :]
        pout_re[:, lanes] = jnp.where(core == 0, a, b)
        pout_im[:, lanes] = jnp.where(core == 0, b, a)


def gather_out(grad, pgrad):
    vmem = pl.BlockSpec(memory_space=pltpu.VMEM)
    dma = pltpu.SemaphoreType.DMA
    tile = jax.ShapeDtypeStruct((TR, N), F32)
    patch = jax.ShapeDtypeStruct((N, N), F32)
    came = pl.pallas_call(
        out_kernel,
        out_shape=(
            jax.ShapeDtypeStruct((2, TR, H), F32),
            jax.ShapeDtypeStruct((2, 2, N, H), F32),
            jax.ShapeDtypeStruct((2 * N, H), F32),
            jax.ShapeDtypeStruct((2 * N, H), F32),
        ),
        in_specs=[vmem, vmem],
        out_specs=(vmem, vmem, vmem, vmem),
        scratch_shapes=[
            pltpu.VMEM((2, N, H), F32),
            pltpu.VMEM((2, N, H), F32),
            pltpu.VMEM((2, N, H), F32),
            pltpu.VMEM((2 * N, H), F32),
            pltpu.VMEM((15, 32, H), F32),
            pltpu.VMEM((8, 32, H), F32),
            dma((2,)), dma((2,)), dma(()), dma(()), dma(()), dma(()),
            dma((2,)), dma((2,)), dma((2, 15)), dma((2, 15)), dma((7,)), dma((7,)),
        ],
        compiler_params=pltpu.CompilerParams(
            collective_id=1, has_side_effects=True, vmem_limit_bytes=20 << 20),
        name="gather_out",
    )(grad, pgrad)
    return pl.pallas_call(
        finish_kernel,
        out_shape=(tile, tile, patch, patch),
        in_specs=[vmem] * 5,
        out_specs=(vmem,) * 4,
        compiler_params=pltpu.CompilerParams(vmem_limit_bytes=20 << 20),
        name="finish",
    )(grad, *came)


def per_device(obj_re, obj_im, probe_re, probe_im, amplitude, offsets, counts):
    tables = jnp.asarray(half_dft_tables())
    reg, amp = halo(obj_re, obj_im, amplitude)
    grad, pgrad = positions(jnp.swapaxes(offsets, 2, 3), counts, reg, probe_re, probe_im, tables, amp)
    return gather_out(grad, pgrad)


def solution(mesh):
    return jax.shard_map(
        per_device,
        mesh=mesh,
        in_specs=(
            P("tx", "ty"),
            P("tx", "ty"),
            P(),
            P(),
            P("tx", "ty", None, None, None),
            P("tx", None, None, None),
            P("tx", None),
        ),
        out_specs=(P("tx", "ty"), P("tx", "ty"), P(), P()),
        check_vma=False,
    )
```

```python
import math

import jax
import jax.numpy as jnp
import ml_dtypes
import numpy as np
from jax import lax
from jax.experimental import pallas as pl
from jax.experimental.pallas import tpu as pltpu
from jax.sharding import PartitionSpec as P

N = 256
H = 128
TR = 512
SLOTS = 12
NTX = 128
ROWS = TR + N
MESH = pl.DeviceIdType.MESH
CH = 32
LAST = 4
PIECE = TR // 8
EDGE = NTX // 2
DETOUR = ((1, 0, 0), (2, 0, 1), (3, 1, 0), (3, 1, 1))
F32 = jnp.float32
BF16 = jnp.bfloat16


def half_dft_tables():
    n = np.arange(H, dtype=np.float64)[:, None]
    k = np.arange(H, dtype=np.float64)[None, :]
    tables = []
    for odd in (0, 1):
        angle = -2.0 * math.pi * (n * (2 * k + odd)) / N
        re, im = np.cos(angle) / 16.0, np.sin(angle) / 16.0
        tables.append(np.block([[re, im], [-im, re]]))
    both = np.stack([tables[0], tables[1], tables[0].T, tables[1].T])
    high = both.astype(ml_dtypes.bfloat16)
    low = (both - high.astype(np.float64)).astype(ml_dtypes.bfloat16)
    return np.stack([high, low])


def split(x):
    high = x.astype(BF16)
    return high, (x - high.astype(F32)).astype(BF16)


def dot(a, b):
    return jnp.dot(a, b, preferred_element_type=F32)


def halo_kernel(
    obj_re, obj_im, amp, reg, amp_out, raw, perm,
    ty_send, ty_recv, up_send, up_recv, diag_send, diag_recv, own_sem, raw_sem,
    relay, detour_send, detour_recv, relay_send,
):
    tx, ty = lax.axis_index("tx"), lax.axis_index("ty")
    up, down = lax.rem(tx + NTX - 1, NTX), lax.rem(tx + 1, NTX)
    partner = (tx, 1 - ty)
    barrier = pltpu.get_barrier_semaphore()
    for device in (partner, (up, ty), (down, ty)):
        pl.semaphore_signal(barrier, inc=1, device_id=device, device_id_type=MESH)
    is_relay = (tx > EDGE) & (tx <= EDGE + 6) & (lax.rem(tx, 2) == 0)

    @pl.when((tx == EDGE) | (tx == EDGE - 1))
    def _():
        for k in range(1, 4):
            pl.semaphore_signal(barrier, inc=1, device_id=(EDGE + 2 * k, ty), device_id_type=MESH)

    @pl.when(is_relay)
    def _():
        for device in (EDGE, EDGE - 1):
            pl.semaphore_signal(barrier, inc=1, device_id=(device, ty), device_id_type=MESH)

    raw_copies = []
    for t in range(2):
        c = pltpu.make_async_copy(amp.at[0, 0, :, :, pl.ds(t * H, H)], raw.at[t], raw_sem.at[t])
        c.start()
        raw_copies.append(c)
    own = []
    for p, obj in enumerate((obj_re, obj_im)):
        for t in range(2):
            c = pltpu.make_async_copy(
                obj.at[:, pl.ds(t * H, H)], reg.at[p, ty + t, pl.ds(0, TR)], own_sem.at[p, t])
            c.start()
            own.append(c)
    i, j = (lax.broadcasted_iota(jnp.int32, (N, N), d) for d in range(2))
    perm[...] = jnp.where(i == jnp.where(j < H, 2 * j, 2 * (j - H) + 1), 1.0, 0.0).astype(BF16)
    at_edge = (tx == EDGE) | (tx == EDGE - 1)

    @pl.when(at_edge)
    def _():
        pl.semaphore_wait(barrier, 6)

    @pl.when(is_relay)
    def _():
        pl.semaphore_wait(barrier, 5)

    @pl.when(jnp.logical_not(at_edge | is_relay))
    def _():
        pl.semaphore_wait(barrier, 3)


    edge = pl.multiple_of((1 - ty) * H, H)
    across = [[], []]
    for half in range(2):
        for p, obj in enumerate((obj_re, obj_im)):
            rows = pl.ds(half * N, N)
            c = pltpu.make_async_remote_copy(
                src_ref=obj.at[rows, pl.ds(edge, H)], dst_ref=reg.at[p, 2 * ty, rows],
                send_sem=ty_send.at[half, p], recv_sem=ty_recv.at[half, p],
                device_id=partner, device_id_type=MESH)
            c.start()
            across[half].append(c)
    objs = (obj_re, obj_im)
    blocks = [(p, t) for p in range(2) for t in range(2)]

    def below(p, t):
        return pltpu.make_async_remote_copy(
            src_ref=objs[p].at[pl.ds(0, N), pl.ds(t * H, H)], dst_ref=reg.at[p, ty + t, pl.ds(TR, N)],
            send_sem=up_send.at[p, t], recv_sem=up_recv.at[p, t],
            device_id=(up, ty), device_id_type=MESH)

    def detour(n):
        k, p, t = DETOUR[n]
        return pltpu.make_async_remote_copy(
            src_ref=objs[p].at[pl.ds(0, N), pl.ds(t * H, H)], dst_ref=relay.at[max(n - 2, 0)],
            send_sem=detour_send.at[n], recv_sem=detour_recv.at[max(n - 2, 0)],
            device_id=(EDGE + 2 * k, ty), device_id_type=MESH)

    def onward(n):
        _, p, t = DETOUR[n]
        return pltpu.make_async_remote_copy(
            src_ref=relay.at[max(n - 2, 0)], dst_ref=reg.at[p, ty + t, pl.ds(TR, N)],
            send_sem=relay_send.at[max(n - 2, 0)], recv_sem=up_recv.at[p, t],
            device_id=(EDGE - 1, ty), device_id_type=MESH)

    def diag(p):
        side = 2 - 2 * ty
        return pltpu.make_async_remote_copy(
            src_ref=reg.at[p, side, pl.ds(0, N)], dst_ref=reg.at[p, side, pl.ds(TR, N)],
            send_sem=diag_send.at[p], recv_sem=diag_recv.at[p],
            device_id=(up, ty), device_id_type=MESH)

    sends_up = (tx > 0) & (tx != EDGE)

    @pl.when(sends_up)
    def _():
        for p, t in blocks:
            below(p, t).start()

    @pl.when(tx == EDGE)
    def _():
        for n in range(4):
            detour(n).start()

    for n in range(4):

        @pl.when(tx == EDGE + 2 * DETOUR[n][0])
        def _():
            detour(n).wait_recv()
            onward(n).start()

    for c in raw_copies:
        c.wait()

    def sort_slot(i, carry):
        for h in range(2):
            rows = [raw[t, i, pl.ds(h, H, stride=2), :] for t in range(2)]
            high, low = split(jnp.concatenate(rows, axis=1))
            amp_out[i, pl.ds(h * H, H), :] = dot(high, perm[...]) + dot(low, perm[...])
        return carry

    lax.fori_loop(0, SLOTS // 2, sort_slot, 0)
    for p in range(2):
        across[0][p].wait()

        @pl.when(tx > 0)
        def _():
            diag(p).start()

    lax.fori_loop(SLOTS // 2, SLOTS, sort_slot, 0)

    for c in own + across[1]:
        c.wait()

    @pl.when(sends_up)
    def _():
        for p, t in blocks:
            below(p, t).wait_send()

    @pl.when(tx == EDGE)
    def _():
        for n in range(4):
            detour(n).wait_send()

    for n in range(4):

        @pl.when(tx == EDGE + 2 * DETOUR[n][0])
        def _():
            onward(n).wait_send()

    @pl.when(tx > 0)
    def _():
        for p in range(2):
            diag(p).wait_send()

    @pl.when(tx < NTX - 1)
    def _():
        for p, t in blocks:
            below(p, t).wait_recv()
        for p in range(2):
            diag(p).wait_recv()


def halo(obj_re, obj_im, amp):
    hbm, vmem = (pl.BlockSpec(memory_space=m) for m in (pltpu.HBM, pltpu.VMEM))
    dma = pltpu.SemaphoreType.DMA
    return pl.pallas_call(
        halo_kernel,
        out_shape=(
            pltpu.VMEM((2, 3, ROWS, H), F32),
            pltpu.VMEM((SLOTS, N, N), F32),
        ),
        in_specs=[hbm, hbm, hbm],
        out_specs=(vmem, vmem),
        scratch_shapes=[
            pltpu.VMEM((2, SLOTS, N, H), F32),
            pltpu.VMEM((N, N), BF16),
            dma((2, 2)), dma((2, 2)), dma((2, 2)), dma((2, 2)), dma((2,)), dma((2,)),
            dma((2, 2)), dma((2,)),
            pltpu.VMEM((2, N, H), F32), dma((4,)), dma((2,)), dma((2,)),
        ],
        compiler_params=pltpu.CompilerParams(
            collective_id=0, has_side_effects=True, vmem_limit_bytes=20 << 20),
        name="halo",
    )(*(pltpu.with_memory_space_constraint(x, pltpu.HBM) for x in (obj_re, obj_im, amp)))


def pair_of_positions(reg, probe_re, probe_im, tables, amp, win, sp, mid):
    lane = lax.broadcasted_iota(jnp.int32, (CH, H), 1)

    def put(s, q, rows, lanes, value):
        high, low = split(value)
        sp[s, 0, q, rows, lanes] = high
        sp[s, 1, q, rows, lanes] = low

    def right(s, q, which):
        high, low = sp[s, 0, q], sp[s, 1, q]
        mid[s, q] = dot(jnp.concatenate([high, low, high], axis=1),
                        jnp.concatenate([tables[0, which], tables[0, which], tables[1, which]], axis=0))

    def left(s, q, which):
        high, low = sp[s, 0, q], sp[s, 1, q]
        mid[s, q] = dot(jnp.concatenate([tables[0, which], tables[1, which], tables[0, which]], axis=1),
                        jnp.concatenate([high, high, low], axis=0))

    def lanes(t):
        return pl.ds(t * H, H)

    def enter(s, place):
        row_at, col_at = place
        back = lax.rem(H - col_at, H)
        from_next = lane >= H - col_at
        for j in range(N // CH):
            rows = pl.ds(j * CH, CH)
            ex = [[None, None], [None, None]]
            w = [[None, None], [None, None]]
            for p in range(2):
                turned = [pltpu.roll(reg[p, t, pl.ds(row_at + j * CH, CH), :], back, 1) for t in range(3)]
                for t in range(2):
                    w[p][t] = jnp.where(from_next, turned[t + 1], turned[t])
                    win[s, p, t, rows, :] = w[p][t]
            for t in range(2):
                pr, pi = probe_re[rows, lanes(t)], probe_im[rows, lanes(t)]
                ex[0][t] = pr * w[0][t] - pi * w[1][t]
                ex[1][t] = pr * w[1][t] + pi * w[0][t]
            for p in range(2):
                put(s, 0, rows, lanes(p), ex[p][0] + ex[p][1])
                put(s, 1, rows, lanes(p), ex[p][0] - ex[p][1])

    def fold_rows(s):
        for j in range(H // CH):
            for q in range(2):
                for p in range(2):
                    top = mid[s, q, pl.ds(j * CH, CH), lanes(p)]
                    low = mid[s, q, pl.ds(H + j * CH, CH), lanes(p)]
                    rows = pl.ds(p * H + j * CH, CH)
                    put(s, 0, rows, lanes(q), top + low)
                    put(s, 1, rows, lanes(q), top - low)

    def compare(s, i, used):
        for j in range(H // CH):
            for h in range(2):
                rows_re, rows_im = pl.ds(j * CH, CH), pl.ds(H + j * CH, CH)
                re, im = mid[s, h, rows_re, :], mid[s, h, rows_im, :]
                measured = amp[i, pl.ds(h * H + j * CH, CH), :]
                keep = 1.0 - measured * lax.rsqrt(jnp.maximum(re * re + im * im, 1.0))
                keep = jnp.where(used, keep, 0.0)
                put(s, h, rows_re, slice(None), re * keep)
                put(s, h, rows_im, slice(None), im * keep)

    def unfold_rows(s):
        for j in range(H // CH):
            for p in range(2):
                for q in range(2):
                    a = mid[s, 0, pl.ds(p * H + j * CH, CH), lanes(q)]
                    b = mid[s, 1, pl.ds(p * H + j * CH, CH), lanes(q)]
                    put(s, q, pl.ds(j * CH, CH), lanes(p), a + b)
                    put(s, q, pl.ds(H + j * CH, CH), lanes(p), a - b)

    def leave(s, place, add_rows, add_probe):
        row_at, col_at = place
        ahead = lax.rem(col_at, H)
        to_next = lane < col_at
        for j in range(N // CH):
            rows = pl.ds(j * CH, CH)
            g = [[None, None], [None, None]]
            for t in range(2):
                chi = []
                for p in range(2):
                    a, b = mid[s, 0, rows, lanes(p)], mid[s, 1, rows, lanes(p)]
                    chi.append(a + b if t == 0 else a - b)
                pr, pi = probe_re[rows, lanes(t)], probe_im[rows, lanes(t)]
                wr, wi = win[s, 0, t, rows, :], win[s, 1, t, rows, :]
                g[0][t] = pltpu.roll(pr * chi[0] + pi * chi[1], ahead, 1)
                g[1][t] = pltpu.roll(pr * chi[1] - pi * chi[0], ahead, 1)
                add_probe(t, rows, wr * chi[0] + wi * chi[1], wr * chi[1] - wi * chi[0])
            for p in range(2):
                add_rows(s, row_at, j, p, (
                    jnp.where(to_next, 0.0, g[p][0]),
                    jnp.where(to_next, g[p][0], g[p][1]),
                    jnp.where(to_next, g[p][1], 0.0)))

    def pair(places, ids, used, add_rows, add_probe):
        stages = [
            lambda s: enter(s, places[s]),
            lambda s: [right(s, q, q) for q in range(2)],
            lambda s: fold_rows(s),
            lambda s: [left(s, h, 2 + h) for h in range(2)],
            lambda s: compare(s, ids[s], used[s]),
            lambda s: [left(s, h, h) for h in range(2)],
            lambda s: unfold_rows(s),
            lambda s: [right(s, q, 2 + q) for q in range(2)],
            lambda s: leave(s, places[s], add_rows, add_probe),
        ]
        stages[0](0)
        for n in range(1, len(stages)):
            stages[n](0)
            stages[n - 1](1)
        stages[-1](1)

    return pair


def place_of(offsets, tx, ty, i):
    row_at, col_at = offsets[0, ty, 0, i] - tx * TR, offsets[0, ty, 1, i] - ty * H
    return jnp.clip(row_at, 0, TR - 1), jnp.clip(col_at, 0, H)


def positions_kernel(
    offsets, counts, reg, probe_re, probe_im, tables, amp, grad, pgrad, win, sp, mid,
):
    tx, ty = lax.axis_index("tx"), lax.axis_index("ty")
    here = jnp.maximum(counts[0, ty] - LAST, 0)
    grad[...] = jnp.zeros_like(grad)
    pgrad[...] = jnp.zeros_like(pgrad)
    pair = pair_of_positions(reg, probe_re, probe_im, tables, amp, win, sp, mid)

    def add_rows(s, row_at, j, p, tiles):
        at = pl.ds(row_at + j * CH, CH)
        for t in range(3):
            grad[p, t, at, :] += tiles[t]

    def add_probe(t, rows, re, im):
        pgrad[0, t, rows, :] += re
        pgrad[1, t, rows, :] += im

    def step(k, carry):
        ids = [2 * k, jnp.minimum(2 * k + 1, here - 1)]
        pair([place_of(offsets, tx, ty, i) for i in ids], ids, [True, 2 * k + 1 < here], add_rows, add_probe)
        return carry

    lax.fori_loop(0, (here + 1) // 2, step, 0)


def positions(offsets, counts, reg, probe_re, probe_im, tables, amp):
    smem = pl.BlockSpec(memory_space=pltpu.SMEM)
    vmem = pl.BlockSpec(memory_space=pltpu.VMEM)
    return pl.pallas_call(
        positions_kernel,
        out_shape=(
            pltpu.VMEM((2, 3, ROWS, H), F32),
            pltpu.VMEM((2, 2, N, H), F32),
        ),
        in_specs=[smem, smem, vmem, vmem, vmem, vmem, vmem],
        out_specs=(vmem, vmem),
        scratch_shapes=[
            pltpu.VMEM((2, 2, 2, N, H), F32),
            pltpu.VMEM((2, 2, 2, N, N), BF16),
            pltpu.VMEM((2, 2, N, N), F32),
        ],
        compiler_params=pltpu.CompilerParams(vmem_limit_bytes=20 << 20),
        name="positions",
    )(offsets, counts, reg, probe_re, probe_im, tables, amp)


def out_kernel(
    offsets, counts, reg, probe_re, probe_im, tables, amp, grad_in, pgrad_in, grad, out_ty, out_up, out_full, out_other,
    pgrad, placed, win, sp, mid, came_diag, edge, core_in, acc, xy_in, shared,
    ty_send, ty_recv, up_send, up_recv, diag_send, diag_recv,
    core_send, core_recv, xy_send, xy_recv, z_send, z_recv,
):
    tx, ty = lax.axis_index("tx"), lax.axis_index("ty")
    up, down = lax.rem(tx + NTX - 1, NTX), lax.rem(tx + 1, NTX)
    partner = (tx, 1 - ty)
    core, y, z, x_lo = lax.rem(tx, 2), lax.rem(tx // 2, 4), lax.rem(tx // 8, 8), tx // 64
    x = ty * 2 + x_lo

    def at(core_, y_, z_, x_):
        return (((lax.rem(x_, 2) * 8 + z_) * 4 + y_) * 2 + core_, x_ // 2)

    core_mate = at(1 - core, y, z, x)
    steps = [(i, j) for i in range(4) for j in range(4) if i or j]
    steps.sort(key=lambda s: -(min(s[0], 4 - s[0]) + min(s[1], 4 - s[1])))
    xy_at = [(lax.rem(y + i, 4), lax.rem(x + j, 4)) for i, j in steps]
    xy_mates = [at(core, i, z, j) for i, j in xy_at]
    z_mates = [at(core, y, lax.rem(z + d, 8), x) for d in (4, 3, 5, 2, 6, 1, 7)]
    greeted = z_mates + xy_mates + [partner, (up, ty), (down, ty), core_mate]
    barrier = pltpu.get_barrier_semaphore()
    for device in greeted:
        pl.semaphore_signal(barrier, inc=1, device_id=device, device_id_type=MESH)

    live = counts[0, ty]
    for margin in (0, CH + N):
        placed[:, :, :, pl.ds(margin, CH), :] = jnp.zeros((LAST, 2, 3, CH, H), F32)
    pgrad[...] = pgrad_in[...]
    pair = pair_of_positions(reg, probe_re, probe_im, tables, amp, win, sp, mid)

    def add_probe(t, rows, re, im):
        pgrad[0, t, rows, :] += re
        pgrad[1, t, rows, :] += im

    def id_of(n):
        return jnp.maximum(live - LAST + n, 0)

    def step(k, carry):
        ids = [id_of(2 * k + s) for s in range(2)]

        def add_rows(s, row_at, j, p, tiles):
            for t in range(3):
                placed[2 * k + s, p, t, pl.ds(CH + j * CH, CH), :] = tiles[t]

        pair([place_of(offsets, tx, ty, i) for i in ids], ids,
             [live - LAST + 2 * k + s >= 0 for s in range(2)], add_rows, add_probe)
        return carry

    lax.fori_loop(0, LAST // 2, step, 0)
    pl.semaphore_wait(barrier, len(greeted))

    def make(src, dst, send_sem, recv_sem, device):
        return pltpu.make_async_remote_copy(
            src_ref=src, dst_ref=dst, send_sem=send_sem, recv_sem=recv_sem,
            device_id=device, device_id_type=MESH)

    def send(*args):
        c = make(*args)
        c.start()
        return c

    def part(i, j):
        return pl.ds(pl.multiple_of((i * 4 + j) * 32, 32), 32)

    side = 2 - 2 * ty
    core_copy = send(pgrad.at[1 - core], core_in, core_send.at[0], core_recv.at[0], core_mate)

    firsts = [place_of(offsets, tx, ty, id_of(n))[0] for n in range(LAST)]

    def place_rows(j, carry):
        rows = pl.ds(pl.multiple_of(j * CH, CH), CH)
        for p in range(2):
            for t in range(3):
                total = grad_in[p, t, rows, :]
                for n in range(LAST):
                    at = jnp.clip(j * CH - firsts[n] + CH, 0, CH + N)
                    total = total + placed[n, p, t, pl.ds(at, CH), :]
                grad[p, t, rows, :] = total
        return carry

    lax.fori_loop(0, ROWS // CH, place_rows, 0)
    diag = make(grad.at[:, side, pl.ds(TR, N)], came_diag, diag_send, diag_recv, (down, ty))
    below = make(grad.at[:, pl.ds(ty, 2), pl.ds(TR, N)], out_up, up_send, up_recv, (down, ty))

    @pl.when(tx < NTX - 1)
    def _():
        diag.start()

    @pl.when(tx == 0)
    def _():
        came_diag[...] = jnp.zeros_like(came_diag)
        out_up[...] = jnp.zeros_like(out_up)

    pieces = []

    def send_pieces(count):
        for _ in range(count):
            n = (len(pieces) + 4) % 8
            rows = pl.ds(n * PIECE, PIECE)
            src = grad.at[:, side, rows] if n >= 4 else edge.at[:, rows]
            pieces.append(send(src, out_ty.at[:, rows], ty_send.at[n], ty_recv.at[n], partner))

    def start_below():
        @pl.when(tx < NTX - 1)
        def _():
            below.start()

    def add_edge():
        @pl.when(tx > 0)
        def _():
            diag.wait_recv()

        for p in range(2):
            edge[p] = grad[p, side, pl.ds(0, N)] + came_diag[p]

    send_pieces(2)
    core_copy.wait()
    for t in range(2):
        acc[pl.ds(t * N, N), :] = pgrad[core, t] + core_in[t]
    xy_copies = [
        send(acc.at[part(*xy_at[d])], xy_in.at[d], xy_send.at[0, d], xy_recv.at[0, d], xy_mates[d])
        for d in range(15)]
    send_pieces(2)
    add_edge()
    for c in xy_copies:
        c.wait()
    total = acc[part(y, x), :]
    for d in range(15):
        total = total + xy_in[d]
    shared[z] = total
    z_copies = [
        send(shared.at[z], shared.at[z], z_send.at[d], z_recv.at[d], z_mates[d]) for d in range(7)]
    start_below()
    send_pieces(4)
    for c in z_copies:
        c.wait()
    total = shared[0]
    for d in range(1, 8):
        total = total + shared[d]
    out_full[part(y, x), :] = total * (1.0 / (NTX * 2 * SLOTS))
    xy_copies = [
        send(out_full.at[part(y, x)], out_full.at[part(y, x)], xy_send.at[1, d], xy_recv.at[1, d], xy_mates[d])
        for d in range(15)]
    for c in xy_copies:
        c.wait()
    core_copy = send(out_full, out_other, core_send.at[1], core_recv.at[1], core_mate)
    for c in pieces:
        c.wait()

    @pl.when(tx < NTX - 1)
    def _():
        diag.wait_send()
        below.wait_send()

    @pl.when(tx > 0)
    def _():
        below.wait_recv()

    core_copy.wait()


def finish_kernel(grad, came_ty, came_up, full, other, out_re, out_im, pout_re, pout_im):
    core, ty = lax.rem(lax.axis_index("tx"), 2), lax.axis_index("ty")
    for p, out in enumerate((out_re, out_im)):
        for t in range(2):
            lanes = pl.ds(t * H, H)
            mine = ty == 1 - t
            ty_rows = [jnp.where(mine, came_ty[p, pl.ds(h * N, N)], 0.0) for h in range(2)]
            out[pl.ds(0, N), lanes] = grad[p, ty + t, pl.ds(0, N)] + came_up[p, t] + ty_rows[0]
            out[pl.ds(N, N), lanes] = grad[p, ty + t, pl.ds(N, N)] + ty_rows[1]
    for t in range(2):
        rows, lanes = pl.ds(t * N, N), pl.ds(t * H, H)
        a, b = full[rows, :], other[rows, :]
        pout_re[:, lanes] = jnp.where(core == 0, a, b)
        pout_im[:, lanes] = jnp.where(core == 0, b, a)


def gather_out(offsets, counts, reg, probe_re, probe_im, tables, amp, grad, pgrad):
    vmem = pl.BlockSpec(memory_space=pltpu.VMEM)
    dma = pltpu.SemaphoreType.DMA
    tile = jax.ShapeDtypeStruct((TR, N), F32)
    patch = jax.ShapeDtypeStruct((N, N), F32)
    smem = pl.BlockSpec(memory_space=pltpu.SMEM)
    grad, *came = pl.pallas_call(
        out_kernel,
        out_shape=(
            pltpu.VMEM((2, 3, ROWS, H), F32),
            jax.ShapeDtypeStruct((2, TR, H), F32),
            jax.ShapeDtypeStruct((2, 2, N, H), F32),
            jax.ShapeDtypeStruct((2 * N, H), F32),
            jax.ShapeDtypeStruct((2 * N, H), F32),
        ),
        in_specs=[smem, smem] + [vmem] * 7,
        out_specs=(vmem,) * 5,
        scratch_shapes=[
            pltpu.VMEM((2, 2, N, H), F32),
            pltpu.VMEM((LAST, 2, 3, N + 2 * CH, H), F32),
            pltpu.VMEM((2, 2, 2, N, H), F32),
            pltpu.VMEM((2, 2, 2, N, N), BF16),
            pltpu.VMEM((2, 2, N, N), F32),
            pltpu.VMEM((2, N, H), F32),
            pltpu.VMEM((2, N, H), F32),
            pltpu.VMEM((2, N, H), F32),
            pltpu.VMEM((2 * N, H), F32),
            pltpu.VMEM((15, 32, H), F32),
            pltpu.VMEM((8, 32, H), F32),
            dma((8,)), dma((8,)), dma(()), dma(()), dma(()), dma(()),
            dma((2,)), dma((2,)), dma((2, 15)), dma((2, 15)), dma((7,)), dma((7,)),
        ],
        compiler_params=pltpu.CompilerParams(
            collective_id=1, has_side_effects=True, vmem_limit_bytes=20 << 20),
        name="gather_out",
    )(offsets, counts, reg, probe_re, probe_im, tables, amp, grad, pgrad)
    return pl.pallas_call(
        finish_kernel,
        out_shape=(tile, tile, patch, patch),
        in_specs=[vmem] * 5,
        out_specs=(vmem,) * 4,
        compiler_params=pltpu.CompilerParams(vmem_limit_bytes=20 << 20),
        name="finish",
    )(grad, *came)


def per_device(obj_re, obj_im, probe_re, probe_im, amplitude, offsets, counts):
    tables = jnp.asarray(half_dft_tables())
    reg, amp = halo(obj_re, obj_im, amplitude)
    shared = (jnp.swapaxes(offsets, 2, 3), counts, reg, probe_re, probe_im, tables, amp)
    grad, pgrad = positions(*shared)
    return gather_out(*shared, grad, pgrad)


def solution(mesh):
    return jax.shard_map(
        per_device,
        mesh=mesh,
        in_specs=(
            P("tx", "ty"),
            P("tx", "ty"),
            P(),
            P(),
            P("tx", "ty", None, None, None),
            P("tx", None, None, None),
            P("tx", None),
        ),
        out_specs=(P("tx", "ty"), P("tx", "ty"), P(), P()),
        check_vma=False,
    )
```

```python
import math

import jax
import jax.numpy as jnp
import ml_dtypes
import numpy as np
from jax import lax
from jax.experimental import pallas as pl
from jax.experimental.pallas import tpu as pltpu
from jax.sharding import PartitionSpec as P

N = 256
H = 128
TR = 512
SLOTS = 12
NTX = 128
ROWS = TR + N
MESH = pl.DeviceIdType.MESH
CH = 32
LAST = 8
PIECE = TR // 8
EDGE = NTX // 2
DETOUR = ((1, 0, 0), (2, 0, 1), (3, 1, 0), (3, 1, 1))
F32 = jnp.float32
BF16 = jnp.bfloat16


def half_dft_tables():
    n = np.arange(H, dtype=np.float64)[:, None]
    k = np.arange(H, dtype=np.float64)[None, :]
    tables = []
    for odd in (0, 1):
        angle = -2.0 * math.pi * (n * (2 * k + odd)) / N
        re, im = np.cos(angle) / 16.0, np.sin(angle) / 16.0
        tables.append(np.block([[re, im], [-im, re]]))
    both = np.stack([tables[0], tables[1], tables[0].T, tables[1].T])
    high = both.astype(ml_dtypes.bfloat16)
    low = (both - high.astype(np.float64)).astype(ml_dtypes.bfloat16)
    return np.stack([high, low])


def split(x):
    high = x.astype(BF16)
    return high, (x - high.astype(F32)).astype(BF16)


def dot(a, b):
    return jnp.dot(a, b, preferred_element_type=F32)


def halo_kernel(
    obj_re, obj_im, amp, reg, amp_out, raw, perm,
    ty_send, ty_recv, up_send, up_recv, diag_send, diag_recv, own_sem, raw_sem,
    relay, detour_send, detour_recv, relay_send,
):
    tx, ty = lax.axis_index("tx"), lax.axis_index("ty")
    up, down = lax.rem(tx + NTX - 1, NTX), lax.rem(tx + 1, NTX)
    partner = (tx, 1 - ty)
    barrier = pltpu.get_barrier_semaphore()
    for device in (partner, (up, ty), (down, ty)):
        pl.semaphore_signal(barrier, inc=1, device_id=device, device_id_type=MESH)
    is_relay = (tx > EDGE) & (tx <= EDGE + 6) & (lax.rem(tx, 2) == 0)

    @pl.when((tx == EDGE) | (tx == EDGE - 1))
    def _():
        for k in range(1, 4):
            pl.semaphore_signal(barrier, inc=1, device_id=(EDGE + 2 * k, ty), device_id_type=MESH)

    @pl.when(is_relay)
    def _():
        for device in (EDGE, EDGE - 1):
            pl.semaphore_signal(barrier, inc=1, device_id=(device, ty), device_id_type=MESH)

    raw_copies = []
    for t in range(2):
        c = pltpu.make_async_copy(amp.at[0, 0, :, :, pl.ds(t * H, H)], raw.at[t], raw_sem.at[t])
        c.start()
        raw_copies.append(c)
    own = []
    for p, obj in enumerate((obj_re, obj_im)):
        for t in range(2):
            c = pltpu.make_async_copy(
                obj.at[:, pl.ds(t * H, H)], reg.at[p, ty + t, pl.ds(0, TR)], own_sem.at[p, t])
            c.start()
            own.append(c)
    i, j = (lax.broadcasted_iota(jnp.int32, (N, N), d) for d in range(2))
    perm[...] = jnp.where(i == jnp.where(j < H, 2 * j, 2 * (j - H) + 1), 1.0, 0.0).astype(BF16)
    at_edge = (tx == EDGE) | (tx == EDGE - 1)

    @pl.when(at_edge)
    def _():
        pl.semaphore_wait(barrier, 6)

    @pl.when(is_relay)
    def _():
        pl.semaphore_wait(barrier, 5)

    @pl.when(jnp.logical_not(at_edge | is_relay))
    def _():
        pl.semaphore_wait(barrier, 3)


    edge = pl.multiple_of((1 - ty) * H, H)
    across = [[], []]
    for half in range(2):
        for p, obj in enumerate((obj_re, obj_im)):
            rows = pl.ds(half * N, N)
            c = pltpu.make_async_remote_copy(
                src_ref=obj.at[rows, pl.ds(edge, H)], dst_ref=reg.at[p, 2 * ty, rows],
                send_sem=ty_send.at[half, p], recv_sem=ty_recv.at[half, p],
                device_id=partner, device_id_type=MESH)
            c.start()
            across[half].append(c)
    objs = (obj_re, obj_im)
    blocks = [(p, t) for p in range(2) for t in range(2)]

    def below(p, t):
        return pltpu.make_async_remote_copy(
            src_ref=objs[p].at[pl.ds(0, N), pl.ds(t * H, H)], dst_ref=reg.at[p, ty + t, pl.ds(TR, N)],
            send_sem=up_send.at[p, t], recv_sem=up_recv.at[p, t],
            device_id=(up, ty), device_id_type=MESH)

    def detour(n):
        k, p, t = DETOUR[n]
        return pltpu.make_async_remote_copy(
            src_ref=objs[p].at[pl.ds(0, N), pl.ds(t * H, H)], dst_ref=relay.at[max(n - 2, 0)],
            send_sem=detour_send.at[n], recv_sem=detour_recv.at[max(n - 2, 0)],
            device_id=(EDGE + 2 * k, ty), device_id_type=MESH)

    def onward(n):
        _, p, t = DETOUR[n]
        return pltpu.make_async_remote_copy(
            src_ref=relay.at[max(n - 2, 0)], dst_ref=reg.at[p, ty + t, pl.ds(TR, N)],
            send_sem=relay_send.at[max(n - 2, 0)], recv_sem=up_recv.at[p, t],
            device_id=(EDGE - 1, ty), device_id_type=MESH)

    def diag(p):
        side = 2 - 2 * ty
        return pltpu.make_async_remote_copy(
            src_ref=reg.at[p, side, pl.ds(0, N)], dst_ref=reg.at[p, side, pl.ds(TR, N)],
            send_sem=diag_send.at[p], recv_sem=diag_recv.at[p],
            device_id=(up, ty), device_id_type=MESH)

    sends_up = (tx > 0) & (tx != EDGE)

    @pl.when(sends_up)
    def _():
        for p, t in blocks:
            below(p, t).start()

    @pl.when(tx == EDGE)
    def _():
        for n in range(4):
            detour(n).start()

    for n in range(4):

        @pl.when(tx == EDGE + 2 * DETOUR[n][0])
        def _():
            detour(n).wait_recv()
            onward(n).start()

    for c in raw_copies:
        c.wait()

    def sort_slot(i, carry):
        for h in range(2):
            rows = [raw[t, i, pl.ds(h, H, stride=2), :] for t in range(2)]
            high, low = split(jnp.concatenate(rows, axis=1))
            amp_out[i, pl.ds(h * H, H), :] = dot(high, perm[...]) + dot(low, perm[...])
        return carry

    lax.fori_loop(0, SLOTS // 2, sort_slot, 0)
    for p in range(2):
        across[0][p].wait()

        @pl.when(tx > 0)
        def _():
            diag(p).start()

    lax.fori_loop(SLOTS // 2, SLOTS, sort_slot, 0)

    for c in own + across[1]:
        c.wait()

    @pl.when(sends_up)
    def _():
        for p, t in blocks:
            below(p, t).wait_send()

    @pl.when(tx == EDGE)
    def _():
        for n in range(4):
            detour(n).wait_send()

    for n in range(4):

        @pl.when(tx == EDGE + 2 * DETOUR[n][0])
        def _():
            onward(n).wait_send()

    @pl.when(tx > 0)
    def _():
        for p in range(2):
            diag(p).wait_send()

    @pl.when(tx < NTX - 1)
    def _():
        for p, t in blocks:
            below(p, t).wait_recv()
        for p in range(2):
            diag(p).wait_recv()


def halo(obj_re, obj_im, amp):
    hbm, vmem = (pl.BlockSpec(memory_space=m) for m in (pltpu.HBM, pltpu.VMEM))
    dma = pltpu.SemaphoreType.DMA
    return pl.pallas_call(
        halo_kernel,
        out_shape=(
            pltpu.VMEM((2, 3, ROWS, H), F32),
            pltpu.VMEM((SLOTS, N, N), F32),
        ),
        in_specs=[hbm, hbm, hbm],
        out_specs=(vmem, vmem),
        scratch_shapes=[
            pltpu.VMEM((2, SLOTS, N, H), F32),
            pltpu.VMEM((N, N), BF16),
            dma((2, 2)), dma((2, 2)), dma((2, 2)), dma((2, 2)), dma((2,)), dma((2,)),
            dma((2, 2)), dma((2,)),
            pltpu.VMEM((2, N, H), F32), dma((4,)), dma((2,)), dma((2,)),
        ],
        compiler_params=pltpu.CompilerParams(
            collective_id=0, has_side_effects=True, vmem_limit_bytes=20 << 20),
        name="halo",
    )(*(pltpu.with_memory_space_constraint(x, pltpu.HBM) for x in (obj_re, obj_im, amp)))


def pair_of_positions(reg, probe_re, probe_im, tables, amp, win, sp, mid):
    lane = lax.broadcasted_iota(jnp.int32, (CH, H), 1)

    def put(s, q, rows, lanes, value):
        high, low = split(value)
        sp[s, 0, q, rows, lanes] = high
        sp[s, 1, q, rows, lanes] = low

    def right(s, q, which):
        high, low = sp[s, 0, q], sp[s, 1, q]
        mid[s, q] = dot(jnp.concatenate([high, low, high], axis=1),
                        jnp.concatenate([tables[0, which], tables[0, which], tables[1, which]], axis=0))

    def left(s, q, which):
        high, low = sp[s, 0, q], sp[s, 1, q]
        mid[s, q] = dot(jnp.concatenate([tables[0, which], tables[1, which], tables[0, which]], axis=1),
                        jnp.concatenate([high, high, low], axis=0))

    def lanes(t):
        return pl.ds(t * H, H)

    def enter(s, place):
        row_at, col_at = place
        back = lax.rem(H - col_at, H)
        from_next = lane >= H - col_at
        for j in range(N // CH):
            rows = pl.ds(j * CH, CH)
            ex = [[None, None], [None, None]]
            w = [[None, None], [None, None]]
            for p in range(2):
                turned = [pltpu.roll(reg[p, t, pl.ds(row_at + j * CH, CH), :], back, 1) for t in range(3)]
                for t in range(2):
                    w[p][t] = jnp.where(from_next, turned[t + 1], turned[t])
                    win[s, p, t, rows, :] = w[p][t]
            for t in range(2):
                pr, pi = probe_re[rows, lanes(t)], probe_im[rows, lanes(t)]
                ex[0][t] = pr * w[0][t] - pi * w[1][t]
                ex[1][t] = pr * w[1][t] + pi * w[0][t]
            for p in range(2):
                put(s, 0, rows, lanes(p), ex[p][0] + ex[p][1])
                put(s, 1, rows, lanes(p), ex[p][0] - ex[p][1])

    def fold_rows(s):
        for j in range(H // CH):
            for q in range(2):
                for p in range(2):
                    top = mid[s, q, pl.ds(j * CH, CH), lanes(p)]
                    low = mid[s, q, pl.ds(H + j * CH, CH), lanes(p)]
                    rows = pl.ds(p * H + j * CH, CH)
                    put(s, 0, rows, lanes(q), top + low)
                    put(s, 1, rows, lanes(q), top - low)

    def compare(s, i, used):
        for j in range(H // CH):
            for h in range(2):
                rows_re, rows_im = pl.ds(j * CH, CH), pl.ds(H + j * CH, CH)
                re, im = mid[s, h, rows_re, :], mid[s, h, rows_im, :]
                measured = amp[i, pl.ds(h * H + j * CH, CH), :]
                keep = 1.0 - measured * lax.rsqrt(jnp.maximum(re * re + im * im, 1.0))
                keep = jnp.where(used, keep, 0.0)
                put(s, h, rows_re, slice(None), re * keep)
                put(s, h, rows_im, slice(None), im * keep)

    def unfold_rows(s):
        for j in range(H // CH):
            for p in range(2):
                for q in range(2):
                    a = mid[s, 0, pl.ds(p * H + j * CH, CH), lanes(q)]
                    b = mid[s, 1, pl.ds(p * H + j * CH, CH), lanes(q)]
                    put(s, q, pl.ds(j * CH, CH), lanes(p), a + b)
                    put(s, q, pl.ds(H + j * CH, CH), lanes(p), a - b)

    def leave(s, place, add_rows, add_probe):
        row_at, col_at = place
        ahead = lax.rem(col_at, H)
        to_next = lane < col_at
        for j in range(N // CH):
            rows = pl.ds(j * CH, CH)
            g = [[None, None], [None, None]]
            for t in range(2):
                chi = []
                for p in range(2):
                    a, b = mid[s, 0, rows, lanes(p)], mid[s, 1, rows, lanes(p)]
                    chi.append(a + b if t == 0 else a - b)
                pr, pi = probe_re[rows, lanes(t)], probe_im[rows, lanes(t)]
                wr, wi = win[s, 0, t, rows, :], win[s, 1, t, rows, :]
                g[0][t] = pltpu.roll(pr * chi[0] + pi * chi[1], ahead, 1)
                g[1][t] = pltpu.roll(pr * chi[1] - pi * chi[0], ahead, 1)
                add_probe(t, rows, wr * chi[0] + wi * chi[1], wr * chi[1] - wi * chi[0])
            for p in range(2):
                add_rows(s, row_at, j, p, (
                    jnp.where(to_next, 0.0, g[p][0]),
                    jnp.where(to_next, g[p][0], g[p][1]),
                    jnp.where(to_next, g[p][1], 0.0)))

    def pair(places, ids, used, add_rows, add_probe):
        stages = [
            lambda s: enter(s, places[s]),
            lambda s: [right(s, q, q) for q in range(2)],
            lambda s: fold_rows(s),
            lambda s: [left(s, h, 2 + h) for h in range(2)],
            lambda s: compare(s, ids[s], used[s]),
            lambda s: [left(s, h, h) for h in range(2)],
            lambda s: unfold_rows(s),
            lambda s: [right(s, q, 2 + q) for q in range(2)],
            lambda s: leave(s, places[s], add_rows, add_probe),
        ]
        stages[0](0)
        for n in range(1, len(stages)):
            stages[n](0)
            stages[n - 1](1)
        stages[-1](1)

    return pair


def place_of(offsets, tx, ty, i):
    row_at, col_at = offsets[0, ty, 0, i] - tx * TR, offsets[0, ty, 1, i] - ty * H
    return jnp.clip(row_at, 0, TR - 1), jnp.clip(col_at, 0, H)


def positions_kernel(
    offsets, counts, reg, probe_re, probe_im, tables, amp, grad, pgrad, win, sp, mid,
):
    tx, ty = lax.axis_index("tx"), lax.axis_index("ty")
    here = jnp.maximum(counts[0, ty] - LAST, 0)
    grad[...] = jnp.zeros_like(grad)
    pgrad[...] = jnp.zeros_like(pgrad)
    pair = pair_of_positions(reg, probe_re, probe_im, tables, amp, win, sp, mid)

    def add_rows(s, row_at, j, p, tiles):
        at = pl.ds(row_at + j * CH, CH)
        for t in range(3):
            grad[p, t, at, :] += tiles[t]

    def add_probe(t, rows, re, im):
        pgrad[0, t, rows, :] += re
        pgrad[1, t, rows, :] += im

    def step(k, carry):
        ids = [2 * k, jnp.minimum(2 * k + 1, here - 1)]
        pair([place_of(offsets, tx, ty, i) for i in ids], ids, [True, 2 * k + 1 < here], add_rows, add_probe)
        return carry

    lax.fori_loop(0, (here + 1) // 2, step, 0)


def positions(offsets, counts, reg, probe_re, probe_im, tables, amp):
    smem = pl.BlockSpec(memory_space=pltpu.SMEM)
    vmem = pl.BlockSpec(memory_space=pltpu.VMEM)
    return pl.pallas_call(
        positions_kernel,
        out_shape=(
            pltpu.VMEM((2, 3, ROWS, H), F32),
            pltpu.VMEM((2, 2, N, H), F32),
        ),
        in_specs=[smem, smem, vmem, vmem, vmem, vmem, vmem],
        out_specs=(vmem, vmem),
        scratch_shapes=[
            pltpu.VMEM((2, 2, 2, N, H), F32),
            pltpu.VMEM((2, 2, 2, N, N), BF16),
            pltpu.VMEM((2, 2, N, N), F32),
        ],
        compiler_params=pltpu.CompilerParams(vmem_limit_bytes=20 << 20),
        name="positions",
    )(offsets, counts, reg, probe_re, probe_im, tables, amp)


def out_kernel(
    offsets, counts, reg, probe_re, probe_im, tables, amp, grad_in, pgrad_in, grad, out_ty, out_up, out_full, out_other,
    pgrad, placed, win, sp, mid, came_diag, edge, core_in, acc, xy_in, shared,
    ty_send, ty_recv, up_send, up_recv, diag_send, diag_recv,
    core_send, core_recv, xy_send, xy_recv, z_send, z_recv,
):
    tx, ty = lax.axis_index("tx"), lax.axis_index("ty")
    up, down = lax.rem(tx + NTX - 1, NTX), lax.rem(tx + 1, NTX)
    partner = (tx, 1 - ty)
    core, y, z, x_lo = lax.rem(tx, 2), lax.rem(tx // 2, 4), lax.rem(tx // 8, 8), tx // 64
    x = ty * 2 + x_lo

    def at(core_, y_, z_, x_):
        return (((lax.rem(x_, 2) * 8 + z_) * 4 + y_) * 2 + core_, x_ // 2)

    core_mate = at(1 - core, y, z, x)
    steps = [(i, j) for i in range(4) for j in range(4) if i or j]
    steps.sort(key=lambda s: -(min(s[0], 4 - s[0]) + min(s[1], 4 - s[1])))
    xy_at = [(lax.rem(y + i, 4), lax.rem(x + j, 4)) for i, j in steps]
    xy_mates = [at(core, i, z, j) for i, j in xy_at]
    z_mates = [at(core, y, lax.rem(z + d, 8), x) for d in (4, 3, 5, 2, 6, 1, 7)]
    greeted = z_mates + xy_mates + [partner, (up, ty), (down, ty), core_mate]
    barrier = pltpu.get_barrier_semaphore()
    for device in greeted:
        pl.semaphore_signal(barrier, inc=1, device_id=device, device_id_type=MESH)

    live = counts[0, ty]
    for margin in (0, CH + N):
        placed[:, :, :, pl.ds(margin, CH), :] = jnp.zeros((LAST, 2, 3, CH, H), F32)
    pgrad[...] = pgrad_in[...]
    pair = pair_of_positions(reg, probe_re, probe_im, tables, amp, win, sp, mid)

    def add_probe(t, rows, re, im):
        pgrad[0, t, rows, :] += re
        pgrad[1, t, rows, :] += im

    def id_of(n):
        return jnp.maximum(live - LAST + n, 0)

    def step(k, carry):
        ids = [id_of(2 * k + s) for s in range(2)]

        def add_rows(s, row_at, j, p, tiles):
            for t in range(3):
                placed[2 * k + s, p, t, pl.ds(CH + j * CH, CH), :] = tiles[t]

        pair([place_of(offsets, tx, ty, i) for i in ids], ids,
             [live - LAST + 2 * k + s >= 0 for s in range(2)], add_rows, add_probe)
        return carry

    lax.fori_loop(0, LAST // 2, step, 0)
    pl.semaphore_wait(barrier, len(greeted))

    def make(src, dst, send_sem, recv_sem, device):
        return pltpu.make_async_remote_copy(
            src_ref=src, dst_ref=dst, send_sem=send_sem, recv_sem=recv_sem,
            device_id=device, device_id_type=MESH)

    def send(*args):
        c = make(*args)
        c.start()
        return c

    def part(i, j):
        return pl.ds(pl.multiple_of((i * 4 + j) * 32, 32), 32)

    side = 2 - 2 * ty
    core_copy = send(pgrad.at[1 - core], core_in, core_send.at[0], core_recv.at[0], core_mate)

    firsts = [place_of(offsets, tx, ty, id_of(n))[0] for n in range(LAST)]

    def place_rows(j, carry):
        rows = pl.ds(pl.multiple_of(j * CH, CH), CH)
        for p in range(2):
            for t in range(3):
                total = grad_in[p, t, rows, :]
                for n in range(LAST):
                    at = jnp.clip(j * CH - firsts[n] + CH, 0, CH + N)
                    total = total + placed[n, p, t, pl.ds(at, CH), :]
                grad[p, t, rows, :] = total
        return carry

    lax.fori_loop(0, ROWS // CH, place_rows, 0)
    diag = make(grad.at[:, side, pl.ds(TR, N)], came_diag, diag_send, diag_recv, (down, ty))
    below = make(grad.at[:, pl.ds(ty, 2), pl.ds(TR, N)], out_up, up_send, up_recv, (down, ty))

    @pl.when(tx < NTX - 1)
    def _():
        diag.start()

    @pl.when(tx == 0)
    def _():
        came_diag[...] = jnp.zeros_like(came_diag)
        out_up[...] = jnp.zeros_like(out_up)

    pieces = []

    def send_pieces(count):
        for _ in range(count):
            n = (len(pieces) + 4) % 8
            rows = pl.ds(n * PIECE, PIECE)
            src = grad.at[:, side, rows] if n >= 4 else edge.at[:, rows]
            pieces.append(send(src, out_ty.at[:, rows], ty_send.at[n], ty_recv.at[n], partner))

    def start_below():
        @pl.when(tx < NTX - 1)
        def _():
            below.start()

    def add_edge():
        @pl.when(tx > 0)
        def _():
            diag.wait_recv()

        for p in range(2):
            edge[p] = grad[p, side, pl.ds(0, N)] + came_diag[p]

    send_pieces(2)
    core_copy.wait()
    for t in range(2):
        acc[pl.ds(t * N, N), :] = pgrad[core, t] + core_in[t]
    xy_copies = [
        send(acc.at[part(*xy_at[d])], xy_in.at[d], xy_send.at[0, d], xy_recv.at[0, d], xy_mates[d])
        for d in range(15)]
    send_pieces(2)
    add_edge()
    for c in xy_copies:
        c.wait()
    total = acc[part(y, x), :]
    for d in range(15):
        total = total + xy_in[d]
    shared[z] = total
    z_copies = [
        send(shared.at[z], shared.at[z], z_send.at[d], z_recv.at[d], z_mates[d]) for d in range(7)]
    start_below()
    send_pieces(4)
    for c in z_copies:
        c.wait()
    total = shared[0]
    for d in range(1, 8):
        total = total + shared[d]
    out_full[part(y, x), :] = total * (1.0 / (NTX * 2 * SLOTS))
    xy_copies = [
        send(out_full.at[part(y, x)], out_full.at[part(y, x)], xy_send.at[1, d], xy_recv.at[1, d], xy_mates[d])
        for d in range(15)]
    for c in xy_copies:
        c.wait()
    core_copy = send(out_full, out_other, core_send.at[1], core_recv.at[1], core_mate)
    for c in pieces:
        c.wait()

    @pl.when(tx < NTX - 1)
    def _():
        diag.wait_send()
        below.wait_send()

    @pl.when(tx > 0)
    def _():
        below.wait_recv()

    core_copy.wait()


def finish_kernel(grad, came_ty, came_up, full, other, out_re, out_im, pout_re, pout_im):
    core, ty = lax.rem(lax.axis_index("tx"), 2), lax.axis_index("ty")
    for p, out in enumerate((out_re, out_im)):
        for t in range(2):
            lanes = pl.ds(t * H, H)
            mine = ty == 1 - t
            ty_rows = [jnp.where(mine, came_ty[p, pl.ds(h * N, N)], 0.0) for h in range(2)]
            out[pl.ds(0, N), lanes] = grad[p, ty + t, pl.ds(0, N)] + came_up[p, t] + ty_rows[0]
            out[pl.ds(N, N), lanes] = grad[p, ty + t, pl.ds(N, N)] + ty_rows[1]
    for t in range(2):
        rows, lanes = pl.ds(t * N, N), pl.ds(t * H, H)
        a, b = full[rows, :], other[rows, :]
        pout_re[:, lanes] = jnp.where(core == 0, a, b)
        pout_im[:, lanes] = jnp.where(core == 0, b, a)


def gather_out(offsets, counts, reg, probe_re, probe_im, tables, amp, grad, pgrad):
    vmem = pl.BlockSpec(memory_space=pltpu.VMEM)
    dma = pltpu.SemaphoreType.DMA
    tile = jax.ShapeDtypeStruct((TR, N), F32)
    patch = jax.ShapeDtypeStruct((N, N), F32)
    smem = pl.BlockSpec(memory_space=pltpu.SMEM)
    grad, *came = pl.pallas_call(
        out_kernel,
        out_shape=(
            pltpu.VMEM((2, 3, ROWS, H), F32),
            jax.ShapeDtypeStruct((2, TR, H), F32),
            jax.ShapeDtypeStruct((2, 2, N, H), F32),
            jax.ShapeDtypeStruct((2 * N, H), F32),
            jax.ShapeDtypeStruct((2 * N, H), F32),
        ),
        in_specs=[smem, smem] + [vmem] * 7,
        out_specs=(vmem,) * 5,
        scratch_shapes=[
            pltpu.VMEM((2, 2, N, H), F32),
            pltpu.VMEM((LAST, 2, 3, N + 2 * CH, H), F32),
            pltpu.VMEM((2, 2, 2, N, H), F32),
            pltpu.VMEM((2, 2, 2, N, N), BF16),
            pltpu.VMEM((2, 2, N, N), F32),
            pltpu.VMEM((2, N, H), F32),
            pltpu.VMEM((2, N, H), F32),
            pltpu.VMEM((2, N, H), F32),
            pltpu.VMEM((2 * N, H), F32),
            pltpu.VMEM((15, 32, H), F32),
            pltpu.VMEM((8, 32, H), F32),
            dma((8,)), dma((8,)), dma(()), dma(()), dma(()), dma(()),
            dma((2,)), dma((2,)), dma((2, 15)), dma((2, 15)), dma((7,)), dma((7,)),
        ],
        compiler_params=pltpu.CompilerParams(
            collective_id=1, has_side_effects=True, vmem_limit_bytes=20 << 20),
        name="gather_out",
    )(offsets, counts, reg, probe_re, probe_im, tables, amp, grad, pgrad)
    return pl.pallas_call(
        finish_kernel,
        out_shape=(tile, tile, patch, patch),
        in_specs=[vmem] * 5,
        out_specs=(vmem,) * 4,
        compiler_params=pltpu.CompilerParams(vmem_limit_bytes=20 << 20),
        name="finish",
    )(grad, *came)


def per_device(obj_re, obj_im, probe_re, probe_im, amplitude, offsets, counts):
    tables = jnp.asarray(half_dft_tables())
    reg, amp = halo(obj_re, obj_im, amplitude)
    shared = (jnp.swapaxes(offsets, 2, 3), counts, reg, probe_re, probe_im, tables, amp)
    grad, pgrad = positions(*shared)
    return gather_out(*shared, grad, pgrad)


def solution(mesh):
    return jax.shard_map(
        per_device,
        mesh=mesh,
        in_specs=(
            P("tx", "ty"),
            P("tx", "ty"),
            P(),
            P(),
            P("tx", "ty", None, None, None),
            P("tx", None, None, None),
            P("tx", None),
        ),
        out_specs=(P("tx", "ty"), P("tx", "ty"), P(), P()),
        check_vma=False,
    )
```

```python
import math

import jax
import jax.numpy as jnp
import ml_dtypes
import numpy as np
from jax import lax
from jax.experimental import pallas as pl
from jax.experimental.pallas import tpu as pltpu
from jax.sharding import PartitionSpec as P

N = 256
H = 128
TR = 512
SLOTS = 12
NTX = 128
ROWS = TR + N
MESH = pl.DeviceIdType.MESH
CH = 32
LAST = 6
EDGE = NTX // 2
DETOUR = ((1, 0, 0), (2, 0, 1), (3, 1, 0), (3, 1, 1))
F32 = jnp.float32
BF16 = jnp.bfloat16


def half_dft_tables():
    n = np.arange(H, dtype=np.float64)[:, None]
    k = np.arange(H, dtype=np.float64)[None, :]
    tables = []
    for odd in (0, 1):
        angle = -2.0 * math.pi * (n * (2 * k + odd)) / N
        re, im = np.cos(angle) / 16.0, np.sin(angle) / 16.0
        tables.append(np.block([[re, im], [-im, re]]))
    both = np.stack([tables[0], tables[1], tables[0].T, tables[1].T])
    high = both.astype(ml_dtypes.bfloat16)
    low = (both - high.astype(np.float64)).astype(ml_dtypes.bfloat16)
    return np.stack([high, low])


def split(x):
    high = x.astype(BF16)
    return high, (x - high.astype(F32)).astype(BF16)


def dot(a, b):
    return jnp.dot(a, b, preferred_element_type=F32)


def halo_kernel(
    obj_re, obj_im, amp, reg, amp_out, blank, raw, perm,
    ty_send, ty_recv, up_send, up_recv, diag_send, diag_recv, own_sem, raw_sem,
    relay, detour_send, detour_recv, relay_send,
):
    tx, ty = lax.axis_index("tx"), lax.axis_index("ty")
    up, down = lax.rem(tx + NTX - 1, NTX), lax.rem(tx + 1, NTX)
    partner = (tx, 1 - ty)
    barrier = pltpu.get_barrier_semaphore()
    for device in (partner, (up, ty), (down, ty)):
        pl.semaphore_signal(barrier, inc=1, device_id=device, device_id_type=MESH)
    is_relay = (tx > EDGE) & (tx <= EDGE + 6) & (lax.rem(tx, 2) == 0)

    @pl.when((tx == EDGE) | (tx == EDGE - 1))
    def _():
        for k in range(1, 4):
            pl.semaphore_signal(barrier, inc=1, device_id=(EDGE + 2 * k, ty), device_id_type=MESH)

    @pl.when(is_relay)
    def _():
        for device in (EDGE, EDGE - 1):
            pl.semaphore_signal(barrier, inc=1, device_id=(device, ty), device_id_type=MESH)

    raw_copies = []
    for t in range(2):
        c = pltpu.make_async_copy(amp.at[0, 0, :, :, pl.ds(t * H, H)], raw.at[t], raw_sem.at[t])
        c.start()
        raw_copies.append(c)
    own = []
    for p, obj in enumerate((obj_re, obj_im)):
        for t in range(2):
            c = pltpu.make_async_copy(
                obj.at[:, pl.ds(t * H, H)], reg.at[p, ty + t, pl.ds(0, TR)], own_sem.at[p, t])
            c.start()
            own.append(c)
    i, j = (lax.broadcasted_iota(jnp.int32, (N, N), d) for d in range(2))
    perm[...] = jnp.where(i == jnp.where(j < H, 2 * j, 2 * (j - H) + 1), 1.0, 0.0).astype(BF16)
    at_edge = (tx == EDGE) | (tx == EDGE - 1)

    @pl.when(at_edge)
    def _():
        pl.semaphore_wait(barrier, 6)

    @pl.when(is_relay)
    def _():
        pl.semaphore_wait(barrier, 5)

    @pl.when(jnp.logical_not(at_edge | is_relay))
    def _():
        pl.semaphore_wait(barrier, 3)


    edge = pl.multiple_of((1 - ty) * H, H)
    across = [[], []]
    for half in range(2):
        for p, obj in enumerate((obj_re, obj_im)):
            rows = pl.ds(half * N, N)
            c = pltpu.make_async_remote_copy(
                src_ref=obj.at[rows, pl.ds(edge, H)], dst_ref=reg.at[p, 2 * ty, rows],
                send_sem=ty_send.at[half, p], recv_sem=ty_recv.at[half, p],
                device_id=partner, device_id_type=MESH)
            c.start()
            across[half].append(c)
    objs = (obj_re, obj_im)
    blocks = [(p, t) for p in range(2) for t in range(2)]

    def below(p, t):
        return pltpu.make_async_remote_copy(
            src_ref=objs[p].at[pl.ds(0, N), pl.ds(t * H, H)], dst_ref=reg.at[p, ty + t, pl.ds(TR, N)],
            send_sem=up_send.at[p, t], recv_sem=up_recv.at[p, t],
            device_id=(up, ty), device_id_type=MESH)

    def detour(n):
        k, p, t = DETOUR[n]
        return pltpu.make_async_remote_copy(
            src_ref=objs[p].at[pl.ds(0, N), pl.ds(t * H, H)], dst_ref=relay.at[max(n - 2, 0)],
            send_sem=detour_send.at[n], recv_sem=detour_recv.at[max(n - 2, 0)],
            device_id=(EDGE + 2 * k, ty), device_id_type=MESH)

    def onward(n):
        _, p, t = DETOUR[n]
        return pltpu.make_async_remote_copy(
            src_ref=relay.at[max(n - 2, 0)], dst_ref=reg.at[p, ty + t, pl.ds(TR, N)],
            send_sem=relay_send.at[max(n - 2, 0)], recv_sem=up_recv.at[p, t],
            device_id=(EDGE - 1, ty), device_id_type=MESH)

    def diag(p):
        side = 2 - 2 * ty
        return pltpu.make_async_remote_copy(
            src_ref=reg.at[p, side, pl.ds(0, N)], dst_ref=reg.at[p, side, pl.ds(TR, N)],
            send_sem=diag_send.at[p], recv_sem=diag_recv.at[p],
            device_id=(up, ty), device_id_type=MESH)

    sends_up = (tx > 0) & (tx != EDGE)

    @pl.when(sends_up)
    def _():
        for p, t in blocks:
            below(p, t).start()

    @pl.when(tx == EDGE)
    def _():
        for n in range(4):
            detour(n).start()

    for n in range(4):

        @pl.when(tx == EDGE + 2 * DETOUR[n][0])
        def _():
            detour(n).wait_recv()
            onward(n).start()

    blank[...] = jnp.zeros_like(blank)
    for c in raw_copies:
        c.wait()

    def sort_slot(i, carry):
        for h in range(2):
            rows = [raw[t, i, pl.ds(h, H, stride=2), :] for t in range(2)]
            high, low = split(jnp.concatenate(rows, axis=1))
            amp_out[i, pl.ds(h * H, H), :] = dot(high, perm[...]) + dot(low, perm[...])
        return carry

    lax.fori_loop(0, SLOTS // 2, sort_slot, 0)
    for p in range(2):
        across[0][p].wait()

        @pl.when(tx > 0)
        def _():
            diag(p).start()

    lax.fori_loop(SLOTS // 2, SLOTS, sort_slot, 0)

    for c in own + across[1]:
        c.wait()

    @pl.when(sends_up)
    def _():
        for p, t in blocks:
            below(p, t).wait_send()

    @pl.when(tx == EDGE)
    def _():
        for n in range(4):
            detour(n).wait_send()

    for n in range(4):

        @pl.when(tx == EDGE + 2 * DETOUR[n][0])
        def _():
            onward(n).wait_send()

    @pl.when(tx > 0)
    def _():
        for p in range(2):
            diag(p).wait_send()

    @pl.when(tx < NTX - 1)
    def _():
        for p, t in blocks:
            below(p, t).wait_recv()
        for p in range(2):
            diag(p).wait_recv()


def halo(obj_re, obj_im, amp):
    hbm, vmem = (pl.BlockSpec(memory_space=m) for m in (pltpu.HBM, pltpu.VMEM))
    dma = pltpu.SemaphoreType.DMA
    return pl.pallas_call(
        halo_kernel,
        out_shape=(
            pltpu.VMEM((2, 3, ROWS, H), F32),
            pltpu.VMEM((SLOTS, N, N), F32),
            pltpu.VMEM((2, 3, ROWS, H), F32),
        ),
        in_specs=[hbm, hbm, hbm],
        out_specs=(vmem, vmem, vmem),
        scratch_shapes=[
            pltpu.VMEM((2, SLOTS, N, H), F32),
            pltpu.VMEM((N, N), BF16),
            dma((2, 2)), dma((2, 2)), dma((2, 2)), dma((2, 2)), dma((2,)), dma((2,)),
            dma((2, 2)), dma((2,)),
            pltpu.VMEM((2, N, H), F32), dma((4,)), dma((2,)), dma((2,)),
        ],
        compiler_params=pltpu.CompilerParams(
            collective_id=0, has_side_effects=True, vmem_limit_bytes=20 << 20),
        name="halo",
    )(*(pltpu.with_memory_space_constraint(x, pltpu.HBM) for x in (obj_re, obj_im, amp)))


def pair_of_positions(reg, probe_re, probe_im, tables, amp, win, sp, mid):
    lane = lax.broadcasted_iota(jnp.int32, (CH, H), 1)

    def put(s, q, rows, lanes, value):
        high, low = split(value)
        sp[s, 0, q, rows, lanes] = high
        sp[s, 1, q, rows, lanes] = low

    def right(s, q, which):
        high, low = sp[s, 0, q], sp[s, 1, q]
        mid[s, q] = dot(jnp.concatenate([high, low, high], axis=1),
                        jnp.concatenate([tables[0, which], tables[0, which], tables[1, which]], axis=0))

    def left(s, q, which):
        high, low = sp[s, 0, q], sp[s, 1, q]
        mid[s, q] = dot(jnp.concatenate([tables[0, which], tables[1, which], tables[0, which]], axis=1),
                        jnp.concatenate([high, high, low], axis=0))

    def lanes(t):
        return pl.ds(t * H, H)

    def enter(s, place):
        row_at, col_at = place
        back = lax.rem(H - col_at, H)
        from_next = lane >= H - col_at
        for j in range(N // CH):
            rows = pl.ds(j * CH, CH)
            ex = [[None, None], [None, None]]
            w = [[None, None], [None, None]]
            for p in range(2):
                turned = [pltpu.roll(reg[p, t, pl.ds(row_at + j * CH, CH), :], back, 1) for t in range(3)]
                for t in range(2):
                    w[p][t] = jnp.where(from_next, turned[t + 1], turned[t])
                    win[s, p, t, rows, :] = w[p][t]
            for t in range(2):
                pr, pi = probe_re[rows, lanes(t)], probe_im[rows, lanes(t)]
                ex[0][t] = pr * w[0][t] - pi * w[1][t]
                ex[1][t] = pr * w[1][t] + pi * w[0][t]
            for p in range(2):
                put(s, 0, rows, lanes(p), ex[p][0] + ex[p][1])
                put(s, 1, rows, lanes(p), ex[p][0] - ex[p][1])

    def fold_rows(s):
        for j in range(H // CH):
            for q in range(2):
                for p in range(2):
                    top = mid[s, q, pl.ds(j * CH, CH), lanes(p)]
                    low = mid[s, q, pl.ds(H + j * CH, CH), lanes(p)]
                    rows = pl.ds(p * H + j * CH, CH)
                    put(s, 0, rows, lanes(q), top + low)
                    put(s, 1, rows, lanes(q), top - low)

    def compare(s, i, used):
        for j in range(H // CH):
            for h in range(2):
                rows_re, rows_im = pl.ds(j * CH, CH), pl.ds(H + j * CH, CH)
                re, im = mid[s, h, rows_re, :], mid[s, h, rows_im, :]
                measured = amp[i, pl.ds(h * H + j * CH, CH), :]
                keep = 1.0 - measured * lax.rsqrt(jnp.maximum(re * re + im * im, 1.0))
                keep = jnp.where(used, keep, 0.0)
                put(s, h, rows_re, slice(None), re * keep)
                put(s, h, rows_im, slice(None), im * keep)

    def unfold_rows(s):
        for j in range(H // CH):
            for p in range(2):
                for q in range(2):
                    a = mid[s, 0, pl.ds(p * H + j * CH, CH), lanes(q)]
                    b = mid[s, 1, pl.ds(p * H + j * CH, CH), lanes(q)]
                    put(s, q, pl.ds(j * CH, CH), lanes(p), a + b)
                    put(s, q, pl.ds(H + j * CH, CH), lanes(p), a - b)

    def leave(s, place, add_rows, add_probe):
        row_at, col_at = place
        ahead = lax.rem(col_at, H)
        to_next = lane < col_at
        for j in range(N // CH):
            rows = pl.ds(j * CH, CH)
            g = [[None, None], [None, None]]
            for t in range(2):
                chi = []
                for p in range(2):
                    a, b = mid[s, 0, rows, lanes(p)], mid[s, 1, rows, lanes(p)]
                    chi.append(a + b if t == 0 else a - b)
                pr, pi = probe_re[rows, lanes(t)], probe_im[rows, lanes(t)]
                wr, wi = win[s, 0, t, rows, :], win[s, 1, t, rows, :]
                g[0][t] = pltpu.roll(pr * chi[0] + pi * chi[1], ahead, 1)
                g[1][t] = pltpu.roll(pr * chi[1] - pi * chi[0], ahead, 1)
                add_probe(t, rows, wr * chi[0] + wi * chi[1], wr * chi[1] - wi * chi[0])
            for p in range(2):
                add_rows(s, row_at, j, p, (
                    jnp.where(to_next, 0.0, g[p][0]),
                    jnp.where(to_next, g[p][0], g[p][1]),
                    jnp.where(to_next, g[p][1], 0.0)))

    def pair(places, ids, used, add_rows, add_probe):
        stages = [
            lambda s: enter(s, places[s]),
            lambda s: [right(s, q, q) for q in range(2)],
            lambda s: fold_rows(s),
            lambda s: [left(s, h, 2 + h) for h in range(2)],
            lambda s: compare(s, ids[s], used[s]),
            lambda s: [left(s, h, h) for h in range(2)],
            lambda s: unfold_rows(s),
            lambda s: [right(s, q, 2 + q) for q in range(2)],
            lambda s: leave(s, places[s], add_rows, add_probe),
        ]
        stages[0](0)
        for n in range(1, len(stages)):
            stages[n](0)
            stages[n - 1](1)
        stages[-1](1)

    return pair


def place_of(offsets, tx, ty, i):
    row_at, col_at = offsets[0, ty, 0, i] - tx * TR, offsets[0, ty, 1, i] - ty * H
    return jnp.clip(row_at, 0, TR - 1), jnp.clip(col_at, 0, H)


def positions_kernel(
    offsets, counts, reg, probe_re, probe_im, tables, amp, blank, grad, pgrad, win, sp, mid,
):
    tx, ty = lax.axis_index("tx"), lax.axis_index("ty")
    here = jnp.maximum(counts[0, ty] - LAST, 0)
    pgrad[...] = jnp.zeros_like(pgrad)
    pair = pair_of_positions(reg, probe_re, probe_im, tables, amp, win, sp, mid)

    def add_rows(s, row_at, j, p, tiles):
        at = pl.ds(row_at + j * CH, CH)
        for t in range(3):
            grad[p, t, at, :] += tiles[t]

    def add_probe(t, rows, re, im):
        pgrad[0, t, rows, :] += re
        pgrad[1, t, rows, :] += im

    def step(k, carry):
        ids = [2 * k, jnp.minimum(2 * k + 1, here - 1)]
        pair([place_of(offsets, tx, ty, i) for i in ids], ids, [True, 2 * k + 1 < here], add_rows, add_probe)
        return carry

    lax.fori_loop(0, (here + 1) // 2, step, 0)


def positions(offsets, counts, reg, probe_re, probe_im, tables, amp, blank):
    smem = pl.BlockSpec(memory_space=pltpu.SMEM)
    vmem = pl.BlockSpec(memory_space=pltpu.VMEM)
    return pl.pallas_call(
        positions_kernel,
        out_shape=(
            pltpu.VMEM((2, 3, ROWS, H), F32),
            pltpu.VMEM((2, 2, N, H), F32),
        ),
        in_specs=[smem, smem] + [vmem] * 6,
        input_output_aliases={7: 0},
        out_specs=(vmem, vmem),
        scratch_shapes=[
            pltpu.VMEM((2, 2, 2, N, H), F32),
            pltpu.VMEM((2, 2, 2, N, N), BF16),
            pltpu.VMEM((2, 2, N, N), F32),
        ],
        compiler_params=pltpu.CompilerParams(vmem_limit_bytes=20 << 20),
        name="positions",
    )(offsets, counts, reg, probe_re, probe_im, tables, amp, blank)


def out_kernel(
    offsets, counts, reg, probe_re, probe_im, tables, amp, grad_in, pgrad_in, grad, out_ty, out_up, out_full, out_other,
    pgrad, placed, win, sp, mid, came_diag, edge, core_in, acc, yz_in, shared,
    ty_send, ty_recv, up_send, up_recv, diag_send, diag_recv,
    core_send, core_recv, yz_send, yz_recv, far_send, far_recv,
):
    tx, ty = lax.axis_index("tx"), lax.axis_index("ty")
    up, down = lax.rem(tx + NTX - 1, NTX), lax.rem(tx + 1, NTX)
    partner = (tx, 1 - ty)
    core, y, z, x_lo = lax.rem(tx, 2), lax.rem(tx // 2, 4), lax.rem(tx // 8, 8), tx // 64
    x = ty * 2 + x_lo

    def at(core_, y_, z_, x_):
        return (((lax.rem(x_, 2) * 8 + z_) * 4 + y_) * 2 + core_, x_ // 2)

    core_mate = at(1 - core, y, z, x)
    z_low, z_high = lax.rem(z, 4), z // 4
    steps = [(i, j) for i in range(4) for j in range(4) if i or j]
    steps.sort(key=lambda s: -(min(s[0], 4 - s[0]) + min(s[1], 4 - s[1])))
    yz_at = [(lax.rem(y + i, 4), lax.rem(z_low + j, 4)) for i, j in steps]
    yz_mates = [at(core, i, z_high * 4 + j, x) for i, j in yz_at]
    hops = [(1, 2), (1, 1), (1, 3), (1, 0), (0, 2), (0, 1), (0, 3)]
    far_mates = [at(core, y, lax.rem(z_high + i, 2) * 4 + z_low, lax.rem(x + j, 4)) for i, j in hops]
    greeted = far_mates + yz_mates + [partner, (up, ty), (down, ty), core_mate]
    barrier = pltpu.get_barrier_semaphore()
    for device in greeted:
        pl.semaphore_signal(barrier, inc=1, device_id=device, device_id_type=MESH)

    live = counts[0, ty]
    for margin in (0, CH + N):
        placed[:, :, :, pl.ds(margin, CH), :] = jnp.zeros((LAST, 2, 3, CH, H), F32)
    pgrad[...] = pgrad_in[...]
    pair = pair_of_positions(reg, probe_re, probe_im, tables, amp, win, sp, mid)

    def add_probe(t, rows, re, im):
        pgrad[0, t, rows, :] += re
        pgrad[1, t, rows, :] += im

    def id_of(n):
        return jnp.maximum(live - LAST + n, 0)

    def step(k, carry):
        ids = [id_of(2 * k + s) for s in range(2)]

        def add_rows(s, row_at, j, p, tiles):
            for t in range(3):
                placed[2 * k + s, p, t, pl.ds(CH + j * CH, CH), :] = tiles[t]

        pair([place_of(offsets, tx, ty, i) for i in ids], ids,
             [live - LAST + 2 * k + s >= 0 for s in range(2)], add_rows, add_probe)
        return carry

    lax.fori_loop(0, LAST // 2, step, 0)
    pl.semaphore_wait(barrier, len(greeted))

    def make(src, dst, send_sem, recv_sem, device):
        return pltpu.make_async_remote_copy(
            src_ref=src, dst_ref=dst, send_sem=send_sem, recv_sem=recv_sem,
            device_id=device, device_id_type=MESH)

    def send(*args):
        c = make(*args)
        c.start()
        return c

    def part(i, j):
        return pl.ds(pl.multiple_of((i * 4 + j) * 32, 32), 32)

    side = 2 - 2 * ty
    core_copy = send(pgrad.at[1 - core], core_in, core_send.at[0], core_recv.at[0], core_mate)

    firsts = [place_of(offsets, tx, ty, id_of(n))[0] for n in range(LAST)]

    def place_rows(j, carry):
        rows = pl.ds(pl.multiple_of(j * CH, CH), CH)
        for p in range(2):
            for t in range(3):
                total = grad_in[p, t, rows, :]
                for n in range(LAST):
                    at = jnp.clip(j * CH - firsts[n] + CH, 0, CH + N)
                    total = total + placed[n, p, t, pl.ds(at, CH), :]
                grad[p, t, rows, :] = total
        return carry

    lax.fori_loop(0, ROWS // CH, place_rows, 0)
    diag = make(grad.at[:, side, pl.ds(TR, N)], came_diag, diag_send, diag_recv, (down, ty))
    below = make(grad.at[:, pl.ds(ty, 2), pl.ds(TR, N)], out_up, up_send, up_recv, (down, ty))

    @pl.when(tx < NTX - 1)
    def _():
        diag.start()

    @pl.when(tx == 0)
    def _():
        came_diag[...] = jnp.zeros_like(came_diag)
        out_up[...] = jnp.zeros_like(out_up)

    far_rows = send(
        grad.at[:, side, pl.ds(N, N)], out_ty.at[:, pl.ds(N, N)], ty_send.at[1], ty_recv.at[1], partner)
    core_copy.wait()
    for t in range(2):
        acc[pl.ds(t * N, N), :] = pgrad[core, t] + core_in[t]
    yz_copies = [
        send(acc.at[part(*yz_at[d])], yz_in.at[d], yz_send.at[0, d], yz_recv.at[0, d], yz_mates[d])
        for d in range(15)]

    @pl.when(tx > 0)
    def _():
        diag.wait_recv()

    for p in range(2):
        edge[p] = grad[p, side, pl.ds(0, N)] + came_diag[p]
    for c in yz_copies:
        c.wait()
    total = acc[part(y, z_low), :]
    for d in range(15):
        total = total + yz_in[d]
    mine = x * 2 + z_high
    shared[mine] = total
    far_copies = [
        send(shared.at[mine], shared.at[mine], far_send.at[d], far_recv.at[d], far_mates[d]) for d in range(7)]
    near_rows = send(edge, out_ty.at[:, pl.ds(0, N)], ty_send.at[0], ty_recv.at[0], partner)

    @pl.when(tx < NTX - 1)
    def _():
        below.start()

    for c in far_copies:
        c.wait()
    total = shared[0]
    for d in range(1, 8):
        total = total + shared[d]
    out_full[part(y, z_low), :] = total * (1.0 / (NTX * 2 * SLOTS))
    yz_copies = [
        send(out_full.at[part(y, z_low)], out_full.at[part(y, z_low)],
             yz_send.at[1, d], yz_recv.at[1, d], yz_mates[d])
        for d in range(15)]
    for c in yz_copies:
        c.wait()
    core_copy = send(out_full, out_other, core_send.at[1], core_recv.at[1], core_mate)

    @pl.when(tx < NTX - 1)
    def _():
        diag.wait_send()
        below.wait_send()

    @pl.when(tx > 0)
    def _():
        below.wait_recv()

    far_rows.wait()
    near_rows.wait()
    core_copy.wait()


def finish_kernel(
    grad, came_ty, came_up, full, other, out_re, out_im, pout_re, pout_im, whole, out_sem, pout_sem,
):
    core, ty = lax.rem(lax.axis_index("tx"), 2), lax.axis_index("ty")

    def probe_copies(re, im):
        return [
            pltpu.make_async_copy(
                src.at[pl.ds(t * N, N)], dst.at[:, pl.ds(t * H, H)], pout_sem.at[k, t])
            for k, (src, dst) in enumerate(((re, pout_re), (im, pout_im))) for t in range(2)]

    @pl.when(core == 0)
    def _():
        for c in probe_copies(full, other):
            c.start()

    @pl.when(core == 1)
    def _():
        for c in probe_copies(other, full):
            c.start()

    copies = []
    for p, out in enumerate((out_re, out_im)):
        for h in range(2):
            rows = pl.ds(h * N, N)
            for t in range(2):
                mine = jnp.where(ty == 1 - t, came_ty[p, rows], 0.0)
                total = grad[p, ty + t, rows] + mine
                whole[p, rows, pl.ds(t * H, H)] = total + came_up[p, t] if h == 0 else total
            copies.append(pltpu.make_async_copy(whole.at[p, rows], out.at[rows], out_sem.at[p, h]))
            copies[-1].start()
    for c in copies + probe_copies(full, other):
        c.wait()


def gather_out(offsets, counts, reg, probe_re, probe_im, tables, amp, grad, pgrad):
    vmem = pl.BlockSpec(memory_space=pltpu.VMEM)
    dma = pltpu.SemaphoreType.DMA
    tile = jax.ShapeDtypeStruct((TR, N), F32)
    patch = jax.ShapeDtypeStruct((N, N), F32)
    smem = pl.BlockSpec(memory_space=pltpu.SMEM)
    grad, *came = pl.pallas_call(
        out_kernel,
        out_shape=(
            pltpu.VMEM((2, 3, ROWS, H), F32),
            jax.ShapeDtypeStruct((2, TR, H), F32),
            jax.ShapeDtypeStruct((2, 2, N, H), F32),
            jax.ShapeDtypeStruct((2 * N, H), F32),
            jax.ShapeDtypeStruct((2 * N, H), F32),
        ),
        in_specs=[smem, smem] + [vmem] * 7,
        out_specs=(vmem,) * 5,
        scratch_shapes=[
            pltpu.VMEM((2, 2, N, H), F32),
            pltpu.VMEM((LAST, 2, 3, N + 2 * CH, H), F32),
            pltpu.VMEM((2, 2, 2, N, H), F32),
            pltpu.VMEM((2, 2, 2, N, N), BF16),
            pltpu.VMEM((2, 2, N, N), F32),
            pltpu.VMEM((2, N, H), F32),
            pltpu.VMEM((2, N, H), F32),
            pltpu.VMEM((2, N, H), F32),
            pltpu.VMEM((2 * N, H), F32),
            pltpu.VMEM((15, 32, H), F32),
            pltpu.VMEM((8, 32, H), F32),
            dma((2,)), dma((2,)), dma(()), dma(()), dma(()), dma(()),
            dma((2,)), dma((2,)), dma((2, 15)), dma((2, 15)), dma((7,)), dma((7,)),
        ],
        compiler_params=pltpu.CompilerParams(
            collective_id=1, has_side_effects=True, vmem_limit_bytes=20 << 20),
        name="gather_out",
    )(offsets, counts, reg, probe_re, probe_im, tables, amp, grad, pgrad)
    return pl.pallas_call(
        finish_kernel,
        out_shape=(tile, tile, patch, patch),
        in_specs=[vmem] * 5,
        out_specs=(pl.BlockSpec(memory_space=pltpu.HBM),) * 4,
        scratch_shapes=[pltpu.VMEM((2, TR, N), F32), dma((2, 2)), dma((2, 2))],
        compiler_params=pltpu.CompilerParams(vmem_limit_bytes=20 << 20),
        name="finish",
    )(grad, *came)


def per_device(obj_re, obj_im, probe_re, probe_im, amplitude, offsets, counts):
    tables = jnp.asarray(half_dft_tables())
    reg, amp, blank = halo(obj_re, obj_im, amplitude)
    shared = (jnp.swapaxes(offsets, 2, 3), counts, reg, probe_re, probe_im, tables, amp)
    grad, pgrad = positions(*shared, blank)
    return gather_out(*shared, grad, pgrad)


def solution(mesh):
    return jax.shard_map(
        per_device,
        mesh=mesh,
        in_specs=(
            P("tx", "ty"),
            P("tx", "ty"),
            P(),
            P(),
            P("tx", "ty", None, None, None),
            P("tx", None, None, None),
            P("tx", None),
        ),
        out_specs=(P("tx", "ty"), P("tx", "ty"), P(), P()),
        check_vma=False,
    )
```

```python
import math

import jax
import jax.numpy as jnp
import ml_dtypes
import numpy as np
from jax import lax
from jax.experimental import pallas as pl
from jax.experimental.pallas import tpu as pltpu
from jax.sharding import PartitionSpec as P

N = 256
H = 128
TR = 512
SLOTS = 12
NTX = 128
ROWS = TR + N
MESH = pl.DeviceIdType.MESH
CH = 32
LAST = 6
EDGE = NTX // 2
DETOUR = ((1, 0, 0), (2, 0, 1), (3, 1, 0), (3, 1, 1))
F32 = jnp.float32
BF16 = jnp.bfloat16


def half_dft_tables():
    n = np.arange(H, dtype=np.float64)[:, None]
    k = np.arange(H, dtype=np.float64)[None, :]
    tables = []
    for odd in (0, 1):
        angle = -2.0 * math.pi * (n * (2 * k + odd)) / N
        re, im = np.cos(angle) / 16.0, np.sin(angle) / 16.0
        tables.append(np.block([[re, im], [-im, re]]))
    both = np.stack([tables[0], tables[1], tables[0].T, tables[1].T])
    high = both.astype(ml_dtypes.bfloat16)
    low = (both - high.astype(np.float64)).astype(ml_dtypes.bfloat16)
    return np.stack([high, low])


def split(x):
    high = x.astype(BF16)
    return high, (x - high.astype(F32)).astype(BF16)


def dot(a, b):
    return jnp.dot(a, b, preferred_element_type=F32)


def halo_kernel(
    obj_re, obj_im, amp, reg, amp_out, blank, raw, perm,
    ty_send, ty_recv, up_send, up_recv, diag_send, diag_recv, own_sem, raw_sem,
    relay, detour_send, detour_recv, relay_send,
):
    tx, ty = lax.axis_index("tx"), lax.axis_index("ty")
    up, down = lax.rem(tx + NTX - 1, NTX), lax.rem(tx + 1, NTX)
    partner = (tx, 1 - ty)
    barrier = pltpu.get_barrier_semaphore()
    for device in (partner, (up, ty), (down, ty)):
        pl.semaphore_signal(barrier, inc=1, device_id=device, device_id_type=MESH)
    is_relay = (tx > EDGE) & (tx <= EDGE + 6) & (lax.rem(tx, 2) == 0)

    @pl.when((tx == EDGE) | (tx == EDGE - 1))
    def _():
        for k in range(1, 4):
            pl.semaphore_signal(barrier, inc=1, device_id=(EDGE + 2 * k, ty), device_id_type=MESH)

    @pl.when(is_relay)
    def _():
        for device in (EDGE, EDGE - 1):
            pl.semaphore_signal(barrier, inc=1, device_id=(device, ty), device_id_type=MESH)

    raw_copies = []
    for t in range(2):
        c = pltpu.make_async_copy(amp.at[0, 0, :, :, pl.ds(t * H, H)], raw.at[t], raw_sem.at[t])
        c.start()
        raw_copies.append(c)
    own = []
    for p, obj in enumerate((obj_re, obj_im)):
        for t in range(2):
            c = pltpu.make_async_copy(
                obj.at[:, pl.ds(t * H, H)], reg.at[p, ty + t, pl.ds(0, TR)], own_sem.at[p, t])
            c.start()
            own.append(c)
    i, j = (lax.broadcasted_iota(jnp.int32, (N, N), d) for d in range(2))
    perm[...] = jnp.where(i == jnp.where(j < H, 2 * j, 2 * (j - H) + 1), 1.0, 0.0).astype(BF16)
    at_edge = (tx == EDGE) | (tx == EDGE - 1)

    @pl.when(at_edge)
    def _():
        pl.semaphore_wait(barrier, 6)

    @pl.when(is_relay)
    def _():
        pl.semaphore_wait(barrier, 5)

    @pl.when(jnp.logical_not(at_edge | is_relay))
    def _():
        pl.semaphore_wait(barrier, 3)


    edge = pl.multiple_of((1 - ty) * H, H)
    across = [[], []]
    for half in range(2):
        for p, obj in enumerate((obj_re, obj_im)):
            rows = pl.ds(half * N, N)
            across[half].append(pltpu.make_async_remote_copy(
                src_ref=obj.at[rows, pl.ds(edge, H)], dst_ref=reg.at[p, 2 * ty, rows],
                send_sem=ty_send.at[half, p], recv_sem=ty_recv.at[half, p],
                device_id=partner, device_id_type=MESH))
    for c in across[0]:
        c.start()
    objs = (obj_re, obj_im)
    blocks = [(p, t) for p in range(2) for t in range(2)]

    def below(p, t):
        return pltpu.make_async_remote_copy(
            src_ref=objs[p].at[pl.ds(0, N), pl.ds(t * H, H)], dst_ref=reg.at[p, ty + t, pl.ds(TR, N)],
            send_sem=up_send.at[p, t], recv_sem=up_recv.at[p, t],
            device_id=(up, ty), device_id_type=MESH)

    def detour(n):
        k, p, t = DETOUR[n]
        return pltpu.make_async_remote_copy(
            src_ref=objs[p].at[pl.ds(0, N), pl.ds(t * H, H)], dst_ref=relay.at[max(n - 2, 0)],
            send_sem=detour_send.at[n], recv_sem=detour_recv.at[max(n - 2, 0)],
            device_id=(EDGE + 2 * k, ty), device_id_type=MESH)

    def onward(n):
        _, p, t = DETOUR[n]
        return pltpu.make_async_remote_copy(
            src_ref=relay.at[max(n - 2, 0)], dst_ref=reg.at[p, ty + t, pl.ds(TR, N)],
            send_sem=relay_send.at[max(n - 2, 0)], recv_sem=up_recv.at[p, t],
            device_id=(EDGE - 1, ty), device_id_type=MESH)

    def diag(p):
        side = 2 - 2 * ty
        return pltpu.make_async_remote_copy(
            src_ref=reg.at[p, side, pl.ds(0, N)], dst_ref=reg.at[p, side, pl.ds(TR, N)],
            send_sem=diag_send.at[p], recv_sem=diag_recv.at[p],
            device_id=(up, ty), device_id_type=MESH)

    sends_up = (tx > 0) & (tx != EDGE)

    @pl.when(sends_up)
    def _():
        for p, t in blocks:
            below(p, t).start()

    @pl.when(tx == EDGE)
    def _():
        for n in range(4):
            detour(n).start()

    blank[...] = jnp.zeros_like(blank)
    for c in raw_copies:
        c.wait()

    def sort_slot(i, carry):
        for h in range(2):
            rows = [raw[t, i, pl.ds(h, H, stride=2), :] for t in range(2)]
            high, low = split(jnp.concatenate(rows, axis=1))
            amp_out[i, pl.ds(h * H, H), :] = dot(high, perm[...]) + dot(low, perm[...])
        return carry

    lax.fori_loop(0, SLOTS // 2, sort_slot, 0)
    for c in across[0]:
        c.wait_send()
    for c in across[1]:
        c.start()
    for p in range(2):
        across[0][p].wait_recv()

        @pl.when(tx > 0)
        def _():
            diag(p).start()

    lax.fori_loop(SLOTS // 2, SLOTS, sort_slot, 0)
    for n in range(4):

        @pl.when(tx == EDGE + 2 * DETOUR[n][0])
        def _():
            detour(n).wait_recv()
            onward(n).start()


    for c in own + across[1]:
        c.wait()

    @pl.when(sends_up)
    def _():
        for p, t in blocks:
            below(p, t).wait_send()

    @pl.when(tx == EDGE)
    def _():
        for n in range(4):
            detour(n).wait_send()

    for n in range(4):

        @pl.when(tx == EDGE + 2 * DETOUR[n][0])
        def _():
            onward(n).wait_send()

    @pl.when(tx > 0)
    def _():
        for p in range(2):
            diag(p).wait_send()

    @pl.when(tx < NTX - 1)
    def _():
        for p, t in blocks:
            below(p, t).wait_recv()
        for p in range(2):
            diag(p).wait_recv()


def halo(obj_re, obj_im, amp):
    hbm, vmem = (pl.BlockSpec(memory_space=m) for m in (pltpu.HBM, pltpu.VMEM))
    dma = pltpu.SemaphoreType.DMA
    return pl.pallas_call(
        halo_kernel,
        out_shape=(
            pltpu.VMEM((2, 3, ROWS, H), F32),
            pltpu.VMEM((SLOTS, N, N), F32),
            pltpu.VMEM((2, 3, ROWS, H), F32),
        ),
        in_specs=[hbm, hbm, hbm],
        out_specs=(vmem, vmem, vmem),
        scratch_shapes=[
            pltpu.VMEM((2, SLOTS, N, H), F32),
            pltpu.VMEM((N, N), BF16),
            dma((2, 2)), dma((2, 2)), dma((2, 2)), dma((2, 2)), dma((2,)), dma((2,)),
            dma((2, 2)), dma((2,)),
            pltpu.VMEM((2, N, H), F32), dma((4,)), dma((2,)), dma((2,)),
        ],
        compiler_params=pltpu.CompilerParams(
            collective_id=0, has_side_effects=True, vmem_limit_bytes=20 << 20),
        name="halo",
    )(*(pltpu.with_memory_space_constraint(x, pltpu.HBM) for x in (obj_re, obj_im, amp)))


def pair_of_positions(reg, probe_re, probe_im, tables, amp, win, sp, mid):
    lane = lax.broadcasted_iota(jnp.int32, (CH, H), 1)

    def put(s, q, rows, lanes, value):
        high, low = split(value)
        sp[s, 0, q, rows, lanes] = high
        sp[s, 1, q, rows, lanes] = low

    def right(s, q, which):
        high, low = sp[s, 0, q], sp[s, 1, q]
        mid[s, q] = dot(jnp.concatenate([high, low, high], axis=1),
                        jnp.concatenate([tables[0, which], tables[0, which], tables[1, which]], axis=0))

    def left(s, q, which):
        high, low = sp[s, 0, q], sp[s, 1, q]
        mid[s, q] = dot(jnp.concatenate([tables[0, which], tables[1, which], tables[0, which]], axis=1),
                        jnp.concatenate([high, high, low], axis=0))

    def lanes(t):
        return pl.ds(t * H, H)

    def enter(s, place):
        row_at, col_at = place
        back = lax.rem(H - col_at, H)
        from_next = lane >= H - col_at
        for j in range(N // CH):
            rows = pl.ds(j * CH, CH)
            ex = [[None, None], [None, None]]
            w = [[None, None], [None, None]]
            for p in range(2):
                turned = [pltpu.roll(reg[p, t, pl.ds(row_at + j * CH, CH), :], back, 1) for t in range(3)]
                for t in range(2):
                    w[p][t] = jnp.where(from_next, turned[t + 1], turned[t])
                    win[s, p, t, rows, :] = w[p][t]
            for t in range(2):
                pr, pi = probe_re[rows, lanes(t)], probe_im[rows, lanes(t)]
                ex[0][t] = pr * w[0][t] - pi * w[1][t]
                ex[1][t] = pr * w[1][t] + pi * w[0][t]
            for p in range(2):
                put(s, 0, rows, lanes(p), ex[p][0] + ex[p][1])
                put(s, 1, rows, lanes(p), ex[p][0] - ex[p][1])

    def fold_rows(s):
        for j in range(H // CH):
            for q in range(2):
                for p in range(2):
                    top = mid[s, q, pl.ds(j * CH, CH), lanes(p)]
                    low = mid[s, q, pl.ds(H + j * CH, CH), lanes(p)]
                    rows = pl.ds(p * H + j * CH, CH)
                    put(s, 0, rows, lanes(q), top + low)
                    put(s, 1, rows, lanes(q), top - low)

    def compare(s, i, used):
        for j in range(H // CH):
            for h in range(2):
                rows_re, rows_im = pl.ds(j * CH, CH), pl.ds(H + j * CH, CH)
                re, im = mid[s, h, rows_re, :], mid[s, h, rows_im, :]
                measured = amp[i, pl.ds(h * H + j * CH, CH), :]
                keep = 1.0 - measured * lax.rsqrt(jnp.maximum(re * re + im * im, 1.0))
                keep = jnp.where(used, keep, 0.0)
                put(s, h, rows_re, slice(None), re * keep)
                put(s, h, rows_im, slice(None), im * keep)

    def unfold_rows(s):
        for j in range(H // CH):
            for p in range(2):
                for q in range(2):
                    a = mid[s, 0, pl.ds(p * H + j * CH, CH), lanes(q)]
                    b = mid[s, 1, pl.ds(p * H + j * CH, CH), lanes(q)]
                    put(s, q, pl.ds(j * CH, CH), lanes(p), a + b)
                    put(s, q, pl.ds(H + j * CH, CH), lanes(p), a - b)

    def leave(s, place, add_rows, add_probe):
        row_at, col_at = place
        ahead = lax.rem(col_at, H)
        to_next = lane < col_at
        for j in range(N // CH):
            rows = pl.ds(j * CH, CH)
            g = [[None, None], [None, None]]
            for t in range(2):
                chi = []
                for p in range(2):
                    a, b = mid[s, 0, rows, lanes(p)], mid[s, 1, rows, lanes(p)]
                    chi.append(a + b if t == 0 else a - b)
                pr, pi = probe_re[rows, lanes(t)], probe_im[rows, lanes(t)]
                wr, wi = win[s, 0, t, rows, :], win[s, 1, t, rows, :]
                g[0][t] = pltpu.roll(pr * chi[0] + pi * chi[1], ahead, 1)
                g[1][t] = pltpu.roll(pr * chi[1] - pi * chi[0], ahead, 1)
                add_probe(t, rows, wr * chi[0] + wi * chi[1], wr * chi[1] - wi * chi[0])
            for p in range(2):
                add_rows(s, row_at, j, p, (
                    jnp.where(to_next, 0.0, g[p][0]),
                    jnp.where(to_next, g[p][0], g[p][1]),
                    jnp.where(to_next, g[p][1], 0.0)))

    def pair(places, ids, used, add_rows, add_probe):
        stages = [
            lambda s: enter(s, places[s]),
            lambda s: [right(s, q, q) for q in range(2)],
            lambda s: fold_rows(s),
            lambda s: [left(s, h, 2 + h) for h in range(2)],
            lambda s: compare(s, ids[s], used[s]),
            lambda s: [left(s, h, h) for h in range(2)],
            lambda s: unfold_rows(s),
            lambda s: [right(s, q, 2 + q) for q in range(2)],
            lambda s: leave(s, places[s], add_rows, add_probe),
        ]
        stages[0](0)
        for n in range(1, len(stages)):
            stages[n](0)
            stages[n - 1](1)
        stages[-1](1)

    return pair


def place_of(offsets, tx, ty, i):
    row_at, col_at = offsets[0, ty, 0, i] - tx * TR, offsets[0, ty, 1, i] - ty * H
    return jnp.clip(row_at, 0, TR - 1), jnp.clip(col_at, 0, H)


def positions_kernel(
    offsets, counts, reg, probe_re, probe_im, tables, amp, blank, grad, pgrad, win, sp, mid,
):
    tx, ty = lax.axis_index("tx"), lax.axis_index("ty")
    here = jnp.maximum(counts[0, ty] - LAST, 0)
    pgrad[...] = jnp.zeros_like(pgrad)
    pair = pair_of_positions(reg, probe_re, probe_im, tables, amp, win, sp, mid)

    def add_rows(s, row_at, j, p, tiles):
        at = pl.ds(row_at + j * CH, CH)
        for t in range(3):
            grad[p, t, at, :] += tiles[t]

    def add_probe(t, rows, re, im):
        pgrad[0, t, rows, :] += re
        pgrad[1, t, rows, :] += im

    def step(k, carry):
        ids = [2 * k, jnp.minimum(2 * k + 1, here - 1)]
        pair([place_of(offsets, tx, ty, i) for i in ids], ids, [True, 2 * k + 1 < here], add_rows, add_probe)
        return carry

    lax.fori_loop(0, (here + 1) // 2, step, 0)


def positions(offsets, counts, reg, probe_re, probe_im, tables, amp, blank):
    smem = pl.BlockSpec(memory_space=pltpu.SMEM)
    vmem = pl.BlockSpec(memory_space=pltpu.VMEM)
    return pl.pallas_call(
        positions_kernel,
        out_shape=(
            pltpu.VMEM((2, 3, ROWS, H), F32),
            pltpu.VMEM((2, 2, N, H), F32),
        ),
        in_specs=[smem, smem] + [vmem] * 6,
        input_output_aliases={7: 0},
        out_specs=(vmem, vmem),
        scratch_shapes=[
            pltpu.VMEM((2, 2, 2, N, H), F32),
            pltpu.VMEM((2, 2, 2, N, N), BF16),
            pltpu.VMEM((2, 2, N, N), F32),
        ],
        compiler_params=pltpu.CompilerParams(vmem_limit_bytes=20 << 20),
        name="positions",
    )(offsets, counts, reg, probe_re, probe_im, tables, amp, blank)


def out_kernel(
    offsets, counts, reg, probe_re, probe_im, tables, amp, grad_in, pgrad_in, grad, out_ty, out_up, out_full, out_other,
    pgrad, placed, win, sp, mid, came_diag, edge, core_in, acc, yz_in, shared,
    ty_send, ty_recv, up_send, up_recv, diag_send, diag_recv,
    core_send, core_recv, yz_send, yz_recv, far_send, far_recv,
):
    tx, ty = lax.axis_index("tx"), lax.axis_index("ty")
    up, down = lax.rem(tx + NTX - 1, NTX), lax.rem(tx + 1, NTX)
    partner = (tx, 1 - ty)
    core, y, z, x_lo = lax.rem(tx, 2), lax.rem(tx // 2, 4), lax.rem(tx // 8, 8), tx // 64
    x = ty * 2 + x_lo

    def at(core_, y_, z_, x_):
        return (((lax.rem(x_, 2) * 8 + z_) * 4 + y_) * 2 + core_, x_ // 2)

    core_mate = at(1 - core, y, z, x)
    z_low, z_high = lax.rem(z, 4), z // 4
    steps = [(i, j) for i in range(4) for j in range(4) if i or j]
    steps.sort(key=lambda s: -(min(s[0], 4 - s[0]) + min(s[1], 4 - s[1])))
    yz_at = [(lax.rem(y + i, 4), lax.rem(z_low + j, 4)) for i, j in steps]
    yz_mates = [at(core, i, z_high * 4 + j, x) for i, j in yz_at]
    hops = [(1, 2), (1, 1), (1, 3), (1, 0), (0, 2), (0, 1), (0, 3)]
    far_mates = [at(core, y, lax.rem(z_high + i, 2) * 4 + z_low, lax.rem(x + j, 4)) for i, j in hops]
    greeted = far_mates + yz_mates + [partner, (up, ty), (down, ty), core_mate]
    barrier = pltpu.get_barrier_semaphore()
    for device in greeted:
        pl.semaphore_signal(barrier, inc=1, device_id=device, device_id_type=MESH)

    live = counts[0, ty]
    for margin in (0, CH + N):
        placed[:, :, :, pl.ds(margin, CH), :] = jnp.zeros((LAST, 2, 3, CH, H), F32)
    pgrad[...] = pgrad_in[...]
    pair = pair_of_positions(reg, probe_re, probe_im, tables, amp, win, sp, mid)

    def add_probe(t, rows, re, im):
        pgrad[0, t, rows, :] += re
        pgrad[1, t, rows, :] += im

    def id_of(n):
        return jnp.maximum(live - LAST + n, 0)

    def step(k, carry):
        ids = [id_of(2 * k + s) for s in range(2)]

        def add_rows(s, row_at, j, p, tiles):
            for t in range(3):
                placed[2 * k + s, p, t, pl.ds(CH + j * CH, CH), :] = tiles[t]

        pair([place_of(offsets, tx, ty, i) for i in ids], ids,
             [live - LAST + 2 * k + s >= 0 for s in range(2)], add_rows, add_probe)
        return carry

    lax.fori_loop(0, LAST // 2, step, 0)
    pl.semaphore_wait(barrier, len(greeted))

    def make(src, dst, send_sem, recv_sem, device):
        return pltpu.make_async_remote_copy(
            src_ref=src, dst_ref=dst, send_sem=send_sem, recv_sem=recv_sem,
            device_id=device, device_id_type=MESH)

    def send(*args):
        c = make(*args)
        c.start()
        return c

    def part(i, j):
        return pl.ds(pl.multiple_of((i * 4 + j) * 32, 32), 32)

    side = 2 - 2 * ty
    core_copy = send(pgrad.at[1 - core], core_in, core_send.at[0], core_recv.at[0], core_mate)

    firsts = [place_of(offsets, tx, ty, id_of(n))[0] for n in range(LAST)]

    def place_rows(j, carry):
        rows = pl.ds(pl.multiple_of(j * CH, CH), CH)
        for p in range(2):
            for t in range(3):
                total = grad_in[p, t, rows, :]
                for n in range(LAST):
                    at = jnp.clip(j * CH - firsts[n] + CH, 0, CH + N)
                    total = total + placed[n, p, t, pl.ds(at, CH), :]
                grad[p, t, rows, :] = total
        return carry

    lax.fori_loop(0, ROWS // CH, place_rows, 0)
    diag = make(grad.at[:, side, pl.ds(TR, N)], came_diag, diag_send, diag_recv, (down, ty))
    below = make(grad.at[:, pl.ds(ty, 2), pl.ds(TR, N)], out_up, up_send, up_recv, (down, ty))

    @pl.when(tx < NTX - 1)
    def _():
        diag.start()

    @pl.when(tx == 0)
    def _():
        came_diag[...] = jnp.zeros_like(came_diag)
        out_up[...] = jnp.zeros_like(out_up)

    far_rows = send(
        grad.at[:, side, pl.ds(N, N)], out_ty.at[:, pl.ds(N, N)], ty_send.at[1], ty_recv.at[1], partner)
    core_copy.wait()
    for t in range(2):
        acc[pl.ds(t * N, N), :] = pgrad[core, t] + core_in[t]
    yz_copies = [
        send(acc.at[part(*yz_at[d])], yz_in.at[d], yz_send.at[0, d], yz_recv.at[0, d], yz_mates[d])
        for d in range(15)]

    @pl.when(tx > 0)
    def _():
        diag.wait_recv()

    for p in range(2):
        edge[p] = grad[p, side, pl.ds(0, N)] + came_diag[p]
    for c in yz_copies:
        c.wait()
    total = acc[part(y, z_low), :]
    for d in range(15):
        total = total + yz_in[d]
    mine = x * 2 + z_high
    shared[mine] = total
    far_copies = [
        send(shared.at[mine], shared.at[mine], far_send.at[d], far_recv.at[d], far_mates[d]) for d in range(7)]
    near_rows = send(edge, out_ty.at[:, pl.ds(0, N)], ty_send.at[0], ty_recv.at[0], partner)

    @pl.when(tx < NTX - 1)
    def _():
        below.start()

    for c in far_copies:
        c.wait()
    total = shared[0]
    for d in range(1, 8):
        total = total + shared[d]
    out_full[part(y, z_low), :] = total * (1.0 / (NTX * 2 * SLOTS))
    yz_copies = [
        send(out_full.at[part(y, z_low)], out_full.at[part(y, z_low)],
             yz_send.at[1, d], yz_recv.at[1, d], yz_mates[d])
        for d in range(15)]
    for c in yz_copies:
        c.wait()
    core_copy = send(out_full, out_other, core_send.at[1], core_recv.at[1], core_mate)

    @pl.when(tx < NTX - 1)
    def _():
        diag.wait_send()
        below.wait_send()

    @pl.when(tx > 0)
    def _():
        below.wait_recv()

    far_rows.wait()
    near_rows.wait()
    core_copy.wait()


def finish_kernel(
    grad, came_ty, came_up, full, other, out_re, out_im, pout_re, pout_im, whole, out_sem, pout_sem,
):
    core, ty = lax.rem(lax.axis_index("tx"), 2), lax.axis_index("ty")

    def probe_copies(re, im):
        return [
            pltpu.make_async_copy(
                src.at[pl.ds(t * N, N)], dst.at[:, pl.ds(t * H, H)], pout_sem.at[k, t])
            for k, (src, dst) in enumerate(((re, pout_re), (im, pout_im))) for t in range(2)]

    @pl.when(core == 0)
    def _():
        for c in probe_copies(full, other):
            c.start()

    @pl.when(core == 1)
    def _():
        for c in probe_copies(other, full):
            c.start()

    copies = []
    for p, out in enumerate((out_re, out_im)):
        for h in range(2):
            rows = pl.ds(h * N, N)
            for t in range(2):
                mine = jnp.where(ty == 1 - t, came_ty[p, rows], 0.0)
                total = grad[p, ty + t, rows] + mine
                whole[p, rows, pl.ds(t * H, H)] = total + came_up[p, t] if h == 0 else total
            copies.append(pltpu.make_async_copy(whole.at[p, rows], out.at[rows], out_sem.at[p, h]))
            copies[-1].start()
    for c in copies + probe_copies(full, other):
        c.wait()


def gather_out(offsets, counts, reg, probe_re, probe_im, tables, amp, grad, pgrad):
    vmem = pl.BlockSpec(memory_space=pltpu.VMEM)
    dma = pltpu.SemaphoreType.DMA
    tile = jax.ShapeDtypeStruct((TR, N), F32)
    patch = jax.ShapeDtypeStruct((N, N), F32)
    smem = pl.BlockSpec(memory_space=pltpu.SMEM)
    grad, *came = pl.pallas_call(
        out_kernel,
        out_shape=(
            pltpu.VMEM((2, 3, ROWS, H), F32),
            jax.ShapeDtypeStruct((2, TR, H), F32),
            jax.ShapeDtypeStruct((2, 2, N, H), F32),
            jax.ShapeDtypeStruct((2 * N, H), F32),
            jax.ShapeDtypeStruct((2 * N, H), F32),
        ),
        in_specs=[smem, smem] + [vmem] * 7,
        out_specs=(vmem,) * 5,
        scratch_shapes=[
            pltpu.VMEM((2, 2, N, H), F32),
            pltpu.VMEM((LAST, 2, 3, N + 2 * CH, H), F32),
            pltpu.VMEM((2, 2, 2, N, H), F32),
            pltpu.VMEM((2, 2, 2, N, N), BF16),
            pltpu.VMEM((2, 2, N, N), F32),
            pltpu.VMEM((2, N, H), F32),
            pltpu.VMEM((2, N, H), F32),
            pltpu.VMEM((2, N, H), F32),
            pltpu.VMEM((2 * N, H), F32),
            pltpu.VMEM((15, 32, H), F32),
            pltpu.VMEM((8, 32, H), F32),
            dma((2,)), dma((2,)), dma(()), dma(()), dma(()), dma(()),
            dma((2,)), dma((2,)), dma((2, 15)), dma((2, 15)), dma((7,)), dma((7,)),
        ],
        compiler_params=pltpu.CompilerParams(
            collective_id=1, has_side_effects=True, vmem_limit_bytes=20 << 20),
        name="gather_out",
    )(offsets, counts, reg, probe_re, probe_im, tables, amp, grad, pgrad)
    return pl.pallas_call(
        finish_kernel,
        out_shape=(tile, tile, patch, patch),
        in_specs=[vmem] * 5,
        out_specs=(pl.BlockSpec(memory_space=pltpu.HBM),) * 4,
        scratch_shapes=[pltpu.VMEM((2, TR, N), F32), dma((2, 2)), dma((2, 2))],
        compiler_params=pltpu.CompilerParams(vmem_limit_bytes=20 << 20),
        name="finish",
    )(grad, *came)


def per_device(obj_re, obj_im, probe_re, probe_im, amplitude, offsets, counts):
    tables = jnp.asarray(half_dft_tables())
    reg, amp, blank = halo(obj_re, obj_im, amplitude)
    shared = (jnp.swapaxes(offsets, 2, 3), counts, reg, probe_re, probe_im, tables, amp)
    grad, pgrad = positions(*shared, blank)
    return gather_out(*shared, grad, pgrad)


def solution(mesh):
    return jax.shard_map(
        per_device,
        mesh=mesh,
        in_specs=(
            P("tx", "ty"),
            P("tx", "ty"),
            P(),
            P(),
            P("tx", "ty", None, None, None),
            P("tx", None, None, None),
            P("tx", None),
        ),
        out_specs=(P("tx", "ty"), P("tx", "ty"), P(), P()),
        check_vma=False,
    )
```

```python
import math

import jax
import jax.numpy as jnp
import ml_dtypes
import numpy as np
from jax import lax
from jax.experimental import pallas as pl
from jax.experimental.pallas import tpu as pltpu
from jax.sharding import PartitionSpec as P

N = 256
H = 128
TR = 512
SLOTS = 12
NTX = 128
ROWS = TR + N
MESH = pl.DeviceIdType.MESH
CH = 32
LAST = 6
EDGE = NTX // 2
DETOUR = ((1, 0, 0), (2, 0, 1), (3, 1, 0), (3, 1, 1))
F32 = jnp.float32
BF16 = jnp.bfloat16


def half_dft_tables():
    n = np.arange(H, dtype=np.float64)[:, None]
    k = np.arange(H, dtype=np.float64)[None, :]
    tables = []
    for odd in (0, 1):
        angle = -2.0 * math.pi * (n * (2 * k + odd)) / N
        re, im = np.cos(angle) / 16.0, np.sin(angle) / 16.0
        tables.append(np.block([[re, im], [-im, re]]))
    both = np.stack([tables[0], tables[1], tables[0].T, tables[1].T])
    high = both.astype(ml_dtypes.bfloat16)
    low = (both - high.astype(np.float64)).astype(ml_dtypes.bfloat16)
    return np.stack([high, low])


def split(x):
    high = x.astype(BF16)
    return high, (x - high.astype(F32)).astype(BF16)


def dot(a, b):
    return jnp.dot(a, b, preferred_element_type=F32)


def halo_kernel(
    obj_re, obj_im, amp, reg, amp_out, blank, raw, perm,
    ty_send, ty_recv, up_send, up_recv, diag_send, diag_recv, own_sem, raw_sem,
    relay, detour_send, detour_recv, relay_send,
):
    tx, ty = lax.axis_index("tx"), lax.axis_index("ty")
    up, down = lax.rem(tx + NTX - 1, NTX), lax.rem(tx + 1, NTX)
    partner = (tx, 1 - ty)
    barrier = pltpu.get_barrier_semaphore()
    for device in (partner, (up, ty), (down, ty)):
        pl.semaphore_signal(barrier, inc=1, device_id=device, device_id_type=MESH)
    is_relay = (tx > EDGE) & (tx <= EDGE + 6) & (lax.rem(tx, 2) == 0)

    @pl.when((tx == EDGE) | (tx == EDGE - 1))
    def _():
        for k in range(1, 4):
            pl.semaphore_signal(barrier, inc=1, device_id=(EDGE + 2 * k, ty), device_id_type=MESH)

    @pl.when(is_relay)
    def _():
        for device in (EDGE, EDGE - 1):
            pl.semaphore_signal(barrier, inc=1, device_id=(device, ty), device_id_type=MESH)

    raw_copies = []
    for t in range(2):
        c = pltpu.make_async_copy(amp.at[0, 0, :, :, pl.ds(t * H, H)], raw.at[t], raw_sem.at[t])
        c.start()
        raw_copies.append(c)
    own = []
    for p, obj in enumerate((obj_re, obj_im)):
        for t in range(2):
            c = pltpu.make_async_copy(
                obj.at[:, pl.ds(t * H, H)], reg.at[p, ty + t, pl.ds(0, TR)], own_sem.at[p, t])
            c.start()
            own.append(c)
    i, j = (lax.broadcasted_iota(jnp.int32, (N, N), d) for d in range(2))
    perm[...] = jnp.where(i == jnp.where(j < H, 2 * j, 2 * (j - H) + 1), 1.0, 0.0).astype(BF16)
    at_edge = (tx == EDGE) | (tx == EDGE - 1)

    @pl.when(at_edge)
    def _():
        pl.semaphore_wait(barrier, 6)

    @pl.when(is_relay)
    def _():
        pl.semaphore_wait(barrier, 5)

    @pl.when(jnp.logical_not(at_edge | is_relay))
    def _():
        pl.semaphore_wait(barrier, 3)


    edge = pl.multiple_of((1 - ty) * H, H)
    across = [[], []]
    for half in range(2):
        for p, obj in enumerate((obj_re, obj_im)):
            rows = pl.ds(half * N, N)
            across[half].append(pltpu.make_async_remote_copy(
                src_ref=obj.at[rows, pl.ds(edge, H)], dst_ref=reg.at[p, 2 * ty, rows],
                send_sem=ty_send.at[half, p], recv_sem=ty_recv.at[half, p],
                device_id=partner, device_id_type=MESH))
    for c in across[0]:
        c.start()
    objs = (obj_re, obj_im)
    blocks = [(p, t) for p in range(2) for t in range(2)]

    def below(p, t):
        return pltpu.make_async_remote_copy(
            src_ref=objs[p].at[pl.ds(0, N), pl.ds(t * H, H)], dst_ref=reg.at[p, ty + t, pl.ds(TR, N)],
            send_sem=up_send.at[p, t], recv_sem=up_recv.at[p, t],
            device_id=(up, ty), device_id_type=MESH)

    def detour(n):
        k, p, t = DETOUR[n]
        return pltpu.make_async_remote_copy(
            src_ref=objs[p].at[pl.ds(0, N), pl.ds(t * H, H)], dst_ref=relay.at[max(n - 2, 0)],
            send_sem=detour_send.at[n], recv_sem=detour_recv.at[max(n - 2, 0)],
            device_id=(EDGE + 2 * k, ty), device_id_type=MESH)

    def onward(n):
        _, p, t = DETOUR[n]
        return pltpu.make_async_remote_copy(
            src_ref=relay.at[max(n - 2, 0)], dst_ref=reg.at[p, ty + t, pl.ds(TR, N)],
            send_sem=relay_send.at[max(n - 2, 0)], recv_sem=up_recv.at[p, t],
            device_id=(EDGE - 1, ty), device_id_type=MESH)

    def diag(p):
        side = 2 - 2 * ty
        return pltpu.make_async_remote_copy(
            src_ref=reg.at[p, side, pl.ds(0, N)], dst_ref=reg.at[p, side, pl.ds(TR, N)],
            send_sem=diag_send.at[p], recv_sem=diag_recv.at[p],
            device_id=(up, ty), device_id_type=MESH)

    sends_up = (tx > 0) & (tx != EDGE)

    @pl.when(sends_up)
    def _():
        for p, t in blocks:
            below(p, t).start()

    @pl.when(tx == EDGE)
    def _():
        for n in range(4):
            detour(n).start()

    blank[...] = jnp.zeros_like(blank)
    for c in raw_copies:
        c.wait()

    def sort_slot(i, carry):
        for h in range(2):
            rows = [raw[t, i, pl.ds(h, H, stride=2), :] for t in range(2)]
            high, low = split(jnp.concatenate(rows, axis=1))
            amp_out[i, pl.ds(h * H, H), :] = dot(high, perm[...]) + dot(low, perm[...])
        return carry

    lax.fori_loop(0, SLOTS // 2, sort_slot, 0)
    for c in across[0]:
        c.wait_send()
    for c in across[1]:
        c.start()
    for p in range(2):
        across[0][p].wait_recv()

        @pl.when(tx > 0)
        def _():
            diag(p).start()

    lax.fori_loop(SLOTS // 2, SLOTS, sort_slot, 0)
    for n in range(4):

        @pl.when(tx == EDGE + 2 * DETOUR[n][0])
        def _():
            detour(n).wait_recv()
            onward(n).start()


    for c in own + across[1]:
        c.wait()

    @pl.when(sends_up)
    def _():
        for p, t in blocks:
            below(p, t).wait_send()

    @pl.when(tx == EDGE)
    def _():
        for n in range(4):
            detour(n).wait_send()

    for n in range(4):

        @pl.when(tx == EDGE + 2 * DETOUR[n][0])
        def _():
            onward(n).wait_send()

    @pl.when(tx > 0)
    def _():
        for p in range(2):
            diag(p).wait_send()

    @pl.when(tx < NTX - 1)
    def _():
        for p, t in blocks:
            below(p, t).wait_recv()
        for p in range(2):
            diag(p).wait_recv()


def halo(obj_re, obj_im, amp):
    hbm, vmem = (pl.BlockSpec(memory_space=m) for m in (pltpu.HBM, pltpu.VMEM))
    dma = pltpu.SemaphoreType.DMA
    return pl.pallas_call(
        halo_kernel,
        out_shape=(
            pltpu.VMEM((2, 3, ROWS, H), F32),
            pltpu.VMEM((SLOTS, N, N), F32),
            pltpu.VMEM((2, 3, ROWS, H), F32),
        ),
        in_specs=[hbm, hbm, hbm],
        out_specs=(vmem, vmem, vmem),
        scratch_shapes=[
            pltpu.VMEM((2, SLOTS, N, H), F32),
            pltpu.VMEM((N, N), BF16),
            dma((2, 2)), dma((2, 2)), dma((2, 2)), dma((2, 2)), dma((2,)), dma((2,)),
            dma((2, 2)), dma((2,)),
            pltpu.VMEM((2, N, H), F32), dma((4,)), dma((2,)), dma((2,)),
        ],
        compiler_params=pltpu.CompilerParams(
            collective_id=0, has_side_effects=True, vmem_limit_bytes=20 << 20),
        name="halo",
    )(*(pltpu.with_memory_space_constraint(x, pltpu.HBM) for x in (obj_re, obj_im, amp)))


def pair_of_positions(reg, probe_re, probe_im, tables, amp, win, sp, mid):
    lane = lax.broadcasted_iota(jnp.int32, (CH, H), 1)

    def put(s, q, rows, lanes, value):
        high, low = split(value)
        sp[s, 0, q, rows, lanes] = high
        sp[s, 1, q, rows, lanes] = low

    def right(s, q, which):
        high, low = sp[s, 0, q], sp[s, 1, q]
        mid[s, q] = dot(jnp.concatenate([high, low, high], axis=1),
                        jnp.concatenate([tables[0, which], tables[0, which], tables[1, which]], axis=0))

    def left(s, q, which):
        high, low = sp[s, 0, q], sp[s, 1, q]
        mid[s, q] = dot(jnp.concatenate([tables[0, which], tables[1, which], tables[0, which]], axis=1),
                        jnp.concatenate([high, high, low], axis=0))

    def lanes(t):
        return pl.ds(t * H, H)

    def enter(s, place):
        row_at, col_at = place
        back = lax.rem(H - col_at, H)
        from_next = lane >= H - col_at
        for j in range(N // CH):
            rows = pl.ds(j * CH, CH)
            ex = [[None, None], [None, None]]
            w = [[None, None], [None, None]]
            for p in range(2):
                turned = [pltpu.roll(reg[p, t, pl.ds(row_at + j * CH, CH), :], back, 1) for t in range(3)]
                for t in range(2):
                    w[p][t] = jnp.where(from_next, turned[t + 1], turned[t])
                    win[s, p, t, rows, :] = w[p][t]
            for t in range(2):
                pr, pi = probe_re[rows, lanes(t)], probe_im[rows, lanes(t)]
                ex[0][t] = pr * w[0][t] - pi * w[1][t]
                ex[1][t] = pr * w[1][t] + pi * w[0][t]
            for p in range(2):
                put(s, 0, rows, lanes(p), ex[p][0] + ex[p][1])
                put(s, 1, rows, lanes(p), ex[p][0] - ex[p][1])

    def fold_rows(s):
        for j in range(H // CH):
            for q in range(2):
                for p in range(2):
                    top = mid[s, q, pl.ds(j * CH, CH), lanes(p)]
                    low = mid[s, q, pl.ds(H + j * CH, CH), lanes(p)]
                    rows = pl.ds(p * H + j * CH, CH)
                    put(s, 0, rows, lanes(q), top + low)
                    put(s, 1, rows, lanes(q), top - low)

    def compare(s, i, used):
        for j in range(H // CH):
            for h in range(2):
                rows_re, rows_im = pl.ds(j * CH, CH), pl.ds(H + j * CH, CH)
                re, im = mid[s, h, rows_re, :], mid[s, h, rows_im, :]
                measured = amp[i, pl.ds(h * H + j * CH, CH), :]
                keep = 1.0 - measured * lax.rsqrt(jnp.maximum(re * re + im * im, 1.0))
                keep = jnp.where(used, keep, 0.0)
                put(s, h, rows_re, slice(None), re * keep)
                put(s, h, rows_im, slice(None), im * keep)

    def unfold_rows(s):
        for j in range(H // CH):
            for p in range(2):
                for q in range(2):
                    a = mid[s, 0, pl.ds(p * H + j * CH, CH), lanes(q)]
                    b = mid[s, 1, pl.ds(p * H + j * CH, CH), lanes(q)]
                    put(s, q, pl.ds(j * CH, CH), lanes(p), a + b)
                    put(s, q, pl.ds(H + j * CH, CH), lanes(p), a - b)

    def leave(s, place, add_rows, add_probe):
        row_at, col_at = place
        ahead = lax.rem(col_at, H)
        to_next = lane < col_at
        for j in range(N // CH):
            rows = pl.ds(j * CH, CH)
            g = [[None, None], [None, None]]
            for t in range(2):
                chi = []
                for p in range(2):
                    a, b = mid[s, 0, rows, lanes(p)], mid[s, 1, rows, lanes(p)]
                    chi.append(a + b if t == 0 else a - b)
                pr, pi = probe_re[rows, lanes(t)], probe_im[rows, lanes(t)]
                wr, wi = win[s, 0, t, rows, :], win[s, 1, t, rows, :]
                g[0][t] = pltpu.roll(pr * chi[0] + pi * chi[1], ahead, 1)
                g[1][t] = pltpu.roll(pr * chi[1] - pi * chi[0], ahead, 1)
                add_probe(t, rows, wr * chi[0] + wi * chi[1], wr * chi[1] - wi * chi[0])
            for p in range(2):
                add_rows(s, row_at, j, p, (
                    jnp.where(to_next, 0.0, g[p][0]),
                    jnp.where(to_next, g[p][0], g[p][1]),
                    jnp.where(to_next, g[p][1], 0.0)))

    def pair(places, ids, used, add_rows, add_probe):
        stages = [
            lambda s: enter(s, places[s]),
            lambda s: [right(s, q, q) for q in range(2)],
            lambda s: fold_rows(s),
            lambda s: [left(s, h, 2 + h) for h in range(2)],
            lambda s: compare(s, ids[s], used[s]),
            lambda s: [left(s, h, h) for h in range(2)],
            lambda s: unfold_rows(s),
            lambda s: [right(s, q, 2 + q) for q in range(2)],
            lambda s: leave(s, places[s], add_rows, add_probe),
        ]
        stages[0](0)
        for n in range(1, len(stages)):
            stages[n](0)
            stages[n - 1](1)
        stages[-1](1)

    return pair


def place_of(offsets, tx, ty, i):
    row_at, col_at = offsets[0, ty, 0, i] - tx * TR, offsets[0, ty, 1, i] - ty * H
    return jnp.clip(row_at, 0, TR - 1), jnp.clip(col_at, 0, H)


def positions_kernel(
    offsets, counts, reg, probe_re, probe_im, tables, amp, blank, grad, pgrad, win, sp, mid,
):
    tx, ty = lax.axis_index("tx"), lax.axis_index("ty")
    here = jnp.maximum(counts[0, ty] - LAST, 0)
    pgrad[...] = jnp.zeros_like(pgrad)
    pair = pair_of_positions(reg, probe_re, probe_im, tables, amp, win, sp, mid)

    def add_rows(s, row_at, j, p, tiles):
        at = pl.ds(row_at + j * CH, CH)
        for t in range(3):
            grad[p, t, at, :] += tiles[t]

    def add_probe(t, rows, re, im):
        pgrad[0, t, rows, :] += re
        pgrad[1, t, rows, :] += im

    def step(k, carry):
        ids = [2 * k, jnp.minimum(2 * k + 1, here - 1)]
        pair([place_of(offsets, tx, ty, i) for i in ids], ids, [True, 2 * k + 1 < here], add_rows, add_probe)
        return carry

    lax.fori_loop(0, (here + 1) // 2, step, 0)


def positions(offsets, counts, reg, probe_re, probe_im, tables, amp, blank):
    smem = pl.BlockSpec(memory_space=pltpu.SMEM)
    vmem = pl.BlockSpec(memory_space=pltpu.VMEM)
    return pl.pallas_call(
        positions_kernel,
        out_shape=(
            pltpu.VMEM((2, 3, ROWS, H), F32),
            pltpu.VMEM((2, 2, N, H), F32),
        ),
        in_specs=[smem, smem] + [vmem] * 6,
        input_output_aliases={7: 0},
        out_specs=(vmem, vmem),
        scratch_shapes=[
            pltpu.VMEM((2, 2, 2, N, H), F32),
            pltpu.VMEM((2, 2, 2, N, N), BF16),
            pltpu.VMEM((2, 2, N, N), F32),
        ],
        compiler_params=pltpu.CompilerParams(vmem_limit_bytes=20 << 20),
        name="positions",
    )(offsets, counts, reg, probe_re, probe_im, tables, amp, blank)


def out_kernel(
    offsets, counts, reg, probe_re, probe_im, tables, amp, grad_in, pgrad_in, grad, out_ty, out_up, out_full, out_other,
    pgrad, placed, win, sp, mid, came_diag, edge, core_in, acc, yz_in, shared,
    ty_send, ty_recv, up_send, up_recv, diag_send, diag_recv,
    core_send, core_recv, yz_send, yz_recv, far_send, far_recv,
):
    tx, ty = lax.axis_index("tx"), lax.axis_index("ty")
    up, down = lax.rem(tx + NTX - 1, NTX), lax.rem(tx + 1, NTX)
    partner = (tx, 1 - ty)
    core, y, z, x_lo = lax.rem(tx, 2), lax.rem(tx // 2, 4), lax.rem(tx // 8, 8), tx // 64
    x = ty * 2 + x_lo

    def at(core_, y_, z_, x_):
        return (((lax.rem(x_, 2) * 8 + z_) * 4 + y_) * 2 + core_, x_ // 2)

    core_mate = at(1 - core, y, z, x)
    z_low, z_high = lax.rem(z, 4), z // 4
    steps = [(i, j) for i in range(4) for j in range(4) if i or j]
    steps.sort(key=lambda s: -(min(s[0], 4 - s[0]) + min(s[1], 4 - s[1])))
    yz_at = [(lax.rem(y + i, 4), lax.rem(z_low + j, 4)) for i, j in steps]
    yz_mates = [at(core, i, z_high * 4 + j, x) for i, j in yz_at]
    hops = [(1, 2), (1, 1), (1, 3), (1, 0), (0, 2), (0, 1), (0, 3)]
    far_mates = [at(core, y, lax.rem(z_high + i, 2) * 4 + z_low, lax.rem(x + j, 4)) for i, j in hops]
    greeted = far_mates + yz_mates + [partner, (up, ty), (down, ty), core_mate]
    barrier = pltpu.get_barrier_semaphore()
    for device in greeted:
        pl.semaphore_signal(barrier, inc=1, device_id=device, device_id_type=MESH)

    live = counts[0, ty]
    for margin in (0, CH + N):
        placed[:, :, :, pl.ds(margin, CH), :] = jnp.zeros((LAST, 2, 3, CH, H), F32)
    pgrad[...] = pgrad_in[...]
    pair = pair_of_positions(reg, probe_re, probe_im, tables, amp, win, sp, mid)

    def add_probe(t, rows, re, im):
        pgrad[0, t, rows, :] += re
        pgrad[1, t, rows, :] += im

    def id_of(n):
        return jnp.maximum(live - LAST + n, 0)

    def step(k, carry):
        ids = [id_of(2 * k + s) for s in range(2)]

        def add_rows(s, row_at, j, p, tiles):
            for t in range(3):
                placed[2 * k + s, p, t, pl.ds(CH + j * CH, CH), :] = tiles[t]

        pair([place_of(offsets, tx, ty, i) for i in ids], ids,
             [live - LAST + 2 * k + s >= 0 for s in range(2)], add_rows, add_probe)
        return carry

    lax.fori_loop(0, LAST // 2, step, 0)
    pl.semaphore_wait(barrier, len(greeted))

    def make(src, dst, send_sem, recv_sem, device):
        return pltpu.make_async_remote_copy(
            src_ref=src, dst_ref=dst, send_sem=send_sem, recv_sem=recv_sem,
            device_id=device, device_id_type=MESH)

    def send(*args):
        c = make(*args)
        c.start()
        return c

    def part(i, j):
        return pl.ds(pl.multiple_of((i * 4 + j) * 32, 32), 32)

    side = 2 - 2 * ty
    core_copy = send(pgrad.at[1 - core], core_in, core_send.at[0], core_recv.at[0], core_mate)

    firsts = [place_of(offsets, tx, ty, id_of(n))[0] for n in range(LAST)]

    def place_rows(j, carry):
        rows = pl.ds(pl.multiple_of(j * CH, CH), CH)
        for p in range(2):
            for t in range(3):
                total = grad_in[p, t, rows, :]
                for n in range(LAST):
                    at = jnp.clip(j * CH - firsts[n] + CH, 0, CH + N)
                    total = total + placed[n, p, t, pl.ds(at, CH), :]
                grad[p, t, rows, :] = total
        return carry

    lax.fori_loop(0, ROWS // CH, place_rows, 0)
    diag = make(grad.at[:, side, pl.ds(TR, N)], came_diag, diag_send, diag_recv, (down, ty))
    below = make(grad.at[:, pl.ds(ty, 2), pl.ds(TR, N)], out_up, up_send, up_recv, (down, ty))

    @pl.when(tx < NTX - 1)
    def _():
        diag.start()

    @pl.when(tx == 0)
    def _():
        came_diag[...] = jnp.zeros_like(came_diag)
        out_up[...] = jnp.zeros_like(out_up)

    far_rows = send(
        grad.at[:, side, pl.ds(N, N)], out_ty.at[:, pl.ds(N, N)], ty_send.at[1], ty_recv.at[1], partner)
    core_copy.wait()
    for t in range(2):
        acc[pl.ds(t * N, N), :] = pgrad[core, t] + core_in[t]
    yz_copies = [
        send(acc.at[part(*yz_at[d])], yz_in.at[d], yz_send.at[0, d], yz_recv.at[0, d], yz_mates[d])
        for d in range(15)]
    for c in yz_copies:
        c.wait()
    total = acc[part(y, z_low), :]
    for d in range(15):
        total = total + yz_in[d]
    mine = x * 2 + z_high
    shared[mine] = total
    far_copies = [
        send(shared.at[mine], shared.at[mine], far_send.at[d], far_recv.at[d], far_mates[d]) for d in range(7)]

    @pl.when(tx > 0)
    def _():
        diag.wait_recv()

    for p in range(2):
        edge[p] = grad[p, side, pl.ds(0, N)] + came_diag[p]
    near_rows = send(edge, out_ty.at[:, pl.ds(0, N)], ty_send.at[0], ty_recv.at[0], partner)

    @pl.when(tx < NTX - 1)
    def _():
        below.start()

    for c in far_copies:
        c.wait()
    total = shared[0]
    for d in range(1, 8):
        total = total + shared[d]
    out_full[part(y, z_low), :] = total * (1.0 / (NTX * 2 * SLOTS))
    yz_copies = [
        send(out_full.at[part(y, z_low)], out_full.at[part(y, z_low)],
             yz_send.at[1, d], yz_recv.at[1, d], yz_mates[d])
        for d in range(15)]
    for c in yz_copies:
        c.wait()
    core_copy = send(out_full, out_other, core_send.at[1], core_recv.at[1], core_mate)

    @pl.when(tx < NTX - 1)
    def _():
        diag.wait_send()
        below.wait_send()

    @pl.when(tx > 0)
    def _():
        below.wait_recv()

    far_rows.wait()
    near_rows.wait()
    core_copy.wait()


def finish_kernel(
    grad, came_ty, came_up, full, other, out_re, out_im, pout_re, pout_im, whole, out_sem, pout_sem,
):
    core, ty = lax.rem(lax.axis_index("tx"), 2), lax.axis_index("ty")

    def probe_copies(re, im):
        return [
            pltpu.make_async_copy(
                src.at[pl.ds(t * N, N)], dst.at[:, pl.ds(t * H, H)], pout_sem.at[k, t])
            for k, (src, dst) in enumerate(((re, pout_re), (im, pout_im))) for t in range(2)]

    @pl.when(core == 0)
    def _():
        for c in probe_copies(full, other):
            c.start()

    @pl.when(core == 1)
    def _():
        for c in probe_copies(other, full):
            c.start()

    copies = []
    for p, out in enumerate((out_re, out_im)):
        for h in range(2):
            rows = pl.ds(h * N, N)
            for t in range(2):
                mine = jnp.where(ty == 1 - t, came_ty[p, rows], 0.0)
                total = grad[p, ty + t, rows] + mine
                whole[p, rows, pl.ds(t * H, H)] = total + came_up[p, t] if h == 0 else total
            copies.append(pltpu.make_async_copy(whole.at[p, rows], out.at[rows], out_sem.at[p, h]))
            copies[-1].start()
    for c in copies + probe_copies(full, other):
        c.wait()


def gather_out(offsets, counts, reg, probe_re, probe_im, tables, amp, grad, pgrad):
    vmem = pl.BlockSpec(memory_space=pltpu.VMEM)
    dma = pltpu.SemaphoreType.DMA
    tile = jax.ShapeDtypeStruct((TR, N), F32)
    patch = jax.ShapeDtypeStruct((N, N), F32)
    smem = pl.BlockSpec(memory_space=pltpu.SMEM)
    grad, *came = pl.pallas_call(
        out_kernel,
        out_shape=(
            pltpu.VMEM((2, 3, ROWS, H), F32),
            jax.ShapeDtypeStruct((2, TR, H), F32),
            jax.ShapeDtypeStruct((2, 2, N, H), F32),
            jax.ShapeDtypeStruct((2 * N, H), F32),
            jax.ShapeDtypeStruct((2 * N, H), F32),
        ),
        in_specs=[smem, smem] + [vmem] * 7,
        out_specs=(vmem,) * 5,
        scratch_shapes=[
            pltpu.VMEM((2, 2, N, H), F32),
            pltpu.VMEM((LAST, 2, 3, N + 2 * CH, H), F32),
            pltpu.VMEM((2, 2, 2, N, H), F32),
            pltpu.VMEM((2, 2, 2, N, N), BF16),
            pltpu.VMEM((2, 2, N, N), F32),
            pltpu.VMEM((2, N, H), F32),
            pltpu.VMEM((2, N, H), F32),
            pltpu.VMEM((2, N, H), F32),
            pltpu.VMEM((2 * N, H), F32),
            pltpu.VMEM((15, 32, H), F32),
            pltpu.VMEM((8, 32, H), F32),
            dma((2,)), dma((2,)), dma(()), dma(()), dma(()), dma(()),
            dma((2,)), dma((2,)), dma((2, 15)), dma((2, 15)), dma((7,)), dma((7,)),
        ],
        compiler_params=pltpu.CompilerParams(
            collective_id=1, has_side_effects=True, vmem_limit_bytes=20 << 20),
        name="gather_out",
    )(offsets, counts, reg, probe_re, probe_im, tables, amp, grad, pgrad)
    return pl.pallas_call(
        finish_kernel,
        out_shape=(tile, tile, patch, patch),
        in_specs=[vmem] * 5,
        out_specs=(pl.BlockSpec(memory_space=pltpu.HBM),) * 4,
        scratch_shapes=[pltpu.VMEM((2, TR, N), F32), dma((2, 2)), dma((2, 2))],
        compiler_params=pltpu.CompilerParams(vmem_limit_bytes=20 << 20),
        name="finish",
    )(grad, *came)


def per_device(obj_re, obj_im, probe_re, probe_im, amplitude, offsets, counts):
    tables = jnp.asarray(half_dft_tables())
    reg, amp, blank = halo(obj_re, obj_im, amplitude)
    shared = (jnp.swapaxes(offsets, 2, 3), counts, reg, probe_re, probe_im, tables, amp)
    grad, pgrad = positions(*shared, blank)
    return gather_out(*shared, grad, pgrad)


def solution(mesh):
    return jax.shard_map(
        per_device,
        mesh=mesh,
        in_specs=(
            P("tx", "ty"),
            P("tx", "ty"),
            P(),
            P(),
            P("tx", "ty", None, None, None),
            P("tx", None, None, None),
            P("tx", None),
        ),
        out_specs=(P("tx", "ty"), P("tx", "ty"), P(), P()),
        check_vma=False,
    )
```
